32 devices in a mesh: groups: 2 (over y), expert: 4 (over z), dp: 2 (over x), mp: 2 (over core).
Axes of the slice: x: 2, y: 2, z: 4, core: 2. Of those that a mesh axis runs over, the one named last changes fastest.
Arguments:
- hidden: bfloat16 [1024, 2048], P(('groups', 'expert', 'dp'), 'mp'), parts along dimension 0, may hold values from -6 to 6
- queries: bfloat16 [1024, 2048], P(('groups', 'expert', 'dp'), 'mp'), parts along dimension 0, may hold values from -6 to 120
- memory: bfloat16 [1024, 2, 2048], P(('groups', 'expert', 'dp'), None, 'mp'), parts along dimension 0, may hold values from -6 to 40.5
- target_pair: int32 [1024], P(('groups', 'expert', 'dp')), parts along dimension 0, may hold values from 0 to 15, as said below
- source_pair: int32 [1024], P(('groups', 'expert', 'dp')), parts along dimension 0, may hold values from 0 to 15, as said below
- routes: int32 [1024, 2], P(('groups', 'expert', 'dp')), parts along dimension 0, may hold values from 0 to 3, all different within a row; in each aligned block of 64 rows (0 to 63, 64 to 127, ...) at most 40 rows name the same one
- route_weight: float32 [1024, 2], P(('groups', 'expert', 'dp')), parts along dimension 0, may hold values from 0.1 to 1
- norm_gain: float32 [2048], replicated, may hold values from 0.5 to 1.5
- norm_bias: float32 [2048], replicated, may hold values from -3 to 3
- expert_in: bfloat16 [4, 2048, 8192], P('expert', None, ('dp', 'mp')), may hold values from -0.125 to 0.125
- expert_out: bfloat16 [4, 8192, 2048], P('expert', ('dp', 'mp')), may hold values from -0.0625 to 0.0625
Outputs:
- mixed: bfloat16 [1024, 2048], P(('groups', 'expert', 'dp'), 'mp'), parts along dimension 0
The draws below stay inside these ranges and needn't reach their ends.
There are 2 independent parts, one for each index of `groups`. The reference program is written for one: setup_inputs(seed, part) draws one part's arguments, and reference() takes and returns one part's arrays. A program takes and returns all parts, laid end to end along the dimension named above; an argument that names none is the same for every part. Nothing has to cross between parts.
Inputs may be any that keep to these rules, and one draw needn't show every extreme that they name: `target_pair`: within each batch pair numbers run over 0 to 15; each pair's target tokens form one contiguous run on one index of expert and dp, which holds the tokens of 4 pairs. `source_pair`: within each batch, memory rows read by expert index and then row carry pair numbers that never fall, and every pair has at least one row. `routes`: among the rows of one device no expert is named more than 40 times.
All inputs are finite; a program needn't handle non-finite values.
Results may differ from the reference program's by a relative error of at most 0.008.
Values may be sent and summed in bfloat16 or wider, within the bound.
No kernel may reach another device: no remote copies, remote signals or barrier semaphores. Data moves between devices by JAX's collectives and lax.ppermute only.
A program may use at most 128 MiB of HBM per device.

```python
import math
import jax
import jax.numpy as jnp
import numpy as np
from jax import lax

D = 2048
HEADS = 16
HEAD = 128
FF = 8192
TOK_DEV = 64
SRC_DEV = 64
PAIRS_DEV = 4
EXPERTS = 4
BATCHES = 2
TOKENS = 512
SOURCE_ROWS = 512
PAIRS_ROW = 16
CAP = 40
N_DP = 2
N_MP = 2


def draw_queries(key, part):
    base = jnp.clip(jax.random.normal(key, (TOKENS, D), jnp.float32), -6.0, 6.0)
    return base.astype(jnp.bfloat16)


def draw_memory(key, part):
    base = jnp.clip(jax.random.normal(key, (SOURCE_ROWS, 2, D), jnp.float32), -6.0, 6.0)
    return base.astype(jnp.bfloat16)


def draw_source_pair(key, part):
    per_batch = SRC_DEV * EXPERTS

    def one_batch(subkey):
        cuts = jax.random.permutation(subkey, per_batch - 1)[:PAIRS_ROW - 1] + 1
        marks = jnp.zeros((per_batch,), jnp.int32).at[cuts].set(1)
        return jnp.cumsum(marks).astype(jnp.int32)
    pairs = jax.vmap(one_batch)(jax.random.split(key, BATCHES))
    pairs = pairs.reshape(BATCHES, EXPERTS, SRC_DEV)
    return jnp.swapaxes(pairs, 0, 1).reshape(SOURCE_ROWS).astype(jnp.int32)


def draw_target_pair(key, part):

    def one_batch(subkey):
        owner_key, cut_key = jax.random.split(subkey)
        owned = jax.random.permutation(owner_key, PAIRS_ROW).reshape(EXPERTS, PAIRS_DEV).astype(jnp.int32)

        def one_device(device_key, mine):
            cuts = jax.random.permutation(device_key, TOK_DEV - 1)[:PAIRS_DEV - 1] + 1
            marks = jnp.zeros((TOK_DEV,), jnp.int32).at[cuts].set(1)
            return mine[jnp.cumsum(marks)]
        return jax.vmap(one_device)(jax.random.split(cut_key, EXPERTS), owned)
    pairs = jax.vmap(one_batch)(jax.random.split(key, BATCHES))
    return jnp.swapaxes(pairs, 0, 1).reshape(TOKENS).astype(jnp.int32)


def levels(stream_key, extent, cuts, low, high):
    def one(axis_at, shards_of):
        heights = jax.random.uniform(jax.random.fold_in(jax.random.fold_in(stream_key, 6), axis_at), (shards_of,), jnp.float32, low / len(cuts), high / len(cuts))
        return jnp.repeat(jnp.exp(heights), extent[axis_at] // shards_of).reshape((-1,) + (1,) * (len(extent) - axis_at - 1))

    level = one(*cuts[0])
    for cut in cuts[1:]:
        level = level * one(*cut)
    return level


def routed_block(stream_key, own, number, rows, count, top, most, slope):
    sequence = jax.random.permutation(stream_key, count)
    packed, ordinary = portions_of(count, rows * top, most, slope, True), portions_of(count, rows * top, most, slope, False)
    places = jnp.arange(count)

    def named(tallies, rotation):
        used = int((tallies > 0).sum())
        fixed = max(1, used // 4)
        moved = fixed + (places - fixed + rotation * (used - fixed)) % max(1, count - fixed)
        return jnp.zeros((count,), jnp.int32).at[sequence[jnp.where(places < fixed, places, moved)]].set(jnp.asarray(tallies, jnp.int32))

    tallies = jnp.where(number % 4 == 0, named(packed, number // 4), named(ordinary, number - number // 4 - 1))
    mixed = jax.random.permutation(jax.random.fold_in(own, 3), count)
    donor, taker = mixed[0:count // 2 * 2:2], mixed[1:count // 2 * 2:2]
    margin = jnp.minimum(tallies[donor] - 1, most - tallies[taker]) // 2
    margin = jnp.where((donor == sequence[0]) | (taker == sequence[0]) | (tallies[taker] == 0), 0, jnp.maximum(margin, 0))
    moved = jax.random.randint(jax.random.fold_in(own, 4), (count // 2,), 0, 1 << 20) % (margin + 1)
    tallies = tallies.at[donor].add(-moved).at[taker].add(moved)
    items = jnp.searchsorted(jnp.cumsum(tallies), jnp.arange(rows * top), side="right").astype(jnp.int32)
    table = items.reshape(top, rows).T
    table = table[jax.random.permutation(jax.random.fold_in(own, 1), rows)]
    rotation = jax.random.randint(jax.random.fold_in(own, 2), (rows, 1), 0, top)
    return jnp.take_along_axis(table, (jnp.arange(top)[None, :] + rotation) % top, axis=1)


def portions_of(amount, total, bound, slope, full):
    portions = [(1 << 20) // math.isqrt(standing ** slope) + 1 for standing in range(1, amount + 1)]
    largest = bound if full else min(bound, max(-(-total // amount), total * portions[0] // sum(portions)))
    least = 1 if total - largest >= amount - 1 else 0
    holding, spare = [largest] + [least] * (amount - 1), total - largest - least * (amount - 1)
    while spare > 0:
        free = [i for i in range(1, amount) if holding[i] < largest] or [i for i in range(1, amount) if holding[i] < bound]
        whole, remaining = sum([portions[i] for i in free]), spare
        for i in free:
            addition = min(bound - holding[i], max(1, remaining * portions[i] // whole), spare)
            holding[i] = holding[i] + addition
            spare = spare - addition
    return np.array(holding)


def normal_values(rng, extent, width, most, cuts=(), kind=jnp.bfloat16):
    loudness = levels(rng, extent, cuts, -0.22, 0.18) if cuts else 1.0
    entries = jax.random.normal(rng, extent, jnp.float32) * width * loudness
    return jnp.minimum(jnp.maximum(entries, -most), most).astype(kind)


def setup_inputs(seed: int = 0, part: int = 0) -> dict:
    streams_of = jax.random.split(jax.random.key(seed), 12)
    part_splits = jax.random.split(jax.random.fold_in(streams_of[11], part), 12)
    hidden = normal_values(part_splits[0], (TOKENS, D), 1.0, 6.0, ((0, 8), (1, 2)))
    queries = draw_queries(jax.random.fold_in(jax.random.fold_in(streams_of[11], part), 71), part)
    memory = draw_memory(jax.random.fold_in(jax.random.fold_in(streams_of[11], part), 71), part)
    target_pair = draw_target_pair(jax.random.fold_in(jax.random.fold_in(streams_of[11], part), 71), part)
    source_pair = draw_source_pair(jax.random.fold_in(jax.random.fold_in(streams_of[11], part), 71), part)
    routes_keys = jax.random.split(jax.random.fold_in(part_splits[5], 1), TOKENS // TOK_DEV)
    routes_turns = jax.random.permutation(jax.random.fold_in(part_splits[5], 3), TOKENS // TOK_DEV)
    routes = jax.vmap(lambda own, number: routed_block(jax.random.fold_in(part_splits[5], 2), own, number, TOK_DEV, EXPERTS, 2, CAP, 2))(routes_keys, routes_turns).reshape((TOKENS, 2))
    route_weight = jnp.clip(0.1 + 0.9 * jax.random.uniform(part_splits[6], (TOKENS, 2), jnp.float32) ** levels(part_splits[6], (TOKENS, 2), ((0, 8),), -0.2, 0.2), 0.1, 1.0)
    norm_gain = jnp.clip(1.0 + 0.1 * jax.random.normal(streams_of[7], (D,), jnp.float32), 0.5, 1.5)
    norm_bias = normal_values(streams_of[8], (D,), 0.5, 3.0, (), jnp.float32)
    expert_in = normal_values(streams_of[9], (EXPERTS, D, FF), D ** -0.5, 0.125, ((0, 4), (2, 4)))
    expert_out = normal_values(streams_of[10], (EXPERTS, FF, D), FF ** -0.5, 0.0625, ((0, 4), (1, 4)))
    return {"hidden": hidden, "queries": queries, "memory": memory, "target_pair": target_pair, "source_pair": source_pair, "routes": routes, "route_weight": route_weight, "norm_gain": norm_gain, "norm_bias": norm_bias, "expert_in": expert_in, "expert_out": expert_out}


EPSILON = 1e-05
NEGATIVE = -1e+30

def rounded(values):
    return lax.optimization_barrier(values.astype(jnp.bfloat16)).astype(jnp.float32)

def layer_norm(rows, norm_gain, norm_bias):
    values = rows.astype(jnp.float32)
    center = lax.optimization_barrier(jnp.mean(values, axis=-1, keepdims=True))
    spread = lax.optimization_barrier(jnp.mean(jnp.square(values - center), axis=-1, keepdims=True))
    return rounded((values - center) * lax.rsqrt(spread + EPSILON) * norm_gain + norm_bias)

def by_batch(array, rows_dev):
    rest = array.shape[1:]
    shaped = array.reshape((EXPERTS, BATCHES, rows_dev) + rest)
    shaped = jnp.swapaxes(shaped, 0, 1)
    return shaped.reshape((BATCHES, EXPERTS * rows_dev) + rest)

def attend_batch(operands):
    query_rows, memory_rows, token_pairs, row_pairs = operands
    count = query_rows.shape[0]
    rows = memory_rows.shape[0]
    heads_q = query_rows.astype(jnp.float32).reshape(count, HEADS, HEAD)
    keys = memory_rows[:, 0, :].astype(jnp.float32).reshape(rows, HEADS, HEAD)
    values = memory_rows[:, 1, :].astype(jnp.float32).reshape(rows, HEADS, HEAD)
    score = jnp.einsum('thd,rhd->htr', heads_q, keys) * (1.0 / math.sqrt(HEAD))
    match = (token_pairs[:, None] == row_pairs[None, :])[None]
    masked = jnp.where(match, score, NEGATIVE)
    largest = lax.optimization_barrier(jnp.max(masked, axis=-1, keepdims=True))
    weight = jnp.where(match, jnp.exp(masked - largest), 0.0)
    total = lax.optimization_barrier(jnp.sum(weight, axis=-1))
    context = jnp.einsum('htr,rhd->thd', rounded(weight), values) / jnp.transpose(total)[:, :, None]
    return context.reshape(count, HEADS * HEAD)

def reference(hidden, queries, memory, target_pair, source_pair, routes, route_weight, norm_gain, norm_bias, expert_in, expert_out):
    context = lax.map(attend_batch, (by_batch(queries, TOK_DEV), by_batch(memory, SRC_DEV), by_batch(target_pair, TOK_DEV), by_batch(source_pair, SRC_DEV)))
    context = jnp.swapaxes(context.reshape(BATCHES, EXPERTS, TOK_DEV, D), 0, 1).reshape(TOKENS, D)
    attended = rounded(hidden.astype(jnp.float32) + context)
    sources = EXPERTS * BATCHES
    token_rows = attended.reshape(sources, TOK_DEV, D)
    flat = routes.reshape(sources, 2 * TOK_DEV)
    named = (flat[:, :, None] == jnp.arange(EXPERTS, dtype=jnp.int32)[None, None, :]).astype(jnp.int32)
    slot = lax.optimization_barrier(jnp.sum((jnp.cumsum(named, axis=1) - named) * named, axis=-1))
    dest = (flat * CAP + slot).astype(jnp.int32)
    place = (dest[:, :, None] == jnp.arange(EXPERTS * CAP, dtype=jnp.int32)[None, None, :]).astype(jnp.float32)
    per_token = lax.optimization_barrier(jnp.sum(place.reshape(sources, TOK_DEV, 2, EXPERTS * CAP), axis=2))
    sent = jnp.einsum('stk,std->skd', per_token, token_rows)
    by_expert = jnp.swapaxes(sent.reshape(sources, EXPERTS, CAP, D), 0, 1).reshape(EXPERTS, sources * CAP, D)
    slices = N_DP * N_MP

    def run_expert(operands):
        rows, weight_in, weight_out = operands
        normed = layer_norm(rows, norm_gain, norm_bias)
        w_first = weight_in.astype(jnp.float32).reshape(D, slices, FF // slices)
        w_second = weight_out.astype(jnp.float32).reshape(slices, FF // slices, D)
        active = rounded(jax.nn.relu(jnp.einsum('rd,dsf->srf', normed, w_first)))
        part = rounded(jnp.einsum('srf,sfc->src', active, w_second))
        return lax.optimization_barrier(jnp.sum(part, axis=0))
    outputs = lax.map(run_expert, (by_expert, expert_in, expert_out))
    by_source = jnp.swapaxes(outputs.reshape(EXPERTS, sources, CAP, D), 0, 1).reshape(sources, EXPERTS * CAP, D)
    picked = jax.vmap(lambda table, index: table[index])(by_source, dest)
    picked = picked.reshape(sources, TOK_DEV, 2, D)
    weights = route_weight.reshape(sources, TOK_DEV, 2)
    mixed = token_rows + lax.optimization_barrier(jnp.sum(weights[:, :, :, None] * picked, axis=2))
    return mixed.reshape(TOKENS, D).astype(jnp.bfloat16)
```

```python
import functools
import math

import jax
import jax.numpy as jnp
from jax import lax
from jax.experimental import pallas as pl
from jax.experimental.pallas import tpu as pltpu
from jax.sharding import PartitionSpec as P

HEAD = 128
EPSILON = 1e-05
NEGATIVE = -1e30
META = 16
VMEM_LIMIT = 12 * 1024 * 1024

BF16 = jnp.bfloat16
F32 = jnp.float32
IN_VMEM = pl.BlockSpec(memory_space=pltpu.VMEM)
IN_SMEM = pl.BlockSpec(memory_space=pltpu.SMEM)
IN_HBM = pl.BlockSpec(memory_space=pl.ANY)


def struct(rows, columns, dtype=BF16):
    return jax.ShapeDtypeStruct((rows, columns), dtype)


def call(kernel, outs, specs, scratch=(), flops=0, moved=0):
    return pl.pallas_call(
        kernel,
        out_shape=outs,
        in_specs=specs,
        out_specs=[IN_VMEM] * len(outs),
        scratch_shapes=scratch,
        compiler_params=pltpu.CompilerParams(vmem_limit_bytes=VMEM_LIMIT),
        cost_estimate=pl.CostEstimate(flops=flops, bytes_accessed=moved, transcendentals=0),
    )


def dot(a, b):
    return lax.dot_general(a, b, (((1,), (0,)), ((), ())), preferred_element_type=F32)


def dot_nt(a, b):
    return lax.dot_general(a, b, (((1,), (1,)), ((), ())), preferred_element_type=F32)


def iota(shape, dimension):
    return lax.broadcasted_iota(jnp.int32, shape, dimension)


def wrapped(value, size):
    return jnp.where(value >= size, value - size, value)


def columns_at(start, width):
    return pl.ds(pl.multiple_of(start * width, width), width)


def pack_kernel(experts, at_ref, q_ref, m_ref, h_ref, tp_ref, sp_ref, r_ref, *outs):
    rows, width = q_ref.shape[0], outs[0].shape[1]
    here = at_ref[0]
    row = iota((META, rows), 0)
    kinds = jnp.where(
        row == 0,
        tp_ref[...],
        jnp.where(
            row == 1,
            sp_ref[...],
            jnp.where(row == 2, r_ref[0:1, :], jnp.where(row == 3, r_ref[1:2, :], 0)),
        ),
    )
    kinds = kinds.astype(F32).astype(BF16)
    for step, out in enumerate(outs):
        cols = columns_at(wrapped(here + step, experts), width)
        out[0:rows, :] = q_ref[:, cols]
        out[rows : 2 * rows, :] = m_ref[:, 0, cols]
        out[2 * rows : 3 * rows, :] = m_ref[:, 1, cols]
        out[3 * rows : 4 * rows, :] = h_ref[:, cols]
        moved = (iota((rows, width), 1) == iota((rows, width), 0) + step * rows).astype(BF16)
        out[4 * rows :, :] = dot(kinds, moved).astype(BF16)


def prefetch_kernel(w1_ref, w2_ref, after_ref, o1_ref, o2_ref, sems):
    parts = sems.shape[1]
    size = w1_ref.shape[0] // parts
    copies = []
    for k, (src, dst) in enumerate(((w1_ref, o1_ref), (w2_ref, o2_ref))):
        for part in range(parts):
            rows = pl.ds(part * size, size)
            copies.append(pltpu.make_async_copy(src.at[rows], dst.at[rows], sems.at[k, part]))
    for copy in copies:
        copy.start()
    for copy in copies:
        copy.wait()


def attend_kernel(experts, rows, cap, at_ref, *refs):
    messages, compact, attended = refs[:experts], refs[experts : 2 * experts], refs[2 * experts :]
    width = messages[0].shape[1]
    count = experts * rows
    here = at_ref[0]
    meta = sum(m[4 * rows :, :].astype(F32) for m in messages)
    same = (iota((count, count), 0) == iota((count, count), 1)).astype(BF16)
    columns = dot_nt(same, meta.astype(BF16))
    match = columns[:, 0:1] == meta[1:2, :]
    scale = 1.0 / math.sqrt(HEAD)
    parts = []
    for head in range(width // HEAD):
        lanes = slice(head * HEAD, (head + 1) * HEAD)

        def stacked(kind):
            return jnp.concatenate(
                [m[kind * rows : (kind + 1) * rows, lanes] for m in messages], axis=0
            )

        score = dot_nt(stacked(0), stacked(1)) * scale
        masked = jnp.where(match, score, NEGATIVE)
        largest = jnp.max(masked, axis=-1, keepdims=True)
        weight = jnp.where(match, jnp.exp(masked - largest), 0.0)
        total = jnp.sum(weight, axis=-1, keepdims=True)
        context = dot(weight.astype(BF16), stacked(2)) / total
        parts.append((stacked(3).astype(F32) + context).astype(BF16))
    states = jnp.concatenate(parts, axis=1)
    for block, out in enumerate(attended):
        out[...] = states[block * rows : (block + 1) * rows, :]
    first, second = meta[2:3, :].astype(jnp.int32), meta[3:4, :].astype(jnp.int32)
    expert = wrapped(here + iota((META, count), 0), experts)
    named = ((first == expert) | (second == expert)) & (iota((META, count), 0) < experts)
    before = (iota((count, count), 0) < iota((count, count), 1)) & (
        iota((count, count), 0) // rows == iota((count, count), 1) // rows
    )
    slot = dot(named.astype(BF16), before.astype(BF16)).astype(jnp.int32)
    source = here - iota((META, count), 1) // rows
    source = jnp.where(source < 0, source + experts, source)
    spot = jnp.where(named, source * cap + slot, -1)
    for step, out in enumerate(compact):
        place = iota((experts * cap, count), 0) == spot[step : step + 1, :]
        out[...] = dot(place.astype(BF16), states).astype(BF16)


def first_kernel(experts, tile, at_ref, *refs):
    mine, other = refs[:experts], refs[experts : 2 * experts]
    gain_ref, bias_ref, w_ref, out_ref, x_ref, n_ref = refs[2 * experts :]
    width = mine[0].shape[1]
    here, half = at_ref[0], at_ref[1]
    for step in range(experts):
        source = here - step
        source = jnp.where(source < 0, source + experts, source)
        x_ref[:, columns_at(half * experts + source, width)] = mine[step][...]
        x_ref[:, columns_at((1 - half) * experts + source, width)] = other[step][...]
    values = x_ref[...].astype(F32)
    center = jnp.mean(values, axis=-1, keepdims=True)
    shifted = values - center
    spread = jnp.mean(jnp.square(shifted), axis=-1, keepdims=True)
    normed = shifted * lax.rsqrt(spread + EPSILON) * gain_ref[...] + bias_ref[...]
    n_ref[...] = normed.astype(BF16)

    @pl.loop(0, w_ref.shape[1] // tile)
    def _(at):
        cols = columns_at(at, tile)
        out_ref[:, cols] = jnp.maximum(dot(n_ref[...], w_ref[:, cols]), 0.0).astype(BF16)


def second_kernel(tile, at_ref, a_ref, w_ref, sent_ref, kept_ref):
    half = at_ref[1]
    tiles = sent_ref.shape[1] // tile

    @pl.loop(0, tiles)
    def _(at):
        cols = columns_at(at, tile)
        sent_ref[:, cols] = dot(
            a_ref[...], w_ref[:, columns_at((1 - half) * tiles + at, tile)]
        ).astype(BF16)

    @pl.loop(0, tiles)
    def _(at):
        cols = columns_at(at, tile)
        kept_ref[:, cols] = dot(
            a_ref[...], w_ref[:, columns_at(half * tiles + at, tile)]
        ).astype(BF16)


def split_kernel(experts, at_ref, kept_ref, got_ref, *refs):
    outs, total = refs[:experts], refs[experts]
    cap = outs[0].shape[0]
    total[...] = kept_ref[...].astype(F32) + got_ref[...].astype(F32)
    for step, out in enumerate(outs):
        target = wrapped(at_ref[0] + step, experts)
        out[...] = total[pl.ds(pl.multiple_of(target * cap, 8), cap), :].astype(out.dtype)


def mix_kernel(experts, at_ref, weight_ref, *refs):
    returned, states = refs[:experts], refs[experts : 2 * experts]
    out_ref, total = refs[2 * experts :]
    width = states[0].shape[1]
    share = jnp.zeros(total.shape, F32)
    for step in range(experts):
        weight = weight_ref[step]
        high = weight.astype(BF16)
        rest = weight - high.astype(F32)
        middle = rest.astype(BF16)
        low = (rest - middle.astype(F32)).astype(BF16)
        rows = returned[step][...]
        share = share + (dot(high, rows) + (dot(middle, rows) + dot(low, rows)))
    total[...] = share
    for step in range(experts):
        cols = columns_at(wrapped(at_ref[0] + step, experts), width)
        out_ref[:, cols] = (states[step][...].astype(F32) + total[:, cols]).astype(BF16)


def head_shards(
    hidden,
    queries,
    memory,
    target_pair,
    source_pair,
    routes,
    route_weight,
    norm_gain,
    norm_bias,
    expert_in,
    expert_out,
):
    rows, columns = hidden.shape
    experts = lax.axis_size("expert")
    width = columns // experts
    cap = 2 * rows // experts * 5 // 4
    model = 2 * columns
    hidden_units = expert_in.shape[2]
    here, half = lax.axis_index("expert"), lax.axis_index("mp")
    at = jnp.stack([here, half]).astype(jnp.int32)

    def along(array, step):
        if step % experts == 0:
            return array
        pairs = [(i, (i + step) % experts) for i in range(experts)]
        return lax.ppermute(array, "expert", pairs)

    def swap(array, axis):
        return lax.ppermute(array, axis, [(0, 1), (1, 0)])

    packed = call(
        functools.partial(pack_kernel, experts),
        [struct(4 * rows + META, width)] * experts,
        [IN_SMEM] + [IN_VMEM] * 6,
        moved=16 * rows * columns,
    )(
        at,
        queries,
        memory,
        hidden,
        target_pair.reshape(1, rows),
        source_pair.reshape(1, rows),
        routes.T,
    )
    messages = [along(packed[step], step) for step in range(experts)]

    w_in, w_out = pl.pallas_call(
        prefetch_kernel,
        out_shape=[
            pltpu.VMEM((model, hidden_units), BF16),
            pltpu.VMEM((hidden_units, model), BF16),
        ],
        in_specs=[IN_HBM, IN_HBM, IN_HBM],
        out_specs=[IN_VMEM, IN_VMEM],
        scratch_shapes=[pltpu.SemaphoreType.DMA((2, 4))],
        compiler_params=pltpu.CompilerParams(vmem_limit_bytes=VMEM_LIMIT),
        cost_estimate=pl.CostEstimate(
            flops=0, bytes_accessed=8 * model * hidden_units, transcendentals=0
        ),
    )(expert_in[0], expert_out[0], packed[0])

    named = jnp.any(routes[:, :, None] == jnp.arange(experts)[None, None, :], axis=1)
    named = named.astype(jnp.int32)
    slots = jnp.cumsum(named, axis=0) - named
    chosen = (here - jnp.arange(experts)) % experts
    slot = jnp.take(slots.T, chosen, axis=0)
    weight = jnp.sum(
        jnp.where(routes[None, :, :] == chosen[:, None, None], route_weight[None, :, :], 0.0),
        axis=2,
    )
    weights = jnp.where(
        slot[:, :, None] == jnp.arange(cap)[None, None, :], weight[:, :, None], 0.0
    )

    attended = call(
        functools.partial(attend_kernel, experts, rows, cap),
        [struct(experts * cap, width)] * experts + [struct(rows, width)] * experts,
        [IN_SMEM] + [IN_VMEM] * experts,
        flops=8 * experts * experts * rows * rows * width,
        moved=16 * rows * columns,
    )(at, *messages)
    compact, states = attended[:experts], attended[experts:]

    own = [along(compact[step], step) for step in range(experts)]
    far = [swap(block, "dp") for block in own]

    def first(blocks):
        count = experts * cap
        return call(
            functools.partial(first_kernel, experts, 512),
            [struct(count, hidden_units)],
            [IN_SMEM] + [IN_VMEM] * (2 * experts + 3),
            scratch=[pltpu.VMEM((count, model), BF16)] * 2,
            flops=2 * count * model * hidden_units,
            moved=2 * model * hidden_units,
        )(
            at,
            *blocks,
            *[swap(block, "mp") for block in blocks],
            norm_gain.reshape(1, model),
            norm_bias.reshape(1, model),
            pltpu.with_memory_space_constraint(w_in, pltpu.VMEM),
        )[0]

    def second(active):
        count = experts * cap
        sent, kept = call(
            functools.partial(second_kernel, 512),
            [struct(count, columns)] * 2,
            [IN_SMEM, IN_VMEM, IN_VMEM],
            flops=2 * count * model * hidden_units,
            moved=2 * model * hidden_units,
        )(at, active, pltpu.with_memory_space_constraint(w_out, pltpu.VMEM))
        return kept, swap(sent, "mp")

    def split(kept, got, dtype):
        return call(
            functools.partial(split_kernel, experts),
            [struct(cap, columns, dtype)] * experts,
            [IN_SMEM, IN_VMEM, IN_VMEM],
            scratch=[pltpu.VMEM((experts * cap, columns), F32)],
            moved=8 * experts * cap * columns,
        )(at, kept, got)

    active_own = first(own)
    active_far = first(far)
    gone = [swap(block, "dp") for block in split(*second(active_far), BF16)]
    mine = split(*second(active_own), F32)
    summed = [(block + came.astype(F32)).astype(BF16) for block, came in zip(mine, gone)]
    returned = [along(summed[step], step) for step in range(experts)]
    home = [along(states[step], -step) for step in range(experts)]

    return call(
        functools.partial(mix_kernel, experts),
        [struct(rows, columns)],
        [IN_SMEM] + [IN_VMEM] * (2 * experts + 1),
        scratch=[pltpu.VMEM((rows, columns), F32)],
        flops=6 * rows * experts * cap * columns,
        moved=4 * rows * columns,
    )(at, weights, *returned, *home)[0]


def shards(
    hidden,
    queries,
    memory,
    target_pair,
    source_pair,
    routes,
    route_weight,
    norm_gain,
    norm_bias,
    expert_in,
    expert_out,
):
    tok_rows = hidden.shape[0]
    local_heads = queries.shape[1] // HEAD
    scale = 1.0 / math.sqrt(HEAD)
    query_heads = queries.reshape(tok_rows, local_heads, HEAD)
    running = jnp.full((local_heads, tok_rows), NEGATIVE, jnp.float32)
    rows = lax.all_gather(memory, "expert", axis=0, tiled=True)
    row_pairs = lax.all_gather(source_pair, "expert", axis=0, tiled=True)
    count = rows.shape[0]
    keys = rows[:, 0, :].reshape(count, local_heads, HEAD)
    values = rows[:, 1, :].reshape(count, local_heads, HEAD)
    score = (
        jnp.einsum("thd,rhd->htr", query_heads, keys, preferred_element_type=jnp.float32) * scale
    )
    match = (target_pair[:, None] == row_pairs[None, :])[None]
    masked = jnp.where(match, score, NEGATIVE)
    newest = jnp.maximum(running, jnp.max(masked, axis=-1))
    weight = jnp.where(match, jnp.exp(masked - newest[:, :, None]), 0.0)
    total = jnp.sum(weight, axis=-1)
    summed = jnp.einsum(
        "htr,rhd->htd", weight.astype(jnp.bfloat16), values, preferred_element_type=jnp.float32
    )
    running, total, summed = (newest, total, summed)
    context = jnp.transpose(summed / total[:, :, None], (1, 0, 2)).reshape(
        tok_rows, local_heads * HEAD
    )
    attended = (hidden.astype(jnp.float32) + context).astype(jnp.bfloat16)
    full_rows = lax.all_gather(attended, "mp", axis=1, tiled=True)
    width = full_rows.shape[1]
    experts_all = lax.axis_size("expert")
    batches = lax.axis_size("dp")
    cap = 2 * tok_rows // experts_all * 5 // 4
    flat = routes.reshape(-1)
    named = (flat[:, None] == jnp.arange(experts_all, dtype=jnp.int32)[None, :]).astype(jnp.int32)
    slot = jnp.sum((jnp.cumsum(named, axis=0) - named) * named, axis=1)
    dest = flat * cap + slot
    place = dest[:, None] == jnp.arange(experts_all * cap, dtype=jnp.int32)[None, :]
    per_token = jnp.sum(place.reshape(tok_rows, 2, experts_all * cap).astype(jnp.bfloat16), axis=1)
    outgoing = lax.dot_general(
        per_token, full_rows, (((0,), (0,)), ((), ())), preferred_element_type=jnp.float32
    ).astype(jnp.bfloat16)
    copies = jnp.broadcast_to(
        outgoing.reshape(experts_all, 1, cap, width), (experts_all, batches, cap, width)
    ).reshape(experts_all * batches * cap, width)
    arrived = lax.all_to_all(copies, ("expert", "dp"), split_axis=0, concat_axis=0, tiled=True)
    values = arrived.astype(jnp.float32)
    center = jnp.mean(values, axis=-1, keepdims=True)
    spread = jnp.mean(jnp.square(values - center), axis=-1, keepdims=True)
    normed = ((values - center) * lax.rsqrt(spread + EPSILON) * norm_gain + norm_bias).astype(
        jnp.bfloat16
    )
    active = jax.nn.relu(jnp.dot(normed, expert_in[0], preferred_element_type=jnp.float32)).astype(
        jnp.bfloat16
    )
    partial_value = jnp.dot(active, expert_out[0], preferred_element_type=jnp.float32).astype(
        jnp.bfloat16
    )
    returned = lax.all_to_all(
        partial_value, ("expert", "dp"), split_axis=0, concat_axis=0, tiled=True
    )
    expert_sum = jnp.sum(
        returned.reshape(experts_all, batches, cap, width).astype(jnp.float32), axis=1
    )
    picked = jnp.dot(
        place.astype(jnp.float32),
        expert_sum.reshape(experts_all * cap, width),
        precision=lax.Precision.HIGHEST,
    )
    blended = jnp.sum(picked.reshape(tok_rows, 2, width) * route_weight[:, :, None], axis=1)
    share = lax.psum_scatter(
        blended.astype(jnp.bfloat16), "mp", scatter_dimension=1, tiled=True
    ).astype(jnp.float32)
    return (attended.astype(jnp.float32) + share).astype(jnp.bfloat16)


def layer(hidden, queries, memory, *rest):
    experts = lax.axis_size("expert")
    rows, columns = hidden.shape
    heads = columns // HEAD
    by_heads = (
        lax.axis_size("mp") == 2
        and lax.axis_size("dp") == 2
        and heads % experts == 0
        and memory.shape[0] == rows
        and experts * rows <= columns // experts
        and experts <= META
    )
    return (head_shards if by_heads else shards)(hidden, queries, memory, *rest)


def solution(mesh):
    return jax.shard_map(
        layer,
        mesh=mesh,
        in_specs=(
            P(("groups", "expert", "dp"), "mp"),
            P(("groups", "expert", "dp"), "mp"),
            P(("groups", "expert", "dp"), None, "mp"),
            P(("groups", "expert", "dp")),
            P(("groups", "expert", "dp")),
            P(("groups", "expert", "dp"), None),
            P(("groups", "expert", "dp"), None),
            P(),
            P(),
            P("expert", None, ("dp", "mp")),
            P("expert", ("dp", "mp"), None),
        ),
        out_specs=P(("groups", "expert", "dp"), "mp"),
        check_vma=False,
    )
```

```python
import functools
import math

import jax
import jax.numpy as jnp
from jax import lax
from jax.experimental import pallas as pl
from jax.experimental.pallas import tpu as pltpu
from jax.sharding import PartitionSpec as P

HEAD = 128
EPSILON = 1e-05
NEGATIVE = -1e30
META = 16
VMEM_LIMIT = 12 * 1024 * 1024

BF16 = jnp.bfloat16
F32 = jnp.float32
IN_VMEM = pl.BlockSpec(memory_space=pltpu.VMEM)
IN_SMEM = pl.BlockSpec(memory_space=pltpu.SMEM)
IN_HBM = pl.BlockSpec(memory_space=pltpu.HBM)


def struct(rows, columns, dtype=BF16):
    return jax.ShapeDtypeStruct((rows, columns), dtype)


def call(kernel, outs, specs, scratch=(), flops=0, moved=0):
    return pl.pallas_call(
        kernel,
        out_shape=outs,
        in_specs=specs,
        out_specs=[IN_VMEM] * len(outs),
        scratch_shapes=scratch,
        compiler_params=pltpu.CompilerParams(vmem_limit_bytes=VMEM_LIMIT),
        cost_estimate=pl.CostEstimate(flops=flops, bytes_accessed=moved, transcendentals=0),
    )


def dot(a, b):
    return lax.dot_general(a, b, (((1,), (0,)), ((), ())), preferred_element_type=F32)


def dot_nt(a, b):
    return lax.dot_general(a, b, (((1,), (1,)), ((), ())), preferred_element_type=F32)


def dot_tn(a, b):
    return lax.dot_general(a, b, (((0,), (0,)), ((), ())), preferred_element_type=F32)


def iota(shape, dimension):
    return lax.broadcasted_iota(jnp.int32, shape, dimension)


def in_hbm(array):
    return pltpu.with_memory_space_constraint(array, pltpu.HBM)


def in_vmem(array):
    return pltpu.with_memory_space_constraint(array, pltpu.VMEM)


def columns_at(start, width):
    return pl.ds(pl.multiple_of(start * width, width), width)


def thirds(array):
    high = array.astype(BF16).astype(F32)
    middle = (array - high).astype(BF16).astype(F32)
    low = (array - high - middle).astype(BF16).astype(F32)
    return [high, middle, low]


def pack_kernel(experts, at_ref, q_hbm, m_hbm, h_hbm, tp_hbm, sp_hbm, r_hbm, rw_hbm, *refs):
    outs = refs[:experts]
    m_ref, tp_ref, sp_ref, r_ref, rw_ref, sems, small_sems = refs[experts:]
    rows, width = q_hbm.shape[0], outs[0].shape[1]
    here = at_ref[0]
    small = [
        pltpu.make_async_copy(src, dst, small_sems.at[k])
        for k, (src, dst) in enumerate(
            ((tp_hbm, tp_ref), (sp_hbm, sp_ref), (r_hbm, r_ref), (rw_hbm, rw_ref))
        )
    ]
    large = []
    for step, out in enumerate(outs):
        cols = columns_at(here ^ step, width)
        large.append(
            (
                pltpu.make_async_copy(m_hbm.at[:, :, cols], m_ref.at[step], sems.at[0, step]),
                pltpu.make_async_copy(q_hbm.at[:, cols], out.at[pl.ds(0, rows)], sems.at[1, step]),
                pltpu.make_async_copy(
                    h_hbm.at[:, cols], out.at[pl.ds(3 * rows, rows)], sems.at[2, step]
                ),
            )
        )
    for copy in small:
        copy.start()
    for copies in large:
        for copy in copies:
            copy.start()
    for copy in small:
        copy.wait()
    row = iota((META, rows), 0)
    lines = [tp_ref[...], sp_ref[...], r_ref[0:1, :], r_ref[1:2, :]]
    lines = [line.astype(F32) for line in lines]
    lines += thirds(rw_ref[0:1, :]) + thirds(rw_ref[1:2, :])
    kinds = jnp.zeros((META, rows), F32)
    for k, line in enumerate(lines):
        kinds = jnp.where(row == k, line, kinds)
    kinds = kinds.astype(BF16)
    for step, out in enumerate(outs):
        moved = (iota((rows, width), 1) == iota((rows, width), 0) + step * rows).astype(BF16)
        out[4 * rows :, :] = dot(kinds, moved).astype(BF16)
    for step, out in enumerate(outs):
        large[step][0].wait()
        out[rows : 2 * rows, :] = m_ref[step, :, 0, :]
        out[2 * rows : 3 * rows, :] = m_ref[step, :, 1, :]
    for copies in large:
        copies[1].wait()
        copies[2].wait()


def prefetch_kernel(w1_ref, w2_ref, after_ref, o1_ref, o2_ref, sems):
    parts = sems.shape[1]
    size = w1_ref.shape[0] // parts
    copies = []
    for k, (src, dst) in enumerate(((w1_ref, o1_ref), (w2_ref, o2_ref))):
        for part in range(parts):
            rows = pl.ds(part * size, size)
            copies.append(pltpu.make_async_copy(src.at[rows], dst.at[rows], sems.at[k, part]))
    for copy in copies:
        copy.start()
    for copy in copies:
        copy.wait()


def attend_kernel(experts, rows, cap, at_ref, w1_ref, w2_ref, *refs):
    messages, compact = refs[:experts], refs[experts:]
    width = messages[0].shape[1]
    count = experts * rows
    here = at_ref[0]
    meta = sum(m[4 * rows :, :].astype(F32) for m in messages)
    same = (iota((count, count), 0) == iota((count, count), 1)).astype(BF16)
    columns = dot_nt(same, meta.astype(BF16))
    match = columns[:, 0:1] == meta[1:2, :]
    scale = 1.0 / math.sqrt(HEAD)
    parts = []
    for head in range(width // HEAD):
        lanes = slice(head * HEAD, (head + 1) * HEAD)

        def stacked(kind):
            return jnp.concatenate(
                [m[kind * rows : (kind + 1) * rows, lanes] for m in messages], axis=0
            )

        score = dot_nt(stacked(0), stacked(1)) * scale
        masked = jnp.where(match, score, NEGATIVE)
        largest = jnp.max(masked, axis=-1, keepdims=True)
        weight = jnp.where(match, jnp.exp(masked - largest), 0.0)
        total = jnp.sum(weight, axis=-1, keepdims=True)
        context = dot(weight.astype(BF16), stacked(2)) / total
        parts.append((stacked(3).astype(F32) + context).astype(BF16))
    states = jnp.concatenate(parts, axis=1)
    first, second = meta[2:3, :].astype(jnp.int32), meta[3:4, :].astype(jnp.int32)
    expert = here ^ iota((META, count), 0)
    named = ((first == expert) | (second == expert)) & (iota((META, count), 0) < experts)
    before = (iota((count, count), 0) < iota((count, count), 1)) & (
        iota((count, count), 0) // rows == iota((count, count), 1) // rows
    )
    slot = dot(named.astype(BF16), before.astype(BF16)).astype(jnp.int32)
    source = here ^ (iota((META, count), 1) // rows)
    spot = jnp.where(named, source * cap + slot, -1)
    for step, out in enumerate(compact):
        place = iota((experts * cap, count), 0) == spot[step : step + 1, :]
        place = place.astype(BF16)
        out[0 : experts * cap, :] = dot(place, states).astype(BF16)
        leads = first == (here ^ step)
        values = [jnp.where(leads, meta[4 + k : 5 + k, :], meta[7 + k : 8 + k, :]) for k in range(3)]
        values.append(leads.astype(F32))
        lines = jnp.zeros((META, count), F32)
        for k, value in enumerate(values):
            lines = jnp.where(iota((META, count), 0) == k, value, lines)
        out[experts * cap :, :] = jnp.zeros((META, width), BF16)
        out[experts * cap :, 0 : experts * cap] = dot_nt(lines.astype(BF16), place).astype(BF16)


def first_kernel(experts, tile, at_ref, *refs):
    mine, other = refs[:experts], refs[experts : 2 * experts]
    gain_ref, bias_ref, w_ref, out_ref, x_ref, n_ref = refs[2 * experts :]
    width = mine[0].shape[1]
    here, half = at_ref[0], at_ref[1]
    for step in range(experts):
        source = here ^ step
        x_ref[:, columns_at(half * experts + source, width)] = mine[step][0 : x_ref.shape[0], :]
        x_ref[:, columns_at((1 - half) * experts + source, width)] = other[step][0 : x_ref.shape[0], :]
    for at in range(0, x_ref.shape[0], META):
        block = slice(at, at + META)
        values = x_ref[block, :].astype(F32)
        center = jnp.mean(values, axis=-1, keepdims=True)
        shifted = values - center
        spread = jnp.mean(jnp.square(shifted), axis=-1, keepdims=True)
        normed = shifted * lax.rsqrt(spread + EPSILON) * gain_ref[...] + bias_ref[...]
        n_ref[block, :] = normed.astype(BF16)
    for at in range(0, w_ref.shape[1], tile):
        cols = slice(at, at + tile)
        out_ref[:, cols] = jnp.maximum(dot(n_ref[...], w_ref[:, cols]), 0.0).astype(BF16)


def second_kernel(tile, at_ref, a_ref, w_ref, sent_ref, kept_ref):
    columns = sent_ref.shape[1]
    lower = at_ref[1] == 0
    for at in range(0, columns, tile):
        low = dot(a_ref[...], w_ref[:, at : at + tile])
        high = dot(a_ref[...], w_ref[:, columns + at : columns + at + tile])
        sent_ref[:, at : at + tile] = jnp.where(lower, high, low).astype(BF16)
        kept_ref[:, at : at + tile] = jnp.where(lower, low, high).astype(BF16)


def away_kernel(experts, order, at_ref, kept_ref, got_ref, *refs):
    outs, total = refs[:-1], refs[-1]
    total[...] = kept_ref[...].astype(F32) + got_ref[...].astype(F32)
    cap = total.shape[0] // experts
    each = experts // len(outs)
    for k, step in enumerate(order):
        rows = pl.ds(pl.multiple_of((at_ref[0] ^ step) * cap, 8), cap)
        at = k % each * cap
        outs[k // each][at : at + cap, :] = total[rows, :].astype(BF16)


def base_kernel(experts, at_ref, kept_ref, got_ref, *refs):
    blocks, bases, factors = refs[:experts], refs[experts : 2 * experts], refs[2 * experts : -3]
    total, states, columns = refs[-3:]
    count = total.shape[0]
    cap = count // experts
    width = blocks[0].shape[1]
    lines = blocks[0][count:, 0:count]
    same = (iota((count, count), 0) == iota((count, count), 1)).astype(BF16)
    columns[:, 0:META] = dot_nt(same, lines)
    weight = columns[:, 0:1] + columns[:, 1:2] + columns[:, 2:3]
    leads = columns[:, 3:4]
    for step in range(experts):
        states[:, columns_at(at_ref[0] ^ step, width)] = blocks[step][0:count, :].astype(F32)
    total[...] = (kept_ref[...].astype(F32) + got_ref[...].astype(F32)) * weight + (
        leads * states[...]
    )
    columns[...] = jnp.broadcast_to(weight, columns.shape)
    for step in range(experts):
        rows = pl.ds(pl.multiple_of((at_ref[0] ^ step) * cap, 8), cap)
        bases[step][...] = total[rows, :]
        factors[step][...] = columns[rows, :]


def join_kernel(came_ref, *refs):
    count = len(refs) // 3
    cap = refs[0].shape[0]
    for k in range(count):
        base_ref, factor_ref, out_ref = refs[k], refs[count + k], refs[2 * count + k]
        came = came_ref[k * cap : (k + 1) * cap, :].astype(F32)
        out_ref[...] = (base_ref[...] + factor_ref[:, 0:1] * came).astype(BF16)


def mix_kernel(experts, cap, at_ref, routes_ref, *refs):
    returned, out_ref = refs[:experts], refs[experts]
    rows = out_ref.shape[0]
    expert = at_ref[0] ^ iota((META, rows), 0)
    named = (routes_ref[0:1, :] == expert) | (routes_ref[1:2, :] == expert)
    named = named & (iota((META, rows), 0) < experts)
    before = (iota((rows, rows), 0) < iota((rows, rows), 1)).astype(BF16)
    slot = dot(named.astype(BF16), before).astype(jnp.int32)
    slot = jnp.where(named, slot, -1)
    share = jnp.zeros(out_ref.shape, F32)
    for step in range(experts):
        place = (iota((cap, rows), 0) == slot[step : step + 1, :]).astype(BF16)
        share = share + dot_tn(place, returned[step][...])
    out_ref[...] = share.astype(BF16)


def head_shards(
    hidden,
    queries,
    memory,
    target_pair,
    source_pair,
    routes,
    route_weight,
    norm_gain,
    norm_bias,
    expert_in,
    expert_out,
):
    rows, columns = hidden.shape
    experts = lax.axis_size("expert")
    width = columns // experts
    cap = 2 * rows // experts * 5 // 4
    model = 2 * columns
    hidden_units = expert_in.shape[2]
    here, half = lax.axis_index("expert"), lax.axis_index("mp")
    at = jnp.stack([here, half]).astype(jnp.int32)

    def along(array, step):
        if step == 0:
            return array
        return lax.ppermute(array, "expert", [(i, i ^ step) for i in range(experts)])

    def swap(array, axis):
        return lax.ppermute(array, axis, [(0, 1), (1, 0)])

    packed = call(
        functools.partial(pack_kernel, experts),
        [struct(4 * rows + META, width)] * experts,
        [IN_SMEM] + [IN_HBM] * 7,
        scratch=[
            pltpu.VMEM((experts, rows, 2, width), BF16),
            pltpu.VMEM((1, rows), jnp.int32),
            pltpu.VMEM((1, rows), jnp.int32),
            pltpu.VMEM((2, rows), jnp.int32),
            pltpu.VMEM((2, rows), F32),
            pltpu.SemaphoreType.DMA((3, experts)),
            pltpu.SemaphoreType.DMA((4,)),
        ],
        moved=16 * rows * columns,
    )(
        at,
        in_hbm(queries),
        in_hbm(memory),
        in_hbm(hidden),
        in_hbm(target_pair.reshape(1, rows)),
        in_hbm(source_pair.reshape(1, rows)),
        in_hbm(routes.T),
        in_hbm(route_weight.T),
    )
    order = list(range(experts // 2, experts)) + list(reversed(range(experts // 2)))
    messages = {step: along(packed[step], step) for step in order}
    messages = [messages[step] for step in range(experts)]

    w_in, w_out = pl.pallas_call(
        prefetch_kernel,
        out_shape=[
            pltpu.VMEM((model, hidden_units), BF16),
            pltpu.VMEM((hidden_units, model), BF16),
        ],
        in_specs=[IN_HBM, IN_HBM, IN_VMEM],
        out_specs=[IN_VMEM, IN_VMEM],
        scratch_shapes=[pltpu.SemaphoreType.DMA((2, 4))],
        compiler_params=pltpu.CompilerParams(vmem_limit_bytes=VMEM_LIMIT),
        cost_estimate=pl.CostEstimate(
            flops=0, bytes_accessed=8 * model * hidden_units, transcendentals=0
        ),
    )(in_hbm(expert_in[0]), in_hbm(expert_out[0]), packed[0])

    compact = call(
        functools.partial(attend_kernel, experts, rows, cap),
        [struct(experts * cap + META, width)] * experts,
        [IN_SMEM] + [IN_VMEM] * (2 + experts),
        flops=8 * experts * experts * rows * rows * width,
        moved=16 * rows * columns,
    )(at, in_vmem(w_in), in_vmem(w_out), *messages)

    far = {0: swap(compact[0], "dp")}
    own = {0: compact[0]}
    early, late = order[: experts // 2], order[experts // 2 : -1]
    own.update({step: along(compact[step], step) for step in early})
    held, far[0] = lax.optimization_barrier(([compact[step] for step in late], far[0]))
    own.update({step: along(block, step) for step, block in zip(late, held)})
    far.update({step: swap(own[step], "dp") for step in order[:-1]})
    own_other = {step: swap(own[step], "mp") for step in own}

    def first(blocks, others):
        count = experts * cap
        return call(
            functools.partial(first_kernel, experts, 512),
            [struct(count, hidden_units)],
            [IN_SMEM] + [IN_VMEM] * (2 * experts + 3),
            scratch=[pltpu.VMEM((count, model), BF16)] * 2,
            flops=2 * count * model * hidden_units,
            moved=2 * model * hidden_units,
        )(
            at,
            *[blocks[step] for step in range(experts)],
            *[others[step] for step in range(experts)],
            norm_gain.reshape(1, model),
            norm_bias.reshape(1, model),
            in_vmem(w_in),
        )[0]

    def second(active):
        count = experts * cap
        sent, kept = call(
            functools.partial(second_kernel, 512),
            [struct(count, columns)] * 2,
            [IN_SMEM, IN_VMEM, IN_VMEM],
            flops=2 * count * model * hidden_units,
            moved=2 * model * hidden_units,
        )(at, active, in_vmem(w_out))
        return kept, swap(sent, "mp")

    kept, got = second(first(own, own_other))
    far, kept = lax.optimization_barrier((far, kept))
    far_other = {step: swap(far[step], "mp") for step in order}
    parts = call(
        functools.partial(away_kernel, experts, order),
        [struct(2 * cap, columns)] * (experts // 2),
        [IN_SMEM, IN_VMEM, IN_VMEM],
        scratch=[pltpu.VMEM((experts * cap, columns), F32)],
        moved=8 * experts * cap * columns,
    )(at, *second(first(far, far_other)))
    came = [swap(part, "dp") for part in parts]
    based = call(
        functools.partial(base_kernel, experts),
        [struct(cap, columns, F32)] * experts + [struct(cap, HEAD, F32)] * experts,
        [IN_SMEM] + [IN_VMEM] * (2 + experts),
        scratch=[pltpu.VMEM((experts * cap, columns), F32)] * 2
        + [pltpu.VMEM((experts * cap, HEAD), F32)],
        moved=16 * experts * cap * columns,
    )(at, kept, got, *[own[step] for step in range(experts)])
    returned = {}
    for k, part in enumerate(came):
        steps = order[2 * k : 2 * k + 2]
        joined = call(
            join_kernel,
            [struct(cap, columns)] * 2,
            [IN_VMEM] * 5,
            moved=32 * cap * columns,
        )(part, *[based[step] for step in steps], *[based[experts + step] for step in steps])
        returned.update({step: along(block, step) for step, block in zip(steps, joined)})

    return call(
        functools.partial(mix_kernel, experts, cap),
        [struct(rows, columns)],
        [IN_SMEM] + [IN_VMEM] * (experts + 1),
        flops=2 * rows * experts * cap * columns,
        moved=4 * rows * columns,
    )(at, routes.T, *[returned[step] for step in range(experts)])[0]


def shards(
    hidden,
    queries,
    memory,
    target_pair,
    source_pair,
    routes,
    route_weight,
    norm_gain,
    norm_bias,
    expert_in,
    expert_out,
):
    tok_rows = hidden.shape[0]
    local_heads = queries.shape[1] // HEAD
    scale = 1.0 / math.sqrt(HEAD)
    query_heads = queries.reshape(tok_rows, local_heads, HEAD)
    running = jnp.full((local_heads, tok_rows), NEGATIVE, jnp.float32)
    rows = lax.all_gather(memory, "expert", axis=0, tiled=True)
    row_pairs = lax.all_gather(source_pair, "expert", axis=0, tiled=True)
    count = rows.shape[0]
    keys = rows[:, 0, :].reshape(count, local_heads, HEAD)
    values = rows[:, 1, :].reshape(count, local_heads, HEAD)
    score = (
        jnp.einsum("thd,rhd->htr", query_heads, keys, preferred_element_type=jnp.float32) * scale
    )
    match = (target_pair[:, None] == row_pairs[None, :])[None]
    masked = jnp.where(match, score, NEGATIVE)
    newest = jnp.maximum(running, jnp.max(masked, axis=-1))
    weight = jnp.where(match, jnp.exp(masked - newest[:, :, None]), 0.0)
    total = jnp.sum(weight, axis=-1)
    summed = jnp.einsum(
        "htr,rhd->htd", weight.astype(jnp.bfloat16), values, preferred_element_type=jnp.float32
    )
    running, total, summed = (newest, total, summed)
    context = jnp.transpose(summed / total[:, :, None], (1, 0, 2)).reshape(
        tok_rows, local_heads * HEAD
    )
    attended = (hidden.astype(jnp.float32) + context).astype(jnp.bfloat16)
    full_rows = lax.all_gather(attended, "mp", axis=1, tiled=True)
    width = full_rows.shape[1]
    experts_all = lax.axis_size("expert")
    batches = lax.axis_size("dp")
    cap = 2 * tok_rows // experts_all * 5 // 4
    flat = routes.reshape(-1)
    named = (flat[:, None] == jnp.arange(experts_all, dtype=jnp.int32)[None, :]).astype(jnp.int32)
    slot = jnp.sum((jnp.cumsum(named, axis=0) - named) * named, axis=1)
    dest = flat * cap + slot
    place = dest[:, None] == jnp.arange(experts_all * cap, dtype=jnp.int32)[None, :]
    per_token = jnp.sum(place.reshape(tok_rows, 2, experts_all * cap).astype(jnp.bfloat16), axis=1)
    outgoing = lax.dot_general(
        per_token, full_rows, (((0,), (0,)), ((), ())), preferred_element_type=jnp.float32
    ).astype(jnp.bfloat16)
    copies = jnp.broadcast_to(
        outgoing.reshape(experts_all, 1, cap, width), (experts_all, batches, cap, width)
    ).reshape(experts_all * batches * cap, width)
    arrived = lax.all_to_all(copies, ("expert", "dp"), split_axis=0, concat_axis=0, tiled=True)
    values = arrived.astype(jnp.float32)
    center = jnp.mean(values, axis=-1, keepdims=True)
    spread = jnp.mean(jnp.square(values - center), axis=-1, keepdims=True)
    normed = ((values - center) * lax.rsqrt(spread + EPSILON) * norm_gain + norm_bias).astype(
        jnp.bfloat16
    )
    active = jax.nn.relu(jnp.dot(normed, expert_in[0], preferred_element_type=jnp.float32)).astype(
        jnp.bfloat16
    )
    partial_value = jnp.dot(active, expert_out[0], preferred_element_type=jnp.float32).astype(
        jnp.bfloat16
    )
    returned = lax.all_to_all(
        partial_value, ("expert", "dp"), split_axis=0, concat_axis=0, tiled=True
    )
    expert_sum = jnp.sum(
        returned.reshape(experts_all, batches, cap, width).astype(jnp.float32), axis=1
    )
    picked = jnp.dot(
        place.astype(jnp.float32),
        expert_sum.reshape(experts_all * cap, width),
        precision=lax.Precision.HIGHEST,
    )
    blended = jnp.sum(picked.reshape(tok_rows, 2, width) * route_weight[:, :, None], axis=1)
    share = lax.psum_scatter(
        blended.astype(jnp.bfloat16), "mp", scatter_dimension=1, tiled=True
    ).astype(jnp.float32)
    return (attended.astype(jnp.float32) + share).astype(jnp.bfloat16)


def layer(hidden, queries, memory, *rest):
    experts = lax.axis_size("expert")
    rows, columns = hidden.shape
    heads = columns // HEAD
    by_heads = (
        lax.axis_size("mp") == 2
        and lax.axis_size("dp") == 2
        and heads % experts == 0
        and memory.shape[0] == rows
        and experts * rows <= columns // experts
        and experts <= META
        and experts & (experts - 1) == 0
    )
    return (head_shards if by_heads else shards)(hidden, queries, memory, *rest)


def solution(mesh):
    return jax.shard_map(
        layer,
        mesh=mesh,
        in_specs=(
            P(("groups", "expert", "dp"), "mp"),
            P(("groups", "expert", "dp"), "mp"),
            P(("groups", "expert", "dp"), None, "mp"),
            P(("groups", "expert", "dp")),
            P(("groups", "expert", "dp")),
            P(("groups", "expert", "dp"), None),
            P(("groups", "expert", "dp"), None),
            P(),
            P(),
            P("expert", None, ("dp", "mp")),
            P("expert", ("dp", "mp"), None),
        ),
        out_specs=P(("groups", "expert", "dp"), "mp"),
        check_vma=False,
    )
```

```python
import functools
import math

import jax
import jax.numpy as jnp
from jax import lax
from jax.experimental import pallas as pl
from jax.experimental.pallas import tpu as pltpu
from jax.sharding import PartitionSpec as P

HEAD = 128
EPSILON = 1e-05
NEGATIVE = -1e30
META = 16
LATER = 16 * 1024 * 1024
ORDER = (2, 3, 1, 0)
VMEM_LIMIT = 12 * 1024 * 1024

BF16 = jnp.bfloat16
F32 = jnp.float32
IN_VMEM = pl.BlockSpec(memory_space=pltpu.VMEM)
IN_ANY = pl.BlockSpec(memory_space=pl.ANY)
IN_HBM = pl.BlockSpec(memory_space=pltpu.HBM)


def struct(rows, columns, dtype=BF16):
    return jax.ShapeDtypeStruct((rows, columns), dtype)


def call(kernel, outs, specs, scratch=(), flops=0, moved=0):
    return pl.pallas_call(
        kernel,
        out_shape=outs,
        in_specs=specs,
        out_specs=[IN_VMEM] * len(outs),
        scratch_shapes=scratch,
        compiler_params=pltpu.CompilerParams(vmem_limit_bytes=VMEM_LIMIT),
        cost_estimate=pl.CostEstimate(flops=flops, bytes_accessed=moved, transcendentals=0),
    )


def dot(a, b):
    return lax.dot_general(a, b, (((1,), (0,)), ((), ())), preferred_element_type=F32)


def dot_nt(a, b):
    return lax.dot_general(a, b, (((1,), (1,)), ((), ())), preferred_element_type=F32)


def dot_tn(a, b):
    return lax.dot_general(a, b, (((0,), (0,)), ((), ())), preferred_element_type=F32)


def iota(shape, dimension):
    return lax.broadcasted_iota(jnp.int32, shape, dimension)


def in_hbm(array):
    return pltpu.with_memory_space_constraint(array, pltpu.HBM)


def in_vmem(array):
    return pltpu.with_memory_space_constraint(array, pltpu.VMEM)


def columns_at(start, width):
    return pl.ds(pl.multiple_of(start * width, width), width)


def thirds(array):
    high = array.astype(BF16).astype(F32)
    middle = (array - high).astype(BF16).astype(F32)
    low = (array - high - middle).astype(BF16).astype(F32)
    return [high, middle, low]


def pack_kernel(steps, q_hbm, m_hbm, h_hbm, tp_hbm, sp_hbm, r_hbm, rw_hbm, *refs):
    outs, refs = refs[-7 - len(steps) : -7], refs[-7:]
    m_ref, tp_ref, sp_ref, r_ref, rw_ref, sems, small_sems = refs
    rows, width = q_hbm.shape[0], outs[0].shape[1]
    here = lax.axis_index("expert")
    small = [
        pltpu.make_async_copy(src, dst, small_sems.at[k])
        for k, (src, dst) in enumerate(
            ((tp_hbm, tp_ref), (sp_hbm, sp_ref), (r_hbm, r_ref), (rw_hbm, rw_ref))
        )
    ]
    large = []
    for k, (step, out) in enumerate(zip(steps, outs)):
        cols = columns_at(here ^ step, width)
        large.append(
            (
                pltpu.make_async_copy(m_hbm.at[:, :, cols], m_ref.at[k], sems.at[0, k]),
                pltpu.make_async_copy(q_hbm.at[:, cols], out.at[pl.ds(0, rows)], sems.at[1, k]),
                pltpu.make_async_copy(
                    h_hbm.at[:, cols], out.at[pl.ds(3 * rows, rows)], sems.at[2, k]
                ),
            )
        )
    for copy in small:
        copy.start()
    for copies in large:
        for copy in copies:
            copy.start()
    for copy in small:
        copy.wait()
    row = iota((META, rows), 0)
    lines = [tp_ref[...], sp_ref[...], r_ref[0:1, :], r_ref[1:2, :]]
    lines = [line.astype(F32) for line in lines]
    lines += thirds(rw_ref[0:1, :]) + thirds(rw_ref[1:2, :])
    kinds = jnp.zeros((META, rows), F32)
    for k, line in enumerate(lines):
        kinds = jnp.where(row == k, line, kinds)
    kinds = kinds.astype(BF16)
    for step, out in zip(steps, outs):
        moved = (iota((rows, width), 1) == iota((rows, width), 0) + step * rows).astype(BF16)
        out[4 * rows :, :] = dot(kinds, moved).astype(BF16)
    for k, out in enumerate(outs):
        large[k][0].wait()
        out[rows : 2 * rows, :] = m_ref[k, :, 0, :]
        out[2 * rows : 3 * rows, :] = m_ref[k, :, 1, :]
    for copies in large:
        copies[1].wait()
        copies[2].wait()


def prefetch_kernel(experts, w1_hbm, w2_hbm, gain_hbm, bias_hbm, after_ref, *refs):
    w1_ref, w2_ref, gain_ref, bias_ref, sems, small_sems = refs
    here, half = lax.axis_index("expert"), lax.axis_index("mp")
    size = w1_ref.shape[0] // (2 * experts)
    copies = []
    for part in range(2 * experts):
        core = half if part < experts else 1 - half
        source = columns_at(core * experts + (here ^ ORDER[part % experts]), size)
        target = pl.ds(part * size, size)
        copies += [
            pltpu.make_async_copy(w1_hbm.at[source], w1_ref.at[target], sems.at[0, part]),
            pltpu.make_async_copy(w2_hbm.at[target], w2_ref.at[target], sems.at[1, part]),
            pltpu.make_async_copy(
                gain_hbm.at[:, source], gain_ref.at[:, target], small_sems.at[0, part]
            ),
            pltpu.make_async_copy(
                bias_hbm.at[:, source], bias_ref.at[:, target], small_sems.at[1, part]
            ),
        ]
    for copy in copies:
        copy.start()
    for copy in copies:
        copy.wait()


def attend_kernel(experts, rows, cap, w1_ref, w2_ref, *refs):
    arrived, compact = dict(zip(ORDER, refs[:experts])), refs[experts:]
    messages = [arrived[step] for step in range(experts)]
    width = messages[0].shape[1]
    count = experts * rows
    here = lax.axis_index("expert")
    meta = sum(m[4 * rows :, :].astype(F32) for m in messages)
    same = (iota((count, count), 0) == iota((count, count), 1)).astype(BF16)
    columns = dot_nt(same, meta.astype(BF16))
    match = columns[:, 0:1] == meta[1:2, :]
    scale = 1.0 / math.sqrt(HEAD)
    parts = []
    for head in range(width // HEAD):
        lanes = slice(head * HEAD, (head + 1) * HEAD)

        def stacked(kind):
            return jnp.concatenate(
                [m[kind * rows : (kind + 1) * rows, lanes] for m in messages], axis=0
            )

        score = dot_nt(stacked(0), stacked(1)) * scale
        masked = jnp.where(match, score, NEGATIVE)
        largest = jnp.max(masked, axis=-1, keepdims=True)
        weight = jnp.where(match, jnp.exp(masked - largest), 0.0)
        total = jnp.sum(weight, axis=-1, keepdims=True)
        context = dot(weight.astype(BF16), stacked(2)) / total
        parts.append((stacked(3).astype(F32) + context).astype(BF16))
    states = jnp.concatenate(parts, axis=1)
    first, second = meta[2:3, :].astype(jnp.int32), meta[3:4, :].astype(jnp.int32)
    expert = here ^ iota((META, count), 0)
    named = ((first == expert) | (second == expert)) & (iota((META, count), 0) < experts)
    before = (iota((count, count), 0) < iota((count, count), 1)) & (
        iota((count, count), 0) // rows == iota((count, count), 1) // rows
    )
    slot = dot(named.astype(BF16), before.astype(BF16)).astype(jnp.int32)
    block = (iota((META, count), 1) // rows) ^ iota((META, count), 0)
    spot = jnp.where(named, block * cap + slot, -1)
    for step, out in zip(ORDER, compact):
        place = iota((experts * cap, count), 0) == spot[step : step + 1, :]
        place = place.astype(BF16)
        out[0 : experts * cap, :] = dot(place, states).astype(BF16)
        leads = first == (here ^ step)
        values = [jnp.where(leads, meta[4 + k : 5 + k, :], meta[7 + k : 8 + k, :]) for k in range(3)]
        values.append(leads.astype(F32))
        lines = jnp.zeros((META, count), F32)
        for k, value in enumerate(values):
            lines = jnp.where(iota((META, count), 0) == k, value, lines)
        out[experts * cap :, :] = jnp.zeros((META, width), BF16)
        out[experts * cap :, 0 : experts * cap] = dot_nt(lines.astype(BF16), place).astype(BF16)


def trim_kernel(block_ref, out_ref):
    out_ref[...] = block_ref[0 : out_ref.shape[0], :]


def first_kernel(tile, *refs):
    blocks, (gain_ref, bias_ref, w_ref, out_ref, n_ref) = refs[:-5], refs[-5:]
    width, model = blocks[0].shape[1], n_ref.shape[1]
    for at in range(0, n_ref.shape[0], META):
        rows = slice(at, at + META)
        values = [block[rows, :].astype(F32) for block in blocks]
        center = jnp.sum(sum(values), axis=-1, keepdims=True) * (1.0 / model)
        shifted = [value - center for value in values]
        spread = sum(value * value for value in shifted)
        spread = jnp.sum(spread, axis=-1, keepdims=True) * (1.0 / model)
        scale = lax.rsqrt(spread + EPSILON)
        for k, value in enumerate(shifted):
            cols = slice(k * width, (k + 1) * width)
            normed = value * scale * gain_ref[:, cols] + bias_ref[:, cols]
            n_ref[rows, cols] = normed.astype(BF16)
    for at in range(0, w_ref.shape[1], tile):
        cols = slice(at, at + tile)
        out_ref[:, cols] = jnp.maximum(dot(n_ref[...], w_ref[:, cols]), 0.0).astype(BF16)


def second_kernel(tile, a_ref, w_ref, kept_ref, *sent):
    columns, rows = kept_ref.shape[1], sent[0].shape[0]
    lower = lax.axis_index("mp") == 0
    for at in range(0, columns, tile):
        low = dot(a_ref[...], w_ref[:, at : at + tile])
        high = dot(a_ref[...], w_ref[:, columns + at : columns + at + tile])
        kept_ref[:, at : at + tile] = jnp.where(lower, low, high).astype(BF16)
        other = jnp.where(lower, high, low).astype(BF16)
        for k, out_ref in enumerate(sent):
            out_ref[:, at : at + tile] = other[k * rows : (k + 1) * rows, :]


def row_factors(lines_ref, count):
    same = (iota((count, count), 0) == iota((count, count), 1)).astype(BF16)
    columns = dot_nt(same, lines_ref[count:, 0:count])
    return columns[:, 0:1] + columns[:, 1:2] + columns[:, 2:3], columns[:, 3:4]


def plain_kernel(kept_ref, got_ref, out_ref):
    rows = slice(kept_ref.shape[0] - out_ref.shape[0], kept_ref.shape[0])
    out_ref[...] = (kept_ref[rows, :].astype(F32) + got_ref[rows, :].astype(F32)).astype(BF16)


def gather_states(blocks, states, rows):
    here = lax.axis_index("expert")
    width = blocks[0].shape[1]
    for step, block in zip(ORDER, blocks):
        states[:, columns_at(here ^ step, width)] = block[rows, :].astype(F32)


def base_kernel(experts, kept_ref, *refs):
    got, blocks, refs = refs[:2], refs[2 : 2 + experts], refs[2 + experts :]
    bases, factors, states = refs[:2], refs[2:4], refs[4]
    count = kept_ref.shape[0]
    cap = count // experts
    weight, leads = row_factors(blocks[-1], count)
    gather_states(blocks, states, slice(2 * cap, 4 * cap))
    for k in range(2):
        rows, half = slice((2 + k) * cap, (3 + k) * cap), slice(k * cap, (k + 1) * cap)
        total = kept_ref[rows, :].astype(F32) + got[k][...].astype(F32)
        bases[k][...] = total * weight[rows, :] + leads[rows, :] * states[half, :]
        factors[k][...] = jnp.broadcast_to(weight[rows, :], (cap, HEAD))


def tail_kernel(experts, kept_ref, *refs):
    got, blocks, refs = refs[:2], refs[2 : 2 + experts], refs[2 + experts :]
    far_kept_ref, far_got_ref, lines_ref, _, near0, near1, far0, far1, states = refs
    count = kept_ref.shape[0]
    cap = count // experts
    weight, leads = row_factors(blocks[-1], count)
    far_weight, _ = row_factors(lines_ref, count)
    gather_states(blocks, states, slice(0, 2 * cap))
    for k, (near, far) in enumerate(((near0, far0), (near1, far1))):
        rows = slice(k * cap, (k + 1) * cap)
        total = kept_ref[rows, :].astype(F32) + got[k][...].astype(F32)
        total = total * weight[rows, :] + leads[rows, :] * states[rows, :]
        near[...] = total.astype(BF16)
        total = far_kept_ref[rows, :].astype(F32) + far_got_ref[rows, :].astype(F32)
        far[...] = (total * far_weight[rows, :]).astype(BF16)


def join_kernel(came_ref, *refs):
    count = len(refs) // 3
    cap = refs[0].shape[0]
    for k in range(count):
        base_ref, factor_ref, out_ref = refs[k], refs[count + k], refs[2 * count + k]
        came = came_ref[k * cap : (k + 1) * cap, :].astype(F32)
        out_ref[...] = (base_ref[...] + factor_ref[:, 0:1] * came).astype(BF16)


def mix_kernel(experts, cap, tile, steps, routes_ref, *refs):
    returned, refs = refs[: len(steps)], refs[len(steps) :]
    out_ref = refs[-1]
    rows = out_ref.shape[0]
    expert = lax.axis_index("expert") ^ iota((META, rows), 0)
    named = (routes_ref[0:1, :] == expert) | (routes_ref[1:2, :] == expert)
    named = named & (iota((META, rows), 0) < experts)
    before = (iota((rows, rows), 0) < iota((rows, rows), 1)).astype(BF16)
    slot = jnp.where(named, dot(named.astype(BF16), before), -1.0)
    same = (iota((rows, rows), 0) == iota((rows, rows), 1)).astype(BF16)
    slot = dot_nt(same, slot.astype(BF16)).astype(jnp.int32)
    place = {
        step: (iota((rows, cap), 1) == slot[:, step : step + 1]).astype(BF16) for step in set(steps)
    }
    for at in range(0, out_ref.shape[1], tile):
        cols = slice(at, at + tile)
        share = refs[0][:, cols] if len(refs) > 1 else jnp.zeros((rows, tile), F32)
        for step, block in zip(steps, returned):
            share = share + dot(place[step], block[:, cols])
        out_ref[:, cols] = share.astype(out_ref.dtype)


def head_shards(
    hidden,
    queries,
    memory,
    target_pair,
    source_pair,
    routes,
    route_weight,
    norm_gain,
    norm_bias,
    expert_in,
    expert_out,
):
    rows, columns = hidden.shape
    experts = lax.axis_size("expert")
    width = columns // experts
    cap = 2 * rows // experts * 5 // 4
    model = 2 * columns
    hidden_units = expert_in.shape[2]

    def along(array, step):
        if step == 0:
            return array
        return lax.ppermute(array, "expert", [(i, i ^ step) for i in range(experts)])

    def swap(array, axis):
        return lax.ppermute(array, axis, [(0, 1), (1, 0)])

    def across(array):
        pairs = [(2 * i + j, 2 * (i ^ 1) + 1 - j) for i in range(experts) for j in range(2)]
        return lax.ppermute(array, ("expert", "dp"), pairs)

    def pack(steps, *after):
        return call(
            functools.partial(pack_kernel, steps),
            [struct(4 * rows + META, width)] * len(steps),
            [IN_HBM] * 7 + [IN_ANY] * len(after),
            scratch=[
                pltpu.VMEM((len(steps), rows, 2, width), BF16),
                pltpu.VMEM((1, rows), jnp.int32),
                pltpu.VMEM((1, rows), jnp.int32),
                pltpu.VMEM((2, rows), jnp.int32),
                pltpu.VMEM((2, rows), F32),
                pltpu.SemaphoreType.DMA((3, len(steps))),
                pltpu.SemaphoreType.DMA((4,)),
            ],
            moved=LATER if after else 0,
        )(
            in_hbm(queries),
            in_hbm(memory),
            in_hbm(hidden),
            in_hbm(target_pair.reshape(1, rows)),
            in_hbm(source_pair.reshape(1, rows)),
            in_hbm(routes.T),
            in_hbm(route_weight.T),
            *after,
        )

    packed = {}
    for steps in ((2,), (1,), (3, 0)):
        packed.update(zip(steps, pack(steps, *list(packed.values())[-1:])))
    messages = [along(packed[step], step) for step in ORDER]

    w_in, w_out, gain, bias = pl.pallas_call(
        functools.partial(prefetch_kernel, experts),
        out_shape=[
            pltpu.VMEM((model, hidden_units), BF16),
            pltpu.VMEM((hidden_units, model), BF16),
            pltpu.VMEM((1, model), F32),
            pltpu.VMEM((1, model), F32),
        ],
        in_specs=[IN_HBM] * 4 + [IN_ANY],
        out_specs=[IN_VMEM] * 4,
        scratch_shapes=[pltpu.SemaphoreType.DMA((2, 2 * experts))] * 2,
        compiler_params=pltpu.CompilerParams(vmem_limit_bytes=VMEM_LIMIT),
        cost_estimate=pl.CostEstimate(
            flops=0, bytes_accessed=8 * model * hidden_units, transcendentals=0
        ),
    )(
        in_hbm(expert_in[0]),
        in_hbm(expert_out[0]),
        in_hbm(norm_gain.reshape(1, model)),
        in_hbm(norm_bias.reshape(1, model)),
        packed[0],
    )

    compact = call(
        functools.partial(attend_kernel, experts, rows, cap),
        [struct(experts * cap + META, width)] * experts,
        [IN_VMEM] * (2 + experts),
        flops=8 * experts * experts * rows * rows * width,
        moved=16 * rows * columns,
    )(in_vmem(w_in), in_vmem(w_out), *messages)

    own = {step: along(block, step) for step, block in zip(ORDER, compact)}
    count = experts * cap

    def trim(block):
        return call(trim_kernel, [struct(count, width)], [IN_VMEM])(block)[0]

    trimmed = {step: trim(own[step]) for step in ORDER}
    far = {step: swap(own[step], "dp") for step in (2, 3)}
    far[1] = across(compact[2])
    far[0] = swap(compact[3], "dp")
    own_other = {step: swap(trimmed[step], "mp") for step in ORDER}

    def first(blocks, others, known):
        return call(
            functools.partial(first_kernel, 512),
            [struct(count, hidden_units)],
            [IN_VMEM] * (2 * experts + 3),
            scratch=[pltpu.VMEM((count, model), BF16)],
            flops=known * 2 * count * model * hidden_units,
            moved=known * 2 * model * hidden_units,
        )(
            *[blocks[step] for step in ORDER],
            *[others[step] for step in ORDER],
            in_vmem(gain),
            in_vmem(bias),
            in_vmem(w_in),
        )[0]

    def second(active, parts, known):
        kept, *sent = call(
            functools.partial(second_kernel, 512),
            [struct(count, columns)] + [struct(count // parts, columns)] * parts,
            [IN_VMEM, IN_VMEM],
            flops=known * 2 * count * model * hidden_units,
            moved=known * 2 * model * hidden_units,
        )(active, in_vmem(w_out))
        return kept, [swap(part, "mp") for part in sent]

    own_other[0], far[0], far[1] = lax.optimization_barrier((own_other[0], far[0], far[1]))
    active = first(own, own_other, 0)
    *late, active = lax.optimization_barrier((*[far[step] for step in ORDER], active))
    far = dict(zip(ORDER, late))
    far_other = {step: swap(far[step], "mp") for step in ORDER}
    mine, (theirs,) = second(first(far, far_other, 1), 1, 1)
    kept, got = second(active, experts, 0)
    arrived = [own[step] for step in ORDER]
    based = call(
        functools.partial(base_kernel, experts),
        [struct(cap, columns, F32)] * 2 + [struct(cap, HEAD, F32)] * 2,
        [IN_VMEM] * (3 + experts),
        scratch=[pltpu.VMEM((2 * cap, columns), F32)],
    )(kept, *got[2:], *arrived)
    plain = call(plain_kernel, [struct(2 * cap, columns)], [IN_VMEM] * 2)(mine, theirs)[0]
    joined = call(join_kernel, [struct(cap, columns)] * 2, [IN_VMEM] * 5)(swap(plain, "dp"), *based)
    near0, near1, away0, away1 = call(
        functools.partial(tail_kernel, experts),
        [struct(cap, columns)] * 4,
        [IN_VMEM] * (6 + experts) + [IN_ANY],
        scratch=[pltpu.VMEM((2 * cap, columns), F32)],
        moved=LATER,
    )(kept, *got[:2], *arrived, mine, theirs, far[0], joined[0])
    def mix(steps, blocks, dtype, *before):
        return call(
            functools.partial(mix_kernel, experts, cap, 512, steps),
            [struct(rows, columns, dtype)],
            [IN_VMEM] * (1 + len(blocks) + len(before)),
        )(routes.T, *blocks, *before)[0]

    share = mix((2, 3), [along(joined[0], 2), along(joined[1], 3)], F32)
    direct = [along(near1, 1), near0, across(away1), swap(away0, "dp")]
    return mix((1, 0, 1, 0), direct, BF16, share)


def shards(
    hidden,
    queries,
    memory,
    target_pair,
    source_pair,
    routes,
    route_weight,
    norm_gain,
    norm_bias,
    expert_in,
    expert_out,
):
    tok_rows = hidden.shape[0]
    local_heads = queries.shape[1] // HEAD
    scale = 1.0 / math.sqrt(HEAD)
    query_heads = queries.reshape(tok_rows, local_heads, HEAD)
    running = jnp.full((local_heads, tok_rows), NEGATIVE, jnp.float32)
    rows = lax.all_gather(memory, "expert", axis=0, tiled=True)
    row_pairs = lax.all_gather(source_pair, "expert", axis=0, tiled=True)
    count = rows.shape[0]
    keys = rows[:, 0, :].reshape(count, local_heads, HEAD)
    values = rows[:, 1, :].reshape(count, local_heads, HEAD)
    score = (
        jnp.einsum("thd,rhd->htr", query_heads, keys, preferred_element_type=jnp.float32) * scale
    )
    match = (target_pair[:, None] == row_pairs[None, :])[None]
    masked = jnp.where(match, score, NEGATIVE)
    newest = jnp.maximum(running, jnp.max(masked, axis=-1))
    weight = jnp.where(match, jnp.exp(masked - newest[:, :, None]), 0.0)
    total = jnp.sum(weight, axis=-1)
    summed = jnp.einsum(
        "htr,rhd->htd", weight.astype(jnp.bfloat16), values, preferred_element_type=jnp.float32
    )
    running, total, summed = (newest, total, summed)
    context = jnp.transpose(summed / total[:, :, None], (1, 0, 2)).reshape(
        tok_rows, local_heads * HEAD
    )
    attended = (hidden.astype(jnp.float32) + context).astype(jnp.bfloat16)
    full_rows = lax.all_gather(attended, "mp", axis=1, tiled=True)
    width = full_rows.shape[1]
    experts_all = lax.axis_size("expert")
    batches = lax.axis_size("dp")
    cap = 2 * tok_rows // experts_all * 5 // 4
    flat = routes.reshape(-1)
    named = (flat[:, None] == jnp.arange(experts_all, dtype=jnp.int32)[None, :]).astype(jnp.int32)
    slot = jnp.sum((jnp.cumsum(named, axis=0) - named) * named, axis=1)
    dest = flat * cap + slot
    place = dest[:, None] == jnp.arange(experts_all * cap, dtype=jnp.int32)[None, :]
    per_token = jnp.sum(place.reshape(tok_rows, 2, experts_all * cap).astype(jnp.bfloat16), axis=1)
    outgoing = lax.dot_general(
        per_token, full_rows, (((0,), (0,)), ((), ())), preferred_element_type=jnp.float32
    ).astype(jnp.bfloat16)
    copies = jnp.broadcast_to(
        outgoing.reshape(experts_all, 1, cap, width), (experts_all, batches, cap, width)
    ).reshape(experts_all * batches * cap, width)
    arrived = lax.all_to_all(copies, ("expert", "dp"), split_axis=0, concat_axis=0, tiled=True)
    values = arrived.astype(jnp.float32)
    center = jnp.mean(values, axis=-1, keepdims=True)
    spread = jnp.mean(jnp.square(values - center), axis=-1, keepdims=True)
    normed = ((values - center) * lax.rsqrt(spread + EPSILON) * norm_gain + norm_bias).astype(
        jnp.bfloat16
    )
    active = jax.nn.relu(jnp.dot(normed, expert_in[0], preferred_element_type=jnp.float32)).astype(
        jnp.bfloat16
    )
    partial_value = jnp.dot(active, expert_out[0], preferred_element_type=jnp.float32).astype(
        jnp.bfloat16
    )
    returned = lax.all_to_all(
        partial_value, ("expert", "dp"), split_axis=0, concat_axis=0, tiled=True
    )
    expert_sum = jnp.sum(
        returned.reshape(experts_all, batches, cap, width).astype(jnp.float32), axis=1
    )
    picked = jnp.dot(
        place.astype(jnp.float32),
        expert_sum.reshape(experts_all * cap, width),
        precision=lax.Precision.HIGHEST,
    )
    blended = jnp.sum(picked.reshape(tok_rows, 2, width) * route_weight[:, :, None], axis=1)
    share = lax.psum_scatter(
        blended.astype(jnp.bfloat16), "mp", scatter_dimension=1, tiled=True
    ).astype(jnp.float32)
    return (attended.astype(jnp.float32) + share).astype(jnp.bfloat16)


def layer(hidden, queries, memory, *rest):
    experts = lax.axis_size("expert")
    rows, columns = hidden.shape
    heads = columns // HEAD
    by_heads = (
        lax.axis_size("mp") == 2
        and lax.axis_size("dp") == 2
        and heads % experts == 0
        and memory.shape[0] == rows
        and experts * rows <= columns // experts
        and experts == 4
    )
    return (head_shards if by_heads else shards)(hidden, queries, memory, *rest)


def solution(mesh):
    return jax.shard_map(
        layer,
        mesh=mesh,
        in_specs=(
            P(("groups", "expert", "dp"), "mp"),
            P(("groups", "expert", "dp"), "mp"),
            P(("groups", "expert", "dp"), None, "mp"),
            P(("groups", "expert", "dp")),
            P(("groups", "expert", "dp")),
            P(("groups", "expert", "dp"), None),
            P(("groups", "expert", "dp"), None),
            P(),
            P(),
            P("expert", None, ("dp", "mp")),
            P("expert", ("dp", "mp"), None),
        ),
        out_specs=P(("groups", "expert", "dp"), "mp"),
        check_vma=False,
    )
```

```python
import functools
import math

import jax
import jax.numpy as jnp
from jax import lax
from jax.experimental import pallas as pl
from jax.experimental.pallas import tpu as pltpu
from jax.sharding import PartitionSpec as P

HEAD = 128
EPSILON = 1e-05
NEGATIVE = -1e30
META = 16
LATER = 16 * 1024 * 1024
MIB = 1024 * 1024
ORDER = (2, 3, 1, 0)
VMEM_LIMIT = 12 * 1024 * 1024

BF16 = jnp.bfloat16
F32 = jnp.float32
IN_VMEM = pl.BlockSpec(memory_space=pltpu.VMEM)
IN_ANY = pl.BlockSpec(memory_space=pl.ANY)
IN_HBM = pl.BlockSpec(memory_space=pltpu.HBM)


def struct(rows, columns, dtype=BF16):
    return jax.ShapeDtypeStruct((rows, columns), dtype)


def call(kernel, outs, specs, scratch=(), flops=0, moved=0):
    return pl.pallas_call(
        kernel,
        out_shape=outs,
        in_specs=specs,
        out_specs=[IN_VMEM] * len(outs),
        scratch_shapes=scratch,
        compiler_params=pltpu.CompilerParams(vmem_limit_bytes=VMEM_LIMIT),
        cost_estimate=pl.CostEstimate(flops=flops, bytes_accessed=moved, transcendentals=0),
    )


def dot(a, b):
    return lax.dot_general(a, b, (((1,), (0,)), ((), ())), preferred_element_type=F32)


def dot_nt(a, b):
    return lax.dot_general(a, b, (((1,), (1,)), ((), ())), preferred_element_type=F32)


def dot_tn(a, b):
    return lax.dot_general(a, b, (((0,), (0,)), ((), ())), preferred_element_type=F32)


def iota(shape, dimension):
    return lax.broadcasted_iota(jnp.int32, shape, dimension)


def in_hbm(array):
    return pltpu.with_memory_space_constraint(array, pltpu.HBM)


def in_vmem(array):
    return pltpu.with_memory_space_constraint(array, pltpu.VMEM)


def columns_at(start, width):
    return pl.ds(pl.multiple_of(start * width, width), width)


def thirds(array):
    high = array.astype(BF16).astype(F32)
    middle = (array - high).astype(BF16).astype(F32)
    low = (array - high - middle).astype(BF16).astype(F32)
    return [high, middle, low]


def pack_kernel(steps, q_hbm, m_hbm, h_hbm, tp_hbm, sp_hbm, r_hbm, rw_hbm, *refs):
    outs, refs = refs[-7 - len(steps) : -7], refs[-7:]
    m_ref, tp_ref, sp_ref, r_ref, rw_ref, sems, small_sems = refs
    rows, width = q_hbm.shape[0], outs[0].shape[1]
    here = lax.axis_index("expert")
    small = [
        pltpu.make_async_copy(src, dst, small_sems.at[k])
        for k, (src, dst) in enumerate(
            ((tp_hbm, tp_ref), (sp_hbm, sp_ref), (r_hbm, r_ref), (rw_hbm, rw_ref))
        )
    ]
    large = []
    for k, (step, out) in enumerate(zip(steps, outs)):
        cols = columns_at(here ^ step, width)
        large.append(
            (
                pltpu.make_async_copy(m_hbm.at[:, :, cols], m_ref.at[k], sems.at[0, k]),
                pltpu.make_async_copy(q_hbm.at[:, cols], out.at[pl.ds(0, rows)], sems.at[1, k]),
                pltpu.make_async_copy(
                    h_hbm.at[:, cols], out.at[pl.ds(3 * rows, rows)], sems.at[2, k]
                ),
            )
        )
    for copy in small:
        copy.start()
    for copies in large:
        for copy in copies:
            copy.start()
    for copy in small:
        copy.wait()
    row = iota((META, rows), 0)
    lines = [tp_ref[...], sp_ref[...], r_ref[0:1, :], r_ref[1:2, :]]
    lines = [line.astype(F32) for line in lines]
    lines += thirds(rw_ref[0:1, :]) + thirds(rw_ref[1:2, :])
    kinds = jnp.zeros((META, rows), F32)
    for k, line in enumerate(lines):
        kinds = jnp.where(row == k, line, kinds)
    kinds = kinds.astype(BF16)
    for step, out in zip(steps, outs):
        moved = (iota((rows, width), 1) == iota((rows, width), 0) + step * rows).astype(BF16)
        out[4 * rows :, :] = dot(kinds, moved).astype(BF16)
    for k, out in enumerate(outs):
        large[k][0].wait()
        out[rows : 2 * rows, :] = m_ref[k, :, 0, :]
        out[2 * rows : 3 * rows, :] = m_ref[k, :, 1, :]
    for copies in large:
        copies[1].wait()
        copies[2].wait()


def prefetch_kernel(experts, w1_hbm, w2_hbm, gain_hbm, bias_hbm, after_ref, *refs):
    w1_ref, w2_ref, gain_ref, bias_ref, sems, small_sems = refs
    here, half = lax.axis_index("expert"), lax.axis_index("mp")
    size = w1_ref.shape[0] // (2 * experts)
    copies = []
    for part in range(2 * experts):
        core = half if part < experts else 1 - half
        source = columns_at(core * experts + (here ^ ORDER[part % experts]), size)
        target = pl.ds(part * size, size)
        copies += [
            pltpu.make_async_copy(w1_hbm.at[source], w1_ref.at[target], sems.at[0, part]),
            pltpu.make_async_copy(w2_hbm.at[target], w2_ref.at[target], sems.at[1, part]),
            pltpu.make_async_copy(
                gain_hbm.at[:, source], gain_ref.at[:, target], small_sems.at[0, part]
            ),
            pltpu.make_async_copy(
                bias_hbm.at[:, source], bias_ref.at[:, target], small_sems.at[1, part]
            ),
        ]
    for copy in copies:
        copy.start()
    for copy in copies:
        copy.wait()


def attend_kernel(experts, rows, cap, w1_ref, w2_ref, *refs):
    arrived, compact = dict(zip(ORDER, refs[:experts])), refs[experts:]
    messages = [arrived[step] for step in range(experts)]
    width = messages[0].shape[1]
    count = experts * rows
    here = lax.axis_index("expert")
    meta = sum(m[4 * rows :, :].astype(F32) for m in messages)
    same = (iota((count, count), 0) == iota((count, count), 1)).astype(BF16)
    columns = dot_nt(same, meta.astype(BF16))
    match = columns[:, 0:1] == meta[1:2, :]
    scale = 1.0 / math.sqrt(HEAD)
    parts = []
    for head in range(width // HEAD):
        lanes = slice(head * HEAD, (head + 1) * HEAD)

        def stacked(kind):
            return jnp.concatenate(
                [m[kind * rows : (kind + 1) * rows, lanes] for m in messages], axis=0
            )

        score = dot_nt(stacked(0), stacked(1)) * scale
        masked = jnp.where(match, score, NEGATIVE)
        largest = jnp.max(masked, axis=-1, keepdims=True)
        weight = jnp.where(match, jnp.exp(masked - largest), 0.0)
        total = jnp.sum(weight, axis=-1, keepdims=True)
        context = dot(weight.astype(BF16), stacked(2)) / total
        parts.append((stacked(3).astype(F32) + context).astype(BF16))
    states = jnp.concatenate(parts, axis=1)
    first, second = meta[2:3, :].astype(jnp.int32), meta[3:4, :].astype(jnp.int32)
    expert = here ^ iota((META, count), 0)
    named = ((first == expert) | (second == expert)) & (iota((META, count), 0) < experts)
    before = (iota((count, count), 0) < iota((count, count), 1)) & (
        iota((count, count), 0) // rows == iota((count, count), 1) // rows
    )
    slot = dot(named.astype(BF16), before.astype(BF16)).astype(jnp.int32)
    block = (iota((META, count), 1) // rows) ^ iota((META, count), 0)
    spot = jnp.where(named, block * cap + slot, -1)
    for step, out in zip(ORDER, compact):
        place = iota((experts * cap, count), 0) == spot[step : step + 1, :]
        place = place.astype(BF16)
        out[0 : experts * cap, :] = dot(place, states).astype(BF16)
        leads = first == (here ^ step)
        values = [jnp.where(leads, meta[4 + k : 5 + k, :], meta[7 + k : 8 + k, :]) for k in range(3)]
        values.append(leads.astype(F32))
        lines = jnp.zeros((META, count), F32)
        for k, value in enumerate(values):
            lines = jnp.where(iota((META, count), 0) == k, value, lines)
        out[experts * cap :, :] = jnp.zeros((META, width), BF16)
        out[experts * cap :, 0 : experts * cap] = dot_nt(lines.astype(BF16), place).astype(BF16)


def copy_kernel(block_ref, out_ref):
    out_ref[...] = block_ref[...]


def trim_kernel(block_ref, out_ref):
    out_ref[...] = block_ref[0 : out_ref.shape[0], :]


def pair_kernel(left_ref, right_ref, out_ref):
    rows, width = slice(0, out_ref.shape[0]), left_ref.shape[1]
    out_ref[:, 0:width] = left_ref[rows, :]
    out_ref[:, width:] = right_ref[rows, :]


def first_kernel(tile, *refs):
    blocks, (gain_ref, bias_ref, w_ref, out_ref, n_ref) = refs[:-5], refs[-5:]
    width, model = min(block.shape[1] for block in blocks), n_ref.shape[1]
    pieces = [
        (block, slice(at, at + width)) for block in blocks for at in range(0, block.shape[1], width)
    ]
    for at in range(0, n_ref.shape[0], META):
        rows = slice(at, at + META)
        values = [block[rows, cols].astype(F32) for block, cols in pieces]
        center = jnp.sum(sum(values), axis=-1, keepdims=True) * (1.0 / model)
        shifted = [value - center for value in values]
        spread = sum(value * value for value in shifted)
        spread = jnp.sum(spread, axis=-1, keepdims=True) * (1.0 / model)
        scale = lax.rsqrt(spread + EPSILON)
        for k, value in enumerate(shifted):
            cols = slice(k * width, (k + 1) * width)
            normed = value * scale * gain_ref[:, cols] + bias_ref[:, cols]
            n_ref[rows, cols] = normed.astype(BF16)
    for at in range(0, w_ref.shape[1], tile):
        cols = slice(at, at + tile)
        out_ref[:, cols] = jnp.maximum(dot(n_ref[...], w_ref[:, cols]), 0.0).astype(BF16)


def second_kernel(tile, a_ref, w_ref, kept_ref, *sent):
    columns, rows = kept_ref.shape[1], sent[0].shape[0]
    lower = lax.axis_index("mp") == 0
    for at in range(0, columns, tile):
        low = dot(a_ref[...], w_ref[:, at : at + tile])
        high = dot(a_ref[...], w_ref[:, columns + at : columns + at + tile])
        kept_ref[:, at : at + tile] = jnp.where(lower, low, high).astype(BF16)
        other = jnp.where(lower, high, low).astype(BF16)
        for k, out_ref in enumerate(sent):
            out_ref[:, at : at + tile] = other[k * rows : (k + 1) * rows, :]


def half_kernel(tile, other, a_ref, w_ref, *outs):
    columns, rows = outs[0].shape[1], outs[0].shape[0]
    half = lax.axis_index("mp")
    half = 1 - half if other else half
    for at in range(columns // tile):
        part = dot(a_ref[...], w_ref[:, columns_at(half * (columns // tile) + at, tile)])
        for k, out_ref in enumerate(outs):
            out_ref[:, at * tile : (at + 1) * tile] = part[k * rows : (k + 1) * rows, :].astype(BF16)


def row_factors(lines_ref, count):
    same = (iota((count, count), 0) == iota((count, count), 1)).astype(BF16)
    columns = dot_nt(same, lines_ref[count:, 0:count])
    return columns[:, 0:1] + columns[:, 1:2] + columns[:, 2:3], columns[:, 3:4]


def plain_kernel(kept_ref, got_ref, *outs):
    cap = outs[0].shape[0]
    for k, out_ref in enumerate(outs):
        rows, half = slice((2 + k) * cap, (3 + k) * cap), slice(k * cap, (k + 1) * cap)
        total = kept_ref[rows, :].astype(F32) + got_ref[half, :].astype(F32)
        out_ref[...] = total.astype(BF16)


def gather_states(blocks, states, rows):
    here = lax.axis_index("expert")
    width = blocks[0].shape[1]
    for step, block in zip(ORDER, blocks):
        states[:, columns_at(here ^ step, width)] = block[rows, :].astype(F32)


def base_kernel(experts, kept_ref, *refs):
    got_ref, blocks, refs = refs[0], refs[1 : 1 + experts], refs[1 + experts :]
    bases, factors, states = refs[:2], refs[2:4], refs[4]
    count = kept_ref.shape[0]
    cap = count // experts
    weight, leads = row_factors(blocks[-1], count)
    gather_states(blocks, states, slice(2 * cap, 4 * cap))
    for k in range(2):
        rows, half = slice((2 + k) * cap, (3 + k) * cap), slice(k * cap, (k + 1) * cap)
        total = kept_ref[rows, :].astype(F32) + got_ref[half, :].astype(F32)
        bases[k][...] = total * weight[rows, :] + leads[rows, :] * states[half, :]
        factors[k][...] = jnp.broadcast_to(weight[rows, :], (cap, HEAD))


def tail_kernel(experts, kept_ref, *refs):
    got_ref, blocks, refs = refs[0], refs[1 : 1 + experts], refs[1 + experts :]
    far_kept_ref, far_got_ref, lines_ref, _, near0, near1, far0, far1, states = refs
    count = kept_ref.shape[0]
    cap = count // experts
    weight, leads = row_factors(blocks[-1], count)
    far_weight, _ = row_factors(lines_ref, count)
    gather_states(blocks, states, slice(0, 2 * cap))
    for k, (near, far) in enumerate(((near0, far0), (near1, far1))):
        rows = slice(k * cap, (k + 1) * cap)
        total = kept_ref[rows, :].astype(F32) + got_ref[rows, :].astype(F32)
        total = total * weight[rows, :] + leads[rows, :] * states[rows, :]
        near[...] = total.astype(BF16)
        total = far_kept_ref[rows, :].astype(F32) + far_got_ref[rows, :].astype(F32)
        far[...] = (total * far_weight[rows, :]).astype(BF16)


def join_kernel(came_ref, base_ref, factor_ref, out_ref):
    total = base_ref[...] + factor_ref[:, 0:1] * came_ref[...].astype(F32)
    out_ref[...] = total.astype(BF16)


def mix_kernel(experts, cap, tile, steps, routes_ref, *refs):
    returned, refs = refs[: len(steps)], refs[len(steps) :]
    out_ref = refs[-1]
    rows = out_ref.shape[0]
    expert = lax.axis_index("expert") ^ iota((META, rows), 0)
    named = (routes_ref[0:1, :] == expert) | (routes_ref[1:2, :] == expert)
    named = named & (iota((META, rows), 0) < experts)
    before = (iota((rows, rows), 0) < iota((rows, rows), 1)).astype(BF16)
    slot = jnp.where(named, dot(named.astype(BF16), before), -1.0)
    same = (iota((rows, rows), 0) == iota((rows, rows), 1)).astype(BF16)
    slot = dot_nt(same, slot.astype(BF16)).astype(jnp.int32)
    place = {
        step: (iota((rows, cap), 1) == slot[:, step : step + 1]).astype(BF16) for step in set(steps)
    }
    for at in range(0, out_ref.shape[1], tile):
        cols = slice(at, at + tile)
        share = refs[0][:, cols] if len(refs) > 1 else jnp.zeros((rows, tile), F32)
        for step, block in zip(steps, returned):
            share = share + dot(place[step], block[:, cols])
        out_ref[:, cols] = share.astype(out_ref.dtype)


def head_shards(
    hidden,
    queries,
    memory,
    target_pair,
    source_pair,
    routes,
    route_weight,
    norm_gain,
    norm_bias,
    expert_in,
    expert_out,
):
    rows, columns = hidden.shape
    experts = lax.axis_size("expert")
    width = columns // experts
    cap = 2 * rows // experts * 5 // 4
    model = 2 * columns
    hidden_units = expert_in.shape[2]

    def along(array, step):
        if step == 0:
            return array
        return lax.ppermute(array, "expert", [(i, i ^ step) for i in range(experts)])

    def swap(array, axis):
        return lax.ppermute(array, axis, [(0, 1), (1, 0)])

    def across(array):
        pairs = [(2 * i + j, 2 * (i ^ 1) + 1 - j) for i in range(experts) for j in range(2)]
        return lax.ppermute(array, ("expert", "dp"), pairs)

    def pack(steps, *after):
        return call(
            functools.partial(pack_kernel, steps),
            [struct(4 * rows + META, width)] * len(steps),
            [IN_HBM] * 7 + [IN_ANY] * len(after),
            scratch=[
                pltpu.VMEM((len(steps), rows, 2, width), BF16),
                pltpu.VMEM((1, rows), jnp.int32),
                pltpu.VMEM((1, rows), jnp.int32),
                pltpu.VMEM((2, rows), jnp.int32),
                pltpu.VMEM((2, rows), F32),
                pltpu.SemaphoreType.DMA((3, len(steps))),
                pltpu.SemaphoreType.DMA((4,)),
            ],
            moved=LATER if after else 0,
        )(
            in_hbm(queries),
            in_hbm(memory),
            in_hbm(hidden),
            in_hbm(target_pair.reshape(1, rows)),
            in_hbm(source_pair.reshape(1, rows)),
            in_hbm(routes.T),
            in_hbm(route_weight.T),
            *after,
        )

    packed = {}
    for steps in ((2,), (1,), (3, 0)):
        packed.update(zip(steps, pack(steps, *list(packed.values())[-1:])))
    messages = [along(packed[step], step) for step in ORDER]

    w_in, w_out, gain, bias = pl.pallas_call(
        functools.partial(prefetch_kernel, experts),
        out_shape=[
            pltpu.VMEM((model, hidden_units), BF16),
            pltpu.VMEM((hidden_units, model), BF16),
            pltpu.VMEM((1, model), F32),
            pltpu.VMEM((1, model), F32),
        ],
        in_specs=[IN_HBM] * 4 + [IN_ANY],
        out_specs=[IN_VMEM] * 4,
        scratch_shapes=[pltpu.SemaphoreType.DMA((2, 2 * experts))] * 2,
        compiler_params=pltpu.CompilerParams(vmem_limit_bytes=VMEM_LIMIT),
        cost_estimate=pl.CostEstimate(
            flops=0, bytes_accessed=8 * model * hidden_units, transcendentals=0
        ),
    )(
        in_hbm(expert_in[0]),
        in_hbm(expert_out[0]),
        in_hbm(norm_gain.reshape(1, model)),
        in_hbm(norm_bias.reshape(1, model)),
        packed[0],
    )

    compact = call(
        functools.partial(attend_kernel, experts, rows, cap),
        [struct(experts * cap + META, width)] * experts,
        [IN_VMEM] * (2 + experts),
        flops=8 * experts * experts * rows * rows * width,
        moved=16 * rows * columns,
    )(in_vmem(w_in), in_vmem(w_out), *messages)

    def ahead(block, mib):
        return call(copy_kernel, [struct(*block.shape)], [IN_VMEM], moved=mib * MIB)(block)[0]

    compact = dict(zip(ORDER, compact))
    own = {step: along(compact[step], step) for step in ORDER}
    count = experts * cap

    def trim(block):
        return call(trim_kernel, [struct(count, width)], [IN_VMEM])(block)[0]

    def first(blocks, known):
        return call(
            functools.partial(first_kernel, 512),
            [struct(count, hidden_units)],
            [IN_VMEM] * (len(blocks) + 3),
            scratch=[pltpu.VMEM((count, model), BF16)],
            flops=known * 2 * count * model * hidden_units,
            moved=known * 2 * model * hidden_units,
        )(*blocks, in_vmem(gain), in_vmem(bias), in_vmem(w_in))[0]

    def pair(left, right):
        return call(pair_kernel, [struct(count, 2 * width)], [IN_VMEM] * 2)(left, right)[0]

    trimmed = [trim(own[step]) for step in ORDER]
    far1, far0 = across(compact[1]), swap(compact[0], "dp")
    near = pair(own[2], own[3])
    far = swap(near, "dp")
    trimmed[2], far1, far0 = lax.optimization_barrier((trimmed[2], far1, far0))
    near_other = [swap(block, "mp") for block in trimmed]
    far1_other, far0_other = swap(far1, "mp"), swap(far0, "mp")
    active = first([near, own[1], own[0], *near_other], 0)
    far, active = lax.optimization_barrier((far, active))
    far_other = swap(far, "mp")
    kept, *sent = call(
        functools.partial(second_kernel, 512),
        [struct(count, columns)] + [struct(count // 2, columns)] * 2,
        [IN_VMEM, IN_VMEM],
    )(active, in_vmem(w_out))
    got = [swap(part, "mp") for part in sent]
    far_other, kept = lax.optimization_barrier((far_other, kept))

    active = first([far, far1, far0, far_other, far1_other, far0_other], 1)
    active, *got = lax.optimization_barrier((active, *got))

    def half(active, other, parts):
        return call(
            functools.partial(half_kernel, 512, other),
            [struct(count // parts, columns)] * parts,
            [IN_VMEM, IN_VMEM],
            flops=count * model * hidden_units,
            moved=model * hidden_units,
        )(active, in_vmem(w_out))

    theirs = [swap(part, "mp") for part in half(active, True, 2)]
    mine = half(active, False, 1)[0]
    arrived = [own[step] for step in ORDER]
    base2, base3, factor2, factor3 = call(
        functools.partial(base_kernel, experts),
        [struct(cap, columns, F32)] * 2 + [struct(cap, HEAD, F32)] * 2,
        [IN_VMEM] * (2 + experts),
        scratch=[pltpu.VMEM((2 * cap, columns), F32)],
    )(kept, got[1], *arrived)
    theirs[1], base2 = lax.optimization_barrier((theirs[1], base2))
    plain2, plain3 = call(plain_kernel, [struct(cap, columns)] * 2, [IN_VMEM] * 2)(mine, theirs[1])

    def join(came, base, factor, mib):
        return call(join_kernel, [struct(cap, columns)], [IN_VMEM] * 3, moved=mib * MIB)(
            came, base, factor
        )[0]

    joined2 = join(swap(plain2, "dp"), base2, factor2, 4)
    joined3 = join(swap(plain3, "dp"), base3, factor3, 0)
    near0, near1, away0, away1 = call(
        functools.partial(tail_kernel, experts),
        [struct(cap, columns)] * 4,
        [IN_VMEM] * (5 + experts) + [IN_ANY],
        scratch=[pltpu.VMEM((2 * cap, columns), F32)],
        moved=2 * LATER,
    )(kept, got[0], *arrived, mine, theirs[0], far0, plain3)

    def mix(steps, blocks, dtype, *before):
        return call(
            functools.partial(mix_kernel, experts, cap, 512, steps),
            [struct(rows, columns, dtype)],
            [IN_VMEM] * (1 + len(blocks) + len(before)),
        )(routes.T, *blocks, *before)[0]

    direct = [along(near1, 1), near0, across(away1), swap(away0, "dp")]
    share = mix((1, 0, 1, 0), direct, F32)
    return mix((2, 3), [along(joined2, 2), along(joined3, 3)], BF16, share)


def shards(
    hidden,
    queries,
    memory,
    target_pair,
    source_pair,
    routes,
    route_weight,
    norm_gain,
    norm_bias,
    expert_in,
    expert_out,
):
    tok_rows = hidden.shape[0]
    local_heads = queries.shape[1] // HEAD
    scale = 1.0 / math.sqrt(HEAD)
    query_heads = queries.reshape(tok_rows, local_heads, HEAD)
    running = jnp.full((local_heads, tok_rows), NEGATIVE, jnp.float32)
    rows = lax.all_gather(memory, "expert", axis=0, tiled=True)
    row_pairs = lax.all_gather(source_pair, "expert", axis=0, tiled=True)
    count = rows.shape[0]
    keys = rows[:, 0, :].reshape(count, local_heads, HEAD)
    values = rows[:, 1, :].reshape(count, local_heads, HEAD)
    score = (
        jnp.einsum("thd,rhd->htr", query_heads, keys, preferred_element_type=jnp.float32) * scale
    )
    match = (target_pair[:, None] == row_pairs[None, :])[None]
    masked = jnp.where(match, score, NEGATIVE)
    newest = jnp.maximum(running, jnp.max(masked, axis=-1))
    weight = jnp.where(match, jnp.exp(masked - newest[:, :, None]), 0.0)
    total = jnp.sum(weight, axis=-1)
    summed = jnp.einsum(
        "htr,rhd->htd", weight.astype(jnp.bfloat16), values, preferred_element_type=jnp.float32
    )
    running, total, summed = (newest, total, summed)
    context = jnp.transpose(summed / total[:, :, None], (1, 0, 2)).reshape(
        tok_rows, local_heads * HEAD
    )
    attended = (hidden.astype(jnp.float32) + context).astype(jnp.bfloat16)
    full_rows = lax.all_gather(attended, "mp", axis=1, tiled=True)
    width = full_rows.shape[1]
    experts_all = lax.axis_size("expert")
    batches = lax.axis_size("dp")
    cap = 2 * tok_rows // experts_all * 5 // 4
    flat = routes.reshape(-1)
    named = (flat[:, None] == jnp.arange(experts_all, dtype=jnp.int32)[None, :]).astype(jnp.int32)
    slot = jnp.sum((jnp.cumsum(named, axis=0) - named) * named, axis=1)
    dest = flat * cap + slot
    place = dest[:, None] == jnp.arange(experts_all * cap, dtype=jnp.int32)[None, :]
    per_token = jnp.sum(place.reshape(tok_rows, 2, experts_all * cap).astype(jnp.bfloat16), axis=1)
    outgoing = lax.dot_general(
        per_token, full_rows, (((0,), (0,)), ((), ())), preferred_element_type=jnp.float32
    ).astype(jnp.bfloat16)
    copies = jnp.broadcast_to(
        outgoing.reshape(experts_all, 1, cap, width), (experts_all, batches, cap, width)
    ).reshape(experts_all * batches * cap, width)
    arrived = lax.all_to_all(copies, ("expert", "dp"), split_axis=0, concat_axis=0, tiled=True)
    values = arrived.astype(jnp.float32)
    center = jnp.mean(values, axis=-1, keepdims=True)
    spread = jnp.mean(jnp.square(values - center), axis=-1, keepdims=True)
    normed = ((values - center) * lax.rsqrt(spread + EPSILON) * norm_gain + norm_bias).astype(
        jnp.bfloat16
    )
    active = jax.nn.relu(jnp.dot(normed, expert_in[0], preferred_element_type=jnp.float32)).astype(
        jnp.bfloat16
    )
    partial_value = jnp.dot(active, expert_out[0], preferred_element_type=jnp.float32).astype(
        jnp.bfloat16
    )
    returned = lax.all_to_all(
        partial_value, ("expert", "dp"), split_axis=0, concat_axis=0, tiled=True
    )
    expert_sum = jnp.sum(
        returned.reshape(experts_all, batches, cap, width).astype(jnp.float32), axis=1
    )
    picked = jnp.dot(
        place.astype(jnp.float32),
        expert_sum.reshape(experts_all * cap, width),
        precision=lax.Precision.HIGHEST,
    )
    blended = jnp.sum(picked.reshape(tok_rows, 2, width) * route_weight[:, :, None], axis=1)
    share = lax.psum_scatter(
        blended.astype(jnp.bfloat16), "mp", scatter_dimension=1, tiled=True
    ).astype(jnp.float32)
    return (attended.astype(jnp.float32) + share).astype(jnp.bfloat16)


def layer(hidden, queries, memory, *rest):
    experts = lax.axis_size("expert")
    rows, columns = hidden.shape
    heads = columns // HEAD
    by_heads = (
        lax.axis_size("mp") == 2
        and lax.axis_size("dp") == 2
        and heads % experts == 0
        and memory.shape[0] == rows
        and experts * rows <= columns // experts
        and experts == 4
    )
    return (head_shards if by_heads else shards)(hidden, queries, memory, *rest)


def solution(mesh):
    return jax.shard_map(
        layer,
        mesh=mesh,
        in_specs=(
            P(("groups", "expert", "dp"), "mp"),
            P(("groups", "expert", "dp"), "mp"),
            P(("groups", "expert", "dp"), None, "mp"),
            P(("groups", "expert", "dp")),
            P(("groups", "expert", "dp")),
            P(("groups", "expert", "dp"), None),
            P(("groups", "expert", "dp"), None),
            P(),
            P(),
            P("expert", None, ("dp", "mp")),
            P("expert", ("dp", "mp"), None),
        ),
        out_specs=P(("groups", "expert", "dp"), "mp"),
        check_vma=False,
    )
```

```python
import functools
import math

import jax
import jax.numpy as jnp
from jax import lax
from jax.experimental import pallas as pl
from jax.experimental.pallas import tpu as pltpu
from jax.sharding import PartitionSpec as P

HEAD = 128
EPSILON = 1e-05
NEGATIVE = -1e30
META = 16
KINDS = 8
LATER = 16 * 1024 * 1024
MIB = 1024 * 1024
ORDER = (2, 3, 1, 0)
PAIRS = ((2, 3), (1, 0))
VMEM_LIMIT = 12 * 1024 * 1024

BF16 = jnp.bfloat16
F32 = jnp.float32
IN_VMEM = pl.BlockSpec(memory_space=pltpu.VMEM)
IN_ANY = pl.BlockSpec(memory_space=pl.ANY)
IN_HBM = pl.BlockSpec(memory_space=pltpu.HBM)


def struct(rows, columns, dtype=BF16):
    return jax.ShapeDtypeStruct((rows, columns), dtype)


def call(kernel, outs, specs, scratch=(), flops=0, moved=0):
    return pl.pallas_call(
        kernel,
        out_shape=outs,
        in_specs=specs,
        out_specs=[IN_VMEM] * len(outs),
        scratch_shapes=scratch,
        compiler_params=pltpu.CompilerParams(vmem_limit_bytes=VMEM_LIMIT),
        cost_estimate=pl.CostEstimate(flops=flops, bytes_accessed=moved, transcendentals=0),
    )


def dot(a, b):
    return lax.dot_general(a, b, (((1,), (0,)), ((), ())), preferred_element_type=F32)


def dot_nt(a, b):
    return lax.dot_general(a, b, (((1,), (1,)), ((), ())), preferred_element_type=F32)


def dot_tn(a, b):
    return lax.dot_general(a, b, (((0,), (0,)), ((), ())), preferred_element_type=F32)


def iota(shape, dimension):
    return lax.broadcasted_iota(jnp.int32, shape, dimension)


def in_hbm(array):
    return pltpu.with_memory_space_constraint(array, pltpu.HBM)


def in_vmem(array):
    return pltpu.with_memory_space_constraint(array, pltpu.VMEM)


def columns_at(start, width):
    return pl.ds(pl.multiple_of(start * width, width), width)


def halves(array):
    high = array.astype(BF16).astype(F32)
    return [high, (array - high).astype(BF16).astype(F32)]


def pack_kernel(steps, q_hbm, m_hbm, h_hbm, tp_hbm, sp_hbm, r_hbm, rw_hbm, *refs):
    outs, refs = refs[-7 - len(steps) : -7], refs[-7:]
    m_ref, tp_ref, sp_ref, r_ref, rw_ref, sems, small_sems = refs
    rows, width = q_hbm.shape[0], outs[0].shape[1]
    here = lax.axis_index("expert")
    small = [
        pltpu.make_async_copy(src, dst, small_sems.at[k])
        for k, (src, dst) in enumerate(
            ((tp_hbm, tp_ref), (sp_hbm, sp_ref), (r_hbm, r_ref), (rw_hbm, rw_ref))
        )
    ]
    large = []
    for k, (step, out) in enumerate(zip(steps, outs)):
        cols = columns_at(here ^ step, width)
        large.append(
            (
                pltpu.make_async_copy(m_hbm.at[:, :, cols], m_ref.at[k], sems.at[0, k]),
                pltpu.make_async_copy(q_hbm.at[:, cols], out.at[pl.ds(0, rows)], sems.at[1, k]),
                pltpu.make_async_copy(
                    h_hbm.at[:, cols], out.at[pl.ds(3 * rows, rows)], sems.at[2, k]
                ),
            )
        )
    for copy in small:
        copy.start()
    for copies in large:
        for copy in copies:
            copy.start()
    for copy in small:
        copy.wait()
    row = iota((META, rows), 0)
    lines = [tp_ref[...], sp_ref[...], r_ref[0:1, :], r_ref[1:2, :]]
    lines = [line.astype(F32) for line in lines]
    lines += halves(rw_ref[0:1, :]) + halves(rw_ref[1:2, :])
    kinds = jnp.zeros((META, rows), F32)
    for k, line in enumerate(lines):
        kinds = jnp.where(row == k, line, kinds)
    kinds = kinds.astype(BF16)
    for step, out in zip(steps, outs):
        moved = (iota((rows, width), 1) == iota((rows, width), 0) + step * rows).astype(BF16)
        out[4 * rows :, :] = dot(kinds, moved)[0:KINDS, :].astype(BF16)
    for k, out in enumerate(outs):
        large[k][0].wait()
        out[rows : 2 * rows, :] = m_ref[k, :, 0, :]
        out[2 * rows : 3 * rows, :] = m_ref[k, :, 1, :]
    for copies in large:
        copies[1].wait()
        copies[2].wait()


def prefetch_kernel(experts, w1_hbm, w2_hbm, gain_hbm, bias_hbm, after_ref, *refs):
    w1_ref, w2_ref, gain_ref, bias_ref, sems, small_sems = refs
    here, half = lax.axis_index("expert"), lax.axis_index("mp")
    size = w1_ref.shape[0] // (2 * experts)
    copies = []
    for part in range(2 * experts):
        core = half if part < experts else 1 - half
        source = columns_at(core * experts + (here ^ ORDER[part % experts]), size)
        target = pl.ds(part * size, size)
        copies += [
            pltpu.make_async_copy(w1_hbm.at[source], w1_ref.at[target], sems.at[0, part]),
            pltpu.make_async_copy(w2_hbm.at[target], w2_ref.at[target], sems.at[1, part]),
            pltpu.make_async_copy(
                gain_hbm.at[:, source], gain_ref.at[:, target], small_sems.at[0, part]
            ),
            pltpu.make_async_copy(
                bias_hbm.at[:, source], bias_ref.at[:, target], small_sems.at[1, part]
            ),
        ]
    for copy in copies:
        copy.start()
    for copy in copies:
        copy.wait()


def attend_kernel(experts, rows, cap, w1_ref, w2_ref, *refs):
    arrived, compact, factor_ref = dict(zip(ORDER, refs[:experts])), refs[experts:-1], refs[-1]
    messages = [arrived[step] for step in range(experts)]
    width = messages[0].shape[1]
    count = experts * rows
    here = lax.axis_index("expert")
    meta = sum(m[4 * rows :, :].astype(F32) for m in messages)
    same = (iota((count, count), 0) == iota((count, count), 1)).astype(BF16)
    columns = dot_nt(same, meta.astype(BF16))
    match = columns[:, 0:1] == meta[1:2, :]
    scale = 1.0 / math.sqrt(HEAD)
    parts = []
    for head in range(width // HEAD):
        lanes = slice(head * HEAD, (head + 1) * HEAD)

        def stacked(kind):
            return jnp.concatenate(
                [m[kind * rows : (kind + 1) * rows, lanes] for m in messages], axis=0
            )

        score = dot_nt(stacked(0), stacked(1)) * scale
        masked = jnp.where(match, score, NEGATIVE)
        largest = jnp.max(masked, axis=-1, keepdims=True)
        weight = jnp.where(match, jnp.exp(masked - largest), 0.0)
        total = jnp.sum(weight, axis=-1, keepdims=True)
        context = dot(weight.astype(BF16), stacked(2)) / total
        parts.append((stacked(3).astype(F32) + context).astype(BF16))
    states = jnp.concatenate(parts, axis=1)
    first, second = meta[2:3, :].astype(jnp.int32), meta[3:4, :].astype(jnp.int32)
    expert = here ^ iota((META, count), 0)
    named = ((first == expert) | (second == expert)) & (iota((META, count), 0) < experts)
    before = (iota((count, count), 0) < iota((count, count), 1)) & (
        iota((count, count), 0) // rows == iota((count, count), 1) // rows
    )
    slot = dot(named.astype(BF16), before.astype(BF16)).astype(jnp.int32)
    block = (iota((META, count), 1) // rows) ^ iota((META, count), 0)
    spot = jnp.where(named, block * cap + slot, -1)
    for step, out in zip(ORDER, compact):
        place = iota((experts * cap, count), 0) == spot[step : step + 1, :]
        place = place.astype(BF16)
        out[...] = dot(place, states).astype(BF16)
    leads = first == here
    lines = jnp.where(iota((META, count), 0) == 3, leads.astype(F32), 0.0)
    for k in range(2):
        half = jnp.where(leads, meta[4 + k : 5 + k, :], meta[6 + k : 7 + k, :])
        lines = jnp.where(iota((META, count), 0) == k, half, lines)
    factor_ref[...] = jnp.zeros(factor_ref.shape, F32)
    factor_ref[:, 0:META] = dot_nt(place, lines.astype(BF16))


def pair_kernel(left_ref, right_ref, out_ref):
    width = left_ref.shape[1]
    out_ref[:, 0:width] = left_ref[...]
    out_ref[:, width:] = right_ref[...]


def first_kernel(tile, *refs):
    blocks, (gain_ref, bias_ref, w_ref, out_ref, n_ref) = refs[:-5], refs[-5:]
    width, model = min(block.shape[1] for block in blocks), n_ref.shape[1]
    pieces = [
        (block, slice(at, at + width)) for block in blocks for at in range(0, block.shape[1], width)
    ]
    for at in range(0, n_ref.shape[0], META):
        rows = slice(at, at + META)
        values = [block[rows, cols].astype(F32) for block, cols in pieces]
        center = jnp.sum(sum(values), axis=-1, keepdims=True) * (1.0 / model)
        shifted = [value - center for value in values]
        spread = sum(value * value for value in shifted)
        spread = jnp.sum(spread, axis=-1, keepdims=True) * (1.0 / model)
        scale = lax.rsqrt(spread + EPSILON)
        for k, value in enumerate(shifted):
            cols = slice(k * width, (k + 1) * width)
            normed = value * scale * gain_ref[:, cols] + bias_ref[:, cols]
            n_ref[rows, cols] = normed.astype(BF16)
    for at in range(0, w_ref.shape[1], tile):
        cols = slice(at, at + tile)
        out_ref[:, cols] = jnp.maximum(dot(n_ref[...], w_ref[:, cols]), 0.0).astype(BF16)


def second_kernel(tile, a_ref, w_ref, kept_ref, *sent):
    columns, rows = kept_ref.shape[1], sent[0].shape[0]
    lower = lax.axis_index("mp") == 0
    for at in range(0, columns, tile):
        low = dot(a_ref[...], w_ref[:, at : at + tile])
        high = dot(a_ref[...], w_ref[:, columns + at : columns + at + tile])
        kept_ref[:, at : at + tile] = jnp.where(lower, low, high).astype(BF16)
        other = jnp.where(lower, high, low).astype(BF16)
        for k, out_ref in enumerate(sent):
            out_ref[:, at : at + tile] = other[k * rows : (k + 1) * rows, :]


def half_kernel(tile, other, a_ref, w_ref, *outs):
    columns, rows = outs[0].shape[1], outs[0].shape[0]
    half = lax.axis_index("mp")
    half = 1 - half if other else half
    for at in range(columns // tile):
        part = dot(a_ref[...], w_ref[:, columns_at(half * (columns // tile) + at, tile)])
        for k, out_ref in enumerate(outs):
            out_ref[:, at * tile : (at + 1) * tile] = part[k * rows : (k + 1) * rows, :].astype(BF16)


def plain_kernel(start, kept_ref, got_ref, *outs):
    cap = outs[0].shape[0]
    for k, out_ref in enumerate(outs):
        rows, half = slice(start + k * cap, start + (k + 1) * cap), slice(k * cap, (k + 1) * cap)
        total = kept_ref[rows, :].astype(F32) + got_ref[half, :].astype(F32)
        out_ref[...] = total.astype(BF16)


def base_kernel(start, kept_ref, got_ref, factor_ref, *refs):
    blocks, bases, factors, states = refs[: len(PAIRS)], refs[-5:-3], refs[-3:-1], refs[-1]
    here = lax.axis_index("expert")
    cap, width = bases[0].shape[0], blocks[0].shape[1] // 2
    for steps, block in zip(PAIRS, blocks):
        for k, step in enumerate(steps):
            piece = block[start : start + 2 * cap, k * width : (k + 1) * width]
            states[:, columns_at(here ^ step, width)] = piece.astype(F32)
    for k in range(2):
        rows, half = slice(start + k * cap, start + (k + 1) * cap), slice(k * cap, (k + 1) * cap)
        weight = factor_ref[rows, 0:1] + factor_ref[rows, 1:2]
        total = kept_ref[rows, :].astype(F32) + got_ref[half, :].astype(F32)
        bases[k][...] = total * weight + factor_ref[rows, 3:4] * states[half, :]
        factors[k][...] = jnp.broadcast_to(weight, factors[k].shape)


def join_kernel(came_ref, base_ref, factor_ref, out_ref):
    total = base_ref[...] + factor_ref[:, 0:1] * came_ref[...].astype(F32)
    out_ref[...] = total.astype(BF16)


def mix_kernel(experts, cap, tile, steps, routes_ref, *refs):
    returned, (out_hbm, out_ref, sems) = refs[:-3], refs[-3:]
    rows = out_ref.shape[0]
    copies = []
    expert = lax.axis_index("expert") ^ iota((META, rows), 0)
    named = (routes_ref[0:1, :] == expert) | (routes_ref[1:2, :] == expert)
    named = named & (iota((META, rows), 0) < experts)
    before = (iota((rows, rows), 0) < iota((rows, rows), 1)).astype(BF16)
    slot = jnp.where(named, dot(named.astype(BF16), before), -1.0)
    same = (iota((rows, rows), 0) == iota((rows, rows), 1)).astype(BF16)
    slot = dot_nt(same, slot.astype(BF16)).astype(jnp.int32)
    place = {
        step: (iota((rows, cap), 1) == slot[:, step : step + 1]).astype(BF16) for step in set(steps)
    }
    for at in range(0, out_ref.shape[1], tile):
        cols = slice(at, at + tile)
        share = [dot(place[step], block[:, cols]) for step, block in zip(steps, returned)]
        out_ref[:, cols] = sum(share).astype(BF16)
        copies.append(
            pltpu.make_async_copy(out_ref.at[:, cols], out_hbm.at[:, cols], sems.at[at // tile])
        )
        copies[-1].start()
    for copy in copies:
        copy.wait()


def head_shards(
    hidden,
    queries,
    memory,
    target_pair,
    source_pair,
    routes,
    route_weight,
    norm_gain,
    norm_bias,
    expert_in,
    expert_out,
):
    rows, columns = hidden.shape
    experts = lax.axis_size("expert")
    width = columns // experts
    cap = 2 * rows // experts * 5 // 4
    model = 2 * columns
    hidden_units = expert_in.shape[2]

    def along(array, step):
        if step == 0:
            return array
        return lax.ppermute(array, "expert", [(i, i ^ step) for i in range(experts)])

    def swap(array, axis):
        return lax.ppermute(array, axis, [(0, 1), (1, 0)])

    def across(array):
        pairs = [(2 * i + j, 2 * (i ^ 1) + 1 - j) for i in range(experts) for j in range(2)]
        return lax.ppermute(array, ("expert", "dp"), pairs)

    def pack(steps, *after):
        return call(
            functools.partial(pack_kernel, steps),
            [struct(4 * rows + KINDS, width)] * len(steps),
            [IN_HBM] * 7 + [IN_ANY] * len(after),
            scratch=[
                pltpu.VMEM((len(steps), rows, 2, width), BF16),
                pltpu.VMEM((1, rows), jnp.int32),
                pltpu.VMEM((1, rows), jnp.int32),
                pltpu.VMEM((2, rows), jnp.int32),
                pltpu.VMEM((2, rows), F32),
                pltpu.SemaphoreType.DMA((3, len(steps))),
                pltpu.SemaphoreType.DMA((4,)),
            ],
            moved=LATER if after else 0,
        )(
            in_hbm(queries),
            in_hbm(memory),
            in_hbm(hidden),
            in_hbm(target_pair.reshape(1, rows)),
            in_hbm(source_pair.reshape(1, rows)),
            in_hbm(routes.T),
            in_hbm(route_weight.T),
            *after,
        )

    packed = {}
    for steps in ((2,), (1,), (3, 0)):
        packed.update(zip(steps, pack(steps, *list(packed.values())[-1:])))
    messages = [along(packed[step], step) for step in ORDER]

    w_in, w_out, gain, bias = pl.pallas_call(
        functools.partial(prefetch_kernel, experts),
        out_shape=[
            pltpu.VMEM((model, hidden_units), BF16),
            pltpu.VMEM((hidden_units, model), BF16),
            pltpu.VMEM((1, model), F32),
            pltpu.VMEM((1, model), F32),
        ],
        in_specs=[IN_HBM] * 4 + [IN_ANY],
        out_specs=[IN_VMEM] * 4,
        scratch_shapes=[pltpu.SemaphoreType.DMA((2, 2 * experts))] * 2,
        compiler_params=pltpu.CompilerParams(vmem_limit_bytes=VMEM_LIMIT),
        cost_estimate=pl.CostEstimate(
            flops=0, bytes_accessed=8 * model * hidden_units, transcendentals=0
        ),
    )(
        in_hbm(expert_in[0]),
        in_hbm(expert_out[0]),
        in_hbm(norm_gain.reshape(1, model)),
        in_hbm(norm_bias.reshape(1, model)),
        packed[0],
    )

    *compact, factor = call(
        functools.partial(attend_kernel, experts, rows, cap),
        [struct(experts * cap, width)] * experts + [struct(experts * cap, HEAD, F32)],
        [IN_VMEM] * (2 + experts),
        flops=8 * experts * experts * rows * rows * width,
        moved=16 * rows * columns,
    )(in_vmem(w_in), in_vmem(w_out), *messages)

    compact = dict(zip(ORDER, compact))
    own = {step: along(compact[step], step) for step in ORDER}
    count = experts * cap

    def first(blocks, known):
        return call(
            functools.partial(first_kernel, 512),
            [struct(count, hidden_units)],
            [IN_VMEM] * (len(blocks) + 3),
            scratch=[pltpu.VMEM((count, model), BF16)],
            flops=known * 2 * count * model * hidden_units,
            moved=known * 2 * model * hidden_units,
        )(*blocks, in_vmem(gain), in_vmem(bias), in_vmem(w_in))[0]

    def pair(left, right):
        return call(pair_kernel, [struct(count, 2 * width)], [IN_VMEM] * 2)(left, right)[0]

    near = [pair(own[left], own[right]) for left, right in PAIRS]
    far1, far0 = across(compact[1]), swap(compact[0], "dp")
    held, far1, far0 = lax.optimization_barrier((own[1], far1, far0))
    far = [swap(near[0], "dp"), pair(far1, far0)]
    near_other = [swap(block, "mp") for block in (near[0], held, own[0])]
    far_other = [swap(far[1], "mp")]

    active = first([near[0], own[1], own[0]] + near_other, 0)
    kept, *sent = call(
        functools.partial(second_kernel, 512),
        [struct(count, columns)] + [struct(count // 2, columns)] * 2,
        [IN_VMEM, IN_VMEM],
    )(active, in_vmem(w_out))
    far[0], kept = lax.optimization_barrier((far[0], kept))
    far_other = [swap(far[0], "mp")] + far_other
    got = [swap(part, "mp") for part in sent]
    active = first(far + far_other, 1)
    active, *got = lax.optimization_barrier((active, *got))

    def half(active, other, parts):
        return call(
            functools.partial(half_kernel, 512, other),
            [struct(count // parts, columns)] * parts,
            [IN_VMEM, IN_VMEM],
            flops=count * model * hidden_units,
            moved=model * hidden_units,
        )(active, in_vmem(w_out))

    theirs = [swap(part, "mp") for part in half(active, True, 2)]
    mine = half(active, False, 1)[0]

    def base(start, part):
        return call(
            functools.partial(base_kernel, start),
            [struct(cap, columns, F32)] * 2 + [struct(cap, HEAD, F32)] * 2,
            [IN_VMEM] * (3 + len(PAIRS)),
            scratch=[pltpu.VMEM((2 * cap, columns), F32)],
        )(kept, part, factor, *near)

    def plain(start, part):
        return call(
            functools.partial(plain_kernel, start), [struct(cap, columns)] * 2, [IN_VMEM] * 2
        )(mine, part)

    def join(came, base, factor):
        return call(join_kernel, [struct(cap, columns)], [IN_VMEM] * 3)(came, base, factor)[0]

    base2, base3, factor2, factor3 = base(2 * cap, got[1])
    theirs[1], base2 = lax.optimization_barrier((theirs[1], base2))
    base0, base1, factor0, factor1 = base(0, got[0])
    plain2, plain3 = plain(2 * cap, theirs[1])
    plain0, plain1 = plain(0, theirs[0])
    returned = [
        along(join(swap(plain2, "dp"), base2, factor2), 2),
        along(join(swap(plain3, "dp"), base3, factor3), 3),
        along(join(swap(plain1, "dp"), base1, factor1), 1),
        join(swap(plain0, "dp"), base0, factor0),
    ]
    return pl.pallas_call(
        functools.partial(mix_kernel, experts, cap, 256, ORDER),
        out_shape=struct(rows, columns),
        in_specs=[IN_VMEM] * (1 + experts),
        out_specs=IN_HBM,
        scratch_shapes=[
            pltpu.VMEM((rows, columns), BF16),
            pltpu.SemaphoreType.DMA((columns // 256,)),
        ],
        compiler_params=pltpu.CompilerParams(vmem_limit_bytes=VMEM_LIMIT),
        cost_estimate=pl.CostEstimate(flops=1, bytes_accessed=1, transcendentals=0),
    )(routes.T, *returned)


def shards(
    hidden,
    queries,
    memory,
    target_pair,
    source_pair,
    routes,
    route_weight,
    norm_gain,
    norm_bias,
    expert_in,
    expert_out,
):
    tok_rows = hidden.shape[0]
    local_heads = queries.shape[1] // HEAD
    scale = 1.0 / math.sqrt(HEAD)
    query_heads = queries.reshape(tok_rows, local_heads, HEAD)
    running = jnp.full((local_heads, tok_rows), NEGATIVE, jnp.float32)
    rows = lax.all_gather(memory, "expert", axis=0, tiled=True)
    row_pairs = lax.all_gather(source_pair, "expert", axis=0, tiled=True)
    count = rows.shape[0]
    keys = rows[:, 0, :].reshape(count, local_heads, HEAD)
    values = rows[:, 1, :].reshape(count, local_heads, HEAD)
    score = (
        jnp.einsum("thd,rhd->htr", query_heads, keys, preferred_element_type=jnp.float32) * scale
    )
    match = (target_pair[:, None] == row_pairs[None, :])[None]
    masked = jnp.where(match, score, NEGATIVE)
    newest = jnp.maximum(running, jnp.max(masked, axis=-1))
    weight = jnp.where(match, jnp.exp(masked - newest[:, :, None]), 0.0)
    total = jnp.sum(weight, axis=-1)
    summed = jnp.einsum(
        "htr,rhd->htd", weight.astype(jnp.bfloat16), values, preferred_element_type=jnp.float32
    )
    running, total, summed = (newest, total, summed)
    context = jnp.transpose(summed / total[:, :, None], (1, 0, 2)).reshape(
        tok_rows, local_heads * HEAD
    )
    attended = (hidden.astype(jnp.float32) + context).astype(jnp.bfloat16)
    full_rows = lax.all_gather(attended, "mp", axis=1, tiled=True)
    width = full_rows.shape[1]
    experts_all = lax.axis_size("expert")
    batches = lax.axis_size("dp")
    cap = 2 * tok_rows // experts_all * 5 // 4
    flat = routes.reshape(-1)
    named = (flat[:, None] == jnp.arange(experts_all, dtype=jnp.int32)[None, :]).astype(jnp.int32)
    slot = jnp.sum((jnp.cumsum(named, axis=0) - named) * named, axis=1)
    dest = flat * cap + slot
    place = dest[:, None] == jnp.arange(experts_all * cap, dtype=jnp.int32)[None, :]
    per_token = jnp.sum(place.reshape(tok_rows, 2, experts_all * cap).astype(jnp.bfloat16), axis=1)
    outgoing = lax.dot_general(
        per_token, full_rows, (((0,), (0,)), ((), ())), preferred_element_type=jnp.float32
    ).astype(jnp.bfloat16)
    copies = jnp.broadcast_to(
        outgoing.reshape(experts_all, 1, cap, width), (experts_all, batches, cap, width)
    ).reshape(experts_all * batches * cap, width)
    arrived = lax.all_to_all(copies, ("expert", "dp"), split_axis=0, concat_axis=0, tiled=True)
    values = arrived.astype(jnp.float32)
    center = jnp.mean(values, axis=-1, keepdims=True)
    spread = jnp.mean(jnp.square(values - center), axis=-1, keepdims=True)
    normed = ((values - center) * lax.rsqrt(spread + EPSILON) * norm_gain + norm_bias).astype(
        jnp.bfloat16
    )
    active = jax.nn.relu(jnp.dot(normed, expert_in[0], preferred_element_type=jnp.float32)).astype(
        jnp.bfloat16
    )
    partial_value = jnp.dot(active, expert_out[0], preferred_element_type=jnp.float32).astype(
        jnp.bfloat16
    )
    returned = lax.all_to_all(
        partial_value, ("expert", "dp"), split_axis=0, concat_axis=0, tiled=True
    )
    expert_sum = jnp.sum(
        returned.reshape(experts_all, batches, cap, width).astype(jnp.float32), axis=1
    )
    picked = jnp.dot(
        place.astype(jnp.float32),
        expert_sum.reshape(experts_all * cap, width),
        precision=lax.Precision.HIGHEST,
    )
    blended = jnp.sum(picked.reshape(tok_rows, 2, width) * route_weight[:, :, None], axis=1)
    share = lax.psum_scatter(
        blended.astype(jnp.bfloat16), "mp", scatter_dimension=1, tiled=True
    ).astype(jnp.float32)
    return (attended.astype(jnp.float32) + share).astype(jnp.bfloat16)


def layer(hidden, queries, memory, *rest):
    experts = lax.axis_size("expert")
    rows, columns = hidden.shape
    heads = columns // HEAD
    by_heads = (
        lax.axis_size("mp") == 2
        and lax.axis_size("dp") == 2
        and heads % experts == 0
        and memory.shape[0] == rows
        and experts * rows <= columns // experts
        and experts == 4
    )
    return (head_shards if by_heads else shards)(hidden, queries, memory, *rest)


def solution(mesh):
    return jax.shard_map(
        layer,
        mesh=mesh,
        in_specs=(
            P(("groups", "expert", "dp"), "mp"),
            P(("groups", "expert", "dp"), "mp"),
            P(("groups", "expert", "dp"), None, "mp"),
            P(("groups", "expert", "dp")),
            P(("groups", "expert", "dp")),
            P(("groups", "expert", "dp"), None),
            P(("groups", "expert", "dp"), None),
            P(),
            P(),
            P("expert", None, ("dp", "mp")),
            P("expert", ("dp", "mp"), None),
        ),
        out_specs=P(("groups", "expert", "dp"), "mp"),
        check_vma=False,
    )
```

```python
import functools
import math

import jax
import jax.numpy as jnp
from jax import lax
from jax.experimental import pallas as pl
from jax.experimental.pallas import tpu as pltpu
from jax.sharding import PartitionSpec as P

HEAD = 128
EPSILON = 1e-05
NEGATIVE = -1e30
META = 16
KINDS = 8
LATER = 16 * 1024 * 1024
MIB = 1024 * 1024
ORDER = (2, 3, 1, 0)
PAIRS = ((2, 3), (1, 0))
VMEM_LIMIT = 12 * 1024 * 1024

BF16 = jnp.bfloat16
F32 = jnp.float32
IN_VMEM = pl.BlockSpec(memory_space=pltpu.VMEM)
IN_ANY = pl.BlockSpec(memory_space=pl.ANY)
IN_HBM = pl.BlockSpec(memory_space=pltpu.HBM)


def struct(rows, columns, dtype=BF16):
    return jax.ShapeDtypeStruct((rows, columns), dtype)


def call(kernel, outs, specs, scratch=(), flops=0, moved=0):
    return pl.pallas_call(
        kernel,
        out_shape=outs,
        in_specs=specs,
        out_specs=[IN_VMEM] * len(outs),
        scratch_shapes=scratch,
        compiler_params=pltpu.CompilerParams(vmem_limit_bytes=VMEM_LIMIT),
        cost_estimate=pl.CostEstimate(flops=flops, bytes_accessed=moved, transcendentals=0),
    )


def dot(a, b):
    return lax.dot_general(a, b, (((1,), (0,)), ((), ())), preferred_element_type=F32)


def dot_nt(a, b):
    return lax.dot_general(a, b, (((1,), (1,)), ((), ())), preferred_element_type=F32)


def dot_tn(a, b):
    return lax.dot_general(a, b, (((0,), (0,)), ((), ())), preferred_element_type=F32)


def iota(shape, dimension):
    return lax.broadcasted_iota(jnp.int32, shape, dimension)


def in_hbm(array):
    return pltpu.with_memory_space_constraint(array, pltpu.HBM)


def in_vmem(array):
    return pltpu.with_memory_space_constraint(array, pltpu.VMEM)


def columns_at(start, width):
    return pl.ds(pl.multiple_of(start * width, width), width)


def halves(array):
    high = array.astype(BF16).astype(F32)
    return [high, (array - high).astype(BF16).astype(F32)]


def pack_kernel(steps, q_hbm, m_hbm, h_hbm, tp_hbm, sp_hbm, r_hbm, rw_hbm, *refs):
    outs, refs = refs[-7 - len(steps) : -7], refs[-7:]
    m_ref, tp_ref, sp_ref, r_ref, rw_ref, sems, small_sems = refs
    rows, width = q_hbm.shape[0], outs[0].shape[1]
    here = lax.axis_index("expert")
    small = [
        pltpu.make_async_copy(src, dst, small_sems.at[k])
        for k, (src, dst) in enumerate(
            ((tp_hbm, tp_ref), (sp_hbm, sp_ref), (r_hbm, r_ref), (rw_hbm, rw_ref))
        )
    ]
    large = []
    for k, (step, out) in enumerate(zip(steps, outs)):
        cols = columns_at(here ^ step, width)
        large.append(
            (
                pltpu.make_async_copy(m_hbm.at[:, :, cols], m_ref.at[k], sems.at[0, k]),
                pltpu.make_async_copy(q_hbm.at[:, cols], out.at[pl.ds(0, rows)], sems.at[1, k]),
                pltpu.make_async_copy(
                    h_hbm.at[:, cols], out.at[pl.ds(3 * rows, rows)], sems.at[2, k]
                ),
            )
        )
    for copy in small:
        copy.start()
    for copies in large:
        for copy in copies:
            copy.start()
    for copy in small:
        copy.wait()
    row = iota((META, rows), 0)
    lines = [tp_ref[...], sp_ref[...], r_ref[0:1, :], r_ref[1:2, :]]
    lines = [line.astype(F32) for line in lines]
    lines += halves(rw_ref[0:1, :]) + halves(rw_ref[1:2, :])
    kinds = jnp.zeros((META, rows), F32)
    for k, line in enumerate(lines):
        kinds = jnp.where(row == k, line, kinds)
    kinds = kinds.astype(BF16)
    for step, out in zip(steps, outs):
        moved = (iota((rows, width), 1) == iota((rows, width), 0) + step * rows).astype(BF16)
        out[4 * rows :, :] = dot(kinds, moved)[0:KINDS, :].astype(BF16)
    for k, out in enumerate(outs):
        large[k][0].wait()
        out[rows : 2 * rows, :] = m_ref[k, :, 0, :]
        out[2 * rows : 3 * rows, :] = m_ref[k, :, 1, :]
    for copies in large:
        copies[1].wait()
        copies[2].wait()


def prefetch_kernel(experts, w1_hbm, w2_hbm, gain_hbm, bias_hbm, after_ref, *refs):
    w1_ref, w2_ref, gain_ref, bias_ref, sems, small_sems = refs
    here, half = lax.axis_index("expert"), lax.axis_index("mp")
    size = w1_ref.shape[0] // (2 * experts)
    copies = []
    for part in range(2 * experts):
        core = half if part < experts else 1 - half
        source = columns_at(core * experts + (here ^ ORDER[part % experts]), size)
        target = pl.ds(part * size, size)
        copies += [
            pltpu.make_async_copy(w1_hbm.at[source], w1_ref.at[target], sems.at[0, part]),
            pltpu.make_async_copy(w2_hbm.at[target], w2_ref.at[target], sems.at[1, part]),
            pltpu.make_async_copy(
                gain_hbm.at[:, source], gain_ref.at[:, target], small_sems.at[0, part]
            ),
            pltpu.make_async_copy(
                bias_hbm.at[:, source], bias_ref.at[:, target], small_sems.at[1, part]
            ),
        ]
    for copy in copies:
        copy.start()
    for copy in copies:
        copy.wait()


def attend_kernel(experts, rows, cap, w1_ref, w2_ref, *refs):
    arrived, compact = dict(zip(ORDER, refs[:experts])), refs[experts : 2 * experts]
    factor_ref, home_ref = refs[2 * experts :]
    messages = [arrived[step] for step in range(experts)]
    width = messages[0].shape[1]
    count = experts * rows
    here = lax.axis_index("expert")
    meta = sum(m[4 * rows :, :].astype(F32) for m in messages)
    same = (iota((count, count), 0) == iota((count, count), 1)).astype(BF16)
    columns = dot_nt(same, meta.astype(BF16))
    match = columns[:, 0:1] == meta[1:2, :]
    scale = 1.0 / math.sqrt(HEAD)
    parts = []
    for head in range(width // HEAD):
        lanes = slice(head * HEAD, (head + 1) * HEAD)

        def stacked(kind):
            return jnp.concatenate(
                [m[kind * rows : (kind + 1) * rows, lanes] for m in messages], axis=0
            )

        score = dot_nt(stacked(0), stacked(1)) * scale
        masked = jnp.where(match, score, NEGATIVE)
        largest = jnp.max(masked, axis=-1, keepdims=True)
        weight = jnp.where(match, jnp.exp(masked - largest), 0.0)
        total = jnp.sum(weight, axis=-1, keepdims=True)
        context = dot(weight.astype(BF16), stacked(2)) / total
        parts.append((stacked(3).astype(F32) + context).astype(BF16))
    states = jnp.concatenate(parts, axis=1)
    first, second = meta[2:3, :].astype(jnp.int32), meta[3:4, :].astype(jnp.int32)
    expert = here ^ iota((META, count), 0)
    named = ((first == expert) | (second == expert)) & (iota((META, count), 0) < experts)
    before = (iota((count, count), 0) < iota((count, count), 1)) & (
        iota((count, count), 0) // rows == iota((count, count), 1) // rows
    )
    slot = dot(named.astype(BF16), before.astype(BF16)).astype(jnp.int32)
    block = (iota((META, count), 1) // rows) ^ iota((META, count), 0)
    spot = jnp.where(named, block * cap + slot, -1)
    home = jnp.where(named, slot, -1)[:, 0:rows].astype(F32).astype(BF16)
    home = dot_nt(same[0:rows, 0:rows], home).astype(jnp.int32)
    for step in range(experts):
        place = iota((rows, home_ref.shape[1]), 1) == home[:, step : step + 1]
        home_ref[step * rows : (step + 1) * rows, :] = place.astype(BF16)
    for step, out in zip(ORDER, compact):
        place = iota((experts * cap, count), 0) == spot[step : step + 1, :]
        place = place.astype(BF16)
        out[...] = dot(place, states).astype(BF16)
    leads = first == here
    lines = jnp.where(iota((META, count), 0) == 3, leads.astype(F32), 0.0)
    for k in range(2):
        half = jnp.where(leads, meta[4 + k : 5 + k, :], meta[6 + k : 7 + k, :])
        lines = jnp.where(iota((META, count), 0) == k, half, lines)
    factor_ref[...] = jnp.zeros(factor_ref.shape, F32)
    factor_ref[:, 0:META] = dot_nt(place, lines.astype(BF16))


def pair_kernel(left_ref, right_ref, out_ref):
    width = left_ref.shape[1]
    out_ref[:, 0:width] = left_ref[...]
    out_ref[:, width:] = right_ref[...]


def first_kernel(tile, *refs):
    blocks, (gain_ref, bias_ref, w_ref, out_ref, n_ref) = refs[:-5], refs[-5:]
    width, model = min(block.shape[1] for block in blocks), n_ref.shape[1]
    pieces = [
        (block, slice(at, at + width)) for block in blocks for at in range(0, block.shape[1], width)
    ]
    for at in range(0, n_ref.shape[0], META):
        rows = slice(at, at + META)
        values = [block[rows, cols].astype(F32) for block, cols in pieces]
        center = jnp.sum(sum(values), axis=-1, keepdims=True) * (1.0 / model)
        shifted = [value - center for value in values]
        spread = sum(value * value for value in shifted)
        spread = jnp.sum(spread, axis=-1, keepdims=True) * (1.0 / model)
        scale = lax.rsqrt(spread + EPSILON)
        for k, value in enumerate(shifted):
            cols = slice(k * width, (k + 1) * width)
            normed = value * scale * gain_ref[:, cols] + bias_ref[:, cols]
            n_ref[rows, cols] = normed.astype(BF16)
    for at in range(0, w_ref.shape[1], tile):
        cols = slice(at, at + tile)
        out_ref[:, cols] = jnp.maximum(dot(n_ref[...], w_ref[:, cols]), 0.0).astype(BF16)


def second_kernel(tile, a_ref, w_ref, kept_ref, *sent):
    columns, rows = kept_ref.shape[1], sent[0].shape[0]
    lower = lax.axis_index("mp") == 0
    for at in range(0, columns, tile):
        low = dot(a_ref[...], w_ref[:, at : at + tile])
        high = dot(a_ref[...], w_ref[:, columns + at : columns + at + tile])
        kept_ref[:, at : at + tile] = jnp.where(lower, low, high).astype(BF16)
        other = jnp.where(lower, high, low).astype(BF16)
        for k, out_ref in enumerate(sent):
            out_ref[:, at : at + tile] = other[k * rows : (k + 1) * rows, :]


def half_kernel(tile, other, a_ref, w_ref, *outs):
    columns, rows = outs[0].shape[1], outs[0].shape[0]
    half = lax.axis_index("mp")
    half = 1 - half if other else half
    for at in range(columns // tile):
        part = dot(a_ref[...], w_ref[:, columns_at(half * (columns // tile) + at, tile)])
        for k, out_ref in enumerate(outs):
            out_ref[:, at * tile : (at + 1) * tile] = part[k * rows : (k + 1) * rows, :].astype(BF16)


def plain_kernel(start, kept_ref, got_ref, *outs):
    cap = outs[0].shape[0]
    for k, out_ref in enumerate(outs):
        rows, half = slice(start + k * cap, start + (k + 1) * cap), slice(k * cap, (k + 1) * cap)
        total = kept_ref[rows, :].astype(F32) + got_ref[half, :].astype(F32)
        out_ref[...] = total.astype(BF16)


def base_kernel(start, kept_ref, got_ref, factor_ref, *refs):
    blocks, bases, factors, states = refs[: len(PAIRS)], refs[-5:-3], refs[-3:-1], refs[-1]
    here = lax.axis_index("expert")
    cap, width = bases[0].shape[0], blocks[0].shape[1] // 2
    for steps, block in zip(PAIRS, blocks):
        for k, step in enumerate(steps):
            piece = block[start : start + 2 * cap, k * width : (k + 1) * width]
            states[:, columns_at(here ^ step, width)] = piece.astype(F32)
    for k in range(2):
        rows, half = slice(start + k * cap, start + (k + 1) * cap), slice(k * cap, (k + 1) * cap)
        weight = factor_ref[rows, 0:1] + factor_ref[rows, 1:2]
        total = kept_ref[rows, :].astype(F32) + got_ref[half, :].astype(F32)
        bases[k][...] = total * weight + factor_ref[rows, 3:4] * states[half, :]
        factors[k][...] = jnp.broadcast_to(weight, factors[k].shape)


def join_kernel(came_ref, base_ref, factor_ref, out_ref):
    total = base_ref[...] + factor_ref[:, 0:1] * came_ref[...].astype(F32)
    out_ref[...] = total.astype(BF16)


def mix_kernel(tile, steps, place_ref, *refs):
    returned, (out_hbm, out_ref, sems) = refs[:-3], refs[-3:]
    rows, cap = out_ref.shape[0], returned[0].shape[0]
    copies = []
    for at in range(0, out_ref.shape[1], tile):
        cols = slice(at, at + tile)
        share = [
            dot(place_ref[step * rows : (step + 1) * rows, 0:cap], block[:, cols])
            for step, block in zip(steps, returned)
        ]
        out_ref[:, cols] = sum(share).astype(BF16)
        copies.append(
            pltpu.make_async_copy(out_ref.at[:, cols], out_hbm.at[:, cols], sems.at[at // tile])
        )
        copies[-1].start()
    for copy in copies:
        copy.wait()


def head_shards(
    hidden,
    queries,
    memory,
    target_pair,
    source_pair,
    routes,
    route_weight,
    norm_gain,
    norm_bias,
    expert_in,
    expert_out,
):
    rows, columns = hidden.shape
    experts = lax.axis_size("expert")
    width = columns // experts
    cap = 2 * rows // experts * 5 // 4
    model = 2 * columns
    hidden_units = expert_in.shape[2]

    def along(array, step):
        if step == 0:
            return array
        return lax.ppermute(array, "expert", [(i, i ^ step) for i in range(experts)])

    def swap(array, axis):
        return lax.ppermute(array, axis, [(0, 1), (1, 0)])

    def across(array):
        pairs = [(2 * i + j, 2 * (i ^ 1) + 1 - j) for i in range(experts) for j in range(2)]
        return lax.ppermute(array, ("expert", "dp"), pairs)

    def pack(steps, *after):
        return call(
            functools.partial(pack_kernel, steps),
            [struct(4 * rows + KINDS, width)] * len(steps),
            [IN_HBM] * 7 + [IN_ANY] * len(after),
            scratch=[
                pltpu.VMEM((len(steps), rows, 2, width), BF16),
                pltpu.VMEM((1, rows), jnp.int32),
                pltpu.VMEM((1, rows), jnp.int32),
                pltpu.VMEM((2, rows), jnp.int32),
                pltpu.VMEM((2, rows), F32),
                pltpu.SemaphoreType.DMA((3, len(steps))),
                pltpu.SemaphoreType.DMA((4,)),
            ],
            moved=LATER if after else 0,
        )(
            in_hbm(queries),
            in_hbm(memory),
            in_hbm(hidden),
            in_hbm(target_pair.reshape(1, rows)),
            in_hbm(source_pair.reshape(1, rows)),
            in_hbm(routes.T),
            in_hbm(route_weight.T),
            *after,
        )

    packed = {}
    for steps in ((2,), (1,), (3, 0)):
        packed.update(zip(steps, pack(steps, *list(packed.values())[-1:])))
    messages = [along(packed[step], step) for step in ORDER]

    w_in, w_out, gain, bias = pl.pallas_call(
        functools.partial(prefetch_kernel, experts),
        out_shape=[
            pltpu.VMEM((model, hidden_units), BF16),
            pltpu.VMEM((hidden_units, model), BF16),
            pltpu.VMEM((1, model), F32),
            pltpu.VMEM((1, model), F32),
        ],
        in_specs=[IN_HBM] * 4 + [IN_ANY],
        out_specs=[IN_VMEM] * 4,
        scratch_shapes=[pltpu.SemaphoreType.DMA((2, 2 * experts))] * 2,
        compiler_params=pltpu.CompilerParams(vmem_limit_bytes=VMEM_LIMIT),
        cost_estimate=pl.CostEstimate(
            flops=0, bytes_accessed=8 * model * hidden_units, transcendentals=0
        ),
    )(
        in_hbm(expert_in[0]),
        in_hbm(expert_out[0]),
        in_hbm(norm_gain.reshape(1, model)),
        in_hbm(norm_bias.reshape(1, model)),
        packed[0],
    )

    *compact, factor, home = call(
        functools.partial(attend_kernel, experts, rows, cap),
        [struct(experts * cap, width)] * experts
        + [struct(experts * cap, HEAD, F32), struct(experts * rows, HEAD)],
        [IN_VMEM] * (2 + experts),
        flops=8 * experts * experts * rows * rows * width,
        moved=16 * rows * columns,
    )(in_vmem(w_in), in_vmem(w_out), *messages)

    compact = dict(zip(ORDER, compact))
    own = {step: along(compact[step], step) for step in ORDER}
    count = experts * cap

    def first(blocks, known):
        return call(
            functools.partial(first_kernel, 512),
            [struct(count, hidden_units)],
            [IN_VMEM] * (len(blocks) + 3),
            scratch=[pltpu.VMEM((count, model), BF16)],
            flops=known * 2 * count * model * hidden_units,
            moved=known * 2 * model * hidden_units,
        )(*blocks, in_vmem(gain), in_vmem(bias), in_vmem(w_in))[0]

    def pair(left, right):
        return call(pair_kernel, [struct(count, 2 * width)], [IN_VMEM] * 2)(left, right)[0]

    near = [pair(own[left], own[right]) for left, right in PAIRS]
    far1, far0 = across(compact[1]), swap(compact[0], "dp")
    held, far1, far0 = lax.optimization_barrier((own[1], far1, far0))
    far = [swap(near[0], "dp"), pair(far1, far0)]
    near_other = [swap(block, "mp") for block in (near[0], held, own[0])]
    far_other = [swap(far[1], "mp")]

    active = first([near[0], own[1], own[0]] + near_other, 0)
    kept, *sent = call(
        functools.partial(second_kernel, 512),
        [struct(count, columns)] + [struct(count // 2, columns)] * 2,
        [IN_VMEM, IN_VMEM],
    )(active, in_vmem(w_out))
    far[0], kept = lax.optimization_barrier((far[0], kept))
    far_other = [swap(far[0], "mp")] + far_other
    got = [swap(part, "mp") for part in sent]
    active = first(far + far_other, 1)
    active, *got = lax.optimization_barrier((active, *got))

    def half(active, other, parts):
        return call(
            functools.partial(half_kernel, 512, other),
            [struct(count // parts, columns)] * parts,
            [IN_VMEM, IN_VMEM],
            flops=count * model * hidden_units,
            moved=model * hidden_units,
        )(active, in_vmem(w_out))

    theirs = [swap(part, "mp") for part in half(active, True, 2)]
    mine = half(active, False, 1)[0]

    def base(start, part):
        return call(
            functools.partial(base_kernel, start),
            [struct(cap, columns, F32)] * 2 + [struct(cap, HEAD, F32)] * 2,
            [IN_VMEM] * (3 + len(PAIRS)),
            scratch=[pltpu.VMEM((2 * cap, columns), F32)],
        )(kept, part, factor, *near)

    def plain(start, part):
        return call(
            functools.partial(plain_kernel, start), [struct(cap, columns)] * 2, [IN_VMEM] * 2
        )(mine, part)

    def join(came, base, factor):
        return call(join_kernel, [struct(cap, columns)], [IN_VMEM] * 3)(came, base, factor)[0]

    base2, base3, factor2, factor3 = base(2 * cap, got[1])
    theirs[1], base2 = lax.optimization_barrier((theirs[1], base2))
    base0, base1, factor0, factor1 = base(0, got[0])
    plain2, plain3 = plain(2 * cap, theirs[1])
    plain0, plain1 = plain(0, theirs[0])
    returned = [
        along(join(swap(plain2, "dp"), base2, factor2), 2),
        along(join(swap(plain3, "dp"), base3, factor3), 3),
        along(join(swap(plain1, "dp"), base1, factor1), 1),
        join(swap(plain0, "dp"), base0, factor0),
    ]
    return pl.pallas_call(
        functools.partial(mix_kernel, 256, ORDER),
        out_shape=struct(rows, columns),
        in_specs=[IN_VMEM] * (1 + experts),
        out_specs=IN_HBM,
        scratch_shapes=[
            pltpu.VMEM((rows, columns), BF16),
            pltpu.SemaphoreType.DMA((columns // 256,)),
        ],
        compiler_params=pltpu.CompilerParams(vmem_limit_bytes=VMEM_LIMIT),
        cost_estimate=pl.CostEstimate(flops=1, bytes_accessed=1, transcendentals=0),
    )(home, *returned)


def shards(
    hidden,
    queries,
    memory,
    target_pair,
    source_pair,
    routes,
    route_weight,
    norm_gain,
    norm_bias,
    expert_in,
    expert_out,
):
    tok_rows = hidden.shape[0]
    local_heads = queries.shape[1] // HEAD
    scale = 1.0 / math.sqrt(HEAD)
    query_heads = queries.reshape(tok_rows, local_heads, HEAD)
    running = jnp.full((local_heads, tok_rows), NEGATIVE, jnp.float32)
    rows = lax.all_gather(memory, "expert", axis=0, tiled=True)
    row_pairs = lax.all_gather(source_pair, "expert", axis=0, tiled=True)
    count = rows.shape[0]
    keys = rows[:, 0, :].reshape(count, local_heads, HEAD)
    values = rows[:, 1, :].reshape(count, local_heads, HEAD)
    score = (
        jnp.einsum("thd,rhd->htr", query_heads, keys, preferred_element_type=jnp.float32) * scale
    )
    match = (target_pair[:, None] == row_pairs[None, :])[None]
    masked = jnp.where(match, score, NEGATIVE)
    newest = jnp.maximum(running, jnp.max(masked, axis=-1))
    weight = jnp.where(match, jnp.exp(masked - newest[:, :, None]), 0.0)
    total = jnp.sum(weight, axis=-1)
    summed = jnp.einsum(
        "htr,rhd->htd", weight.astype(jnp.bfloat16), values, preferred_element_type=jnp.float32
    )
    running, total, summed = (newest, total, summed)
    context = jnp.transpose(summed / total[:, :, None], (1, 0, 2)).reshape(
        tok_rows, local_heads * HEAD
    )
    attended = (hidden.astype(jnp.float32) + context).astype(jnp.bfloat16)
    full_rows = lax.all_gather(attended, "mp", axis=1, tiled=True)
    width = full_rows.shape[1]
    experts_all = lax.axis_size("expert")
    batches = lax.axis_size("dp")
    cap = 2 * tok_rows // experts_all * 5 // 4
    flat = routes.reshape(-1)
    named = (flat[:, None] == jnp.arange(experts_all, dtype=jnp.int32)[None, :]).astype(jnp.int32)
    slot = jnp.sum((jnp.cumsum(named, axis=0) - named) * named, axis=1)
    dest = flat * cap + slot
    place = dest[:, None] == jnp.arange(experts_all * cap, dtype=jnp.int32)[None, :]
    per_token = jnp.sum(place.reshape(tok_rows, 2, experts_all * cap).astype(jnp.bfloat16), axis=1)
    outgoing = lax.dot_general(
        per_token, full_rows, (((0,), (0,)), ((), ())), preferred_element_type=jnp.float32
    ).astype(jnp.bfloat16)
    copies = jnp.broadcast_to(
        outgoing.reshape(experts_all, 1, cap, width), (experts_all, batches, cap, width)
    ).reshape(experts_all * batches * cap, width)
    arrived = lax.all_to_all(copies, ("expert", "dp"), split_axis=0, concat_axis=0, tiled=True)
    values = arrived.astype(jnp.float32)
    center = jnp.mean(values, axis=-1, keepdims=True)
    spread = jnp.mean(jnp.square(values - center), axis=-1, keepdims=True)
    normed = ((values - center) * lax.rsqrt(spread + EPSILON) * norm_gain + norm_bias).astype(
        jnp.bfloat16
    )
    active = jax.nn.relu(jnp.dot(normed, expert_in[0], preferred_element_type=jnp.float32)).astype(
        jnp.bfloat16
    )
    partial_value = jnp.dot(active, expert_out[0], preferred_element_type=jnp.float32).astype(
        jnp.bfloat16
    )
    returned = lax.all_to_all(
        partial_value, ("expert", "dp"), split_axis=0, concat_axis=0, tiled=True
    )
    expert_sum = jnp.sum(
        returned.reshape(experts_all, batches, cap, width).astype(jnp.float32), axis=1
    )
    picked = jnp.dot(
        place.astype(jnp.float32),
        expert_sum.reshape(experts_all * cap, width),
        precision=lax.Precision.HIGHEST,
    )
    blended = jnp.sum(picked.reshape(tok_rows, 2, width) * route_weight[:, :, None], axis=1)
    share = lax.psum_scatter(
        blended.astype(jnp.bfloat16), "mp", scatter_dimension=1, tiled=True
    ).astype(jnp.float32)
    return (attended.astype(jnp.float32) + share).astype(jnp.bfloat16)


def layer(hidden, queries, memory, *rest):
    experts = lax.axis_size("expert")
    rows, columns = hidden.shape
    heads = columns // HEAD
    by_heads = (
        lax.axis_size("mp") == 2
        and lax.axis_size("dp") == 2
        and heads % experts == 0
        and memory.shape[0] == rows
        and experts * rows <= columns // experts
        and experts == 4
    )
    return (head_shards if by_heads else shards)(hidden, queries, memory, *rest)


def solution(mesh):
    return jax.shard_map(
        layer,
        mesh=mesh,
        in_specs=(
            P(("groups", "expert", "dp"), "mp"),
            P(("groups", "expert", "dp"), "mp"),
            P(("groups", "expert", "dp"), None, "mp"),
            P(("groups", "expert", "dp")),
            P(("groups", "expert", "dp")),
            P(("groups", "expert", "dp"), None),
            P(("groups", "expert", "dp"), None),
            P(),
            P(),
            P("expert", None, ("dp", "mp")),
            P("expert", ("dp", "mp"), None),
        ),
        out_specs=P(("groups", "expert", "dp"), "mp"),
        check_vma=False,
    )
```

```python
import functools
import math

import jax
import jax.numpy as jnp
from jax import lax
from jax.experimental import pallas as pl
from jax.experimental.pallas import tpu as pltpu
from jax.sharding import PartitionSpec as P

HEAD = 128
EPSILON = 1e-05
NEGATIVE = -1e30
META = 16
KINDS = 8
LATER = 16 * 1024 * 1024
MIB = 1024 * 1024
ORDER = (2, 3, 1, 0)
PAIRS = ((2, 3), (1, 0))
VMEM_LIMIT = 12 * 1024 * 1024

BF16 = jnp.bfloat16
F32 = jnp.float32
IN_VMEM = pl.BlockSpec(memory_space=pltpu.VMEM)
IN_ANY = pl.BlockSpec(memory_space=pl.ANY)
IN_HBM = pl.BlockSpec(memory_space=pltpu.HBM)


def struct(rows, columns, dtype=BF16):
    return jax.ShapeDtypeStruct((rows, columns), dtype)


def call(kernel, outs, specs, scratch=(), flops=0, moved=0):
    return pl.pallas_call(
        kernel,
        out_shape=outs,
        in_specs=specs,
        out_specs=[IN_VMEM] * len(outs),
        scratch_shapes=scratch,
        compiler_params=pltpu.CompilerParams(vmem_limit_bytes=VMEM_LIMIT),
        cost_estimate=pl.CostEstimate(flops=flops, bytes_accessed=moved, transcendentals=0),
    )


def dot(a, b):
    return lax.dot_general(a, b, (((1,), (0,)), ((), ())), preferred_element_type=F32)


def dot_nt(a, b):
    return lax.dot_general(a, b, (((1,), (1,)), ((), ())), preferred_element_type=F32)


def dot_tn(a, b):
    return lax.dot_general(a, b, (((0,), (0,)), ((), ())), preferred_element_type=F32)


def iota(shape, dimension):
    return lax.broadcasted_iota(jnp.int32, shape, dimension)


def in_hbm(array):
    return pltpu.with_memory_space_constraint(array, pltpu.HBM)


def in_vmem(array):
    return pltpu.with_memory_space_constraint(array, pltpu.VMEM)


def columns_at(start, width):
    return pl.ds(pl.multiple_of(start * width, width), width)


def halves(array):
    high = array.astype(BF16).astype(F32)
    return [high, (array - high).astype(BF16).astype(F32)]


def pack_kernel(steps, q_hbm, m_hbm, h_hbm, tp_hbm, sp_hbm, r_hbm, rw_hbm, *refs):
    outs, refs = refs[-7 - len(steps) : -7], refs[-7:]
    m_ref, tp_ref, sp_ref, r_ref, rw_ref, sems, small_sems = refs
    rows, width = q_hbm.shape[0], outs[0].shape[1]
    here = lax.axis_index("expert")
    small = [
        pltpu.make_async_copy(src, dst, small_sems.at[k])
        for k, (src, dst) in enumerate(
            ((tp_hbm, tp_ref), (sp_hbm, sp_ref), (r_hbm, r_ref), (rw_hbm, rw_ref))
        )
    ]
    large = []
    for k, (step, out) in enumerate(zip(steps, outs)):
        cols = columns_at(here ^ step, width)
        large.append(
            (
                pltpu.make_async_copy(m_hbm.at[:, :, cols], m_ref.at[k], sems.at[0, k]),
                pltpu.make_async_copy(q_hbm.at[:, cols], out.at[pl.ds(0, rows)], sems.at[1, k]),
                pltpu.make_async_copy(
                    h_hbm.at[:, cols], out.at[pl.ds(3 * rows, rows)], sems.at[2, k]
                ),
            )
        )
    for copy in small:
        copy.start()
    for copies in large:
        for copy in copies:
            copy.start()
    for copy in small:
        copy.wait()
    row = iota((META, rows), 0)
    lines = [tp_ref[...], sp_ref[...], r_ref[0:1, :], r_ref[1:2, :]]
    lines = [line.astype(F32) for line in lines]
    lines += halves(rw_ref[0:1, :]) + halves(rw_ref[1:2, :])
    kinds = jnp.zeros((META, rows), F32)
    for k, line in enumerate(lines):
        kinds = jnp.where(row == k, line, kinds)
    kinds = kinds.astype(BF16)
    for step, out in zip(steps, outs):
        moved = (iota((rows, width), 1) == iota((rows, width), 0) + step * rows).astype(BF16)
        out[4 * rows :, :] = dot(kinds, moved)[0:KINDS, :].astype(BF16)
    for k, out in enumerate(outs):
        large[k][0].wait()
        out[rows : 2 * rows, :] = m_ref[k, :, 0, :]
        out[2 * rows : 3 * rows, :] = m_ref[k, :, 1, :]
    for copies in large:
        copies[1].wait()
        copies[2].wait()


def prefetch_kernel(experts, w1_hbm, w2_hbm, gain_hbm, bias_hbm, after_ref, *refs):
    w1_ref, w2_ref, gain_ref, bias_ref, sems, small_sems = refs
    here, half = lax.axis_index("expert"), lax.axis_index("mp")
    size = w1_ref.shape[0] // (2 * experts)
    copies = []
    for part in range(2 * experts):
        core = half if part < experts else 1 - half
        source = columns_at(core * experts + (here ^ ORDER[part % experts]), size)
        target = pl.ds(part * size, size)
        copies += [
            pltpu.make_async_copy(w1_hbm.at[source], w1_ref.at[target], sems.at[0, part]),
            pltpu.make_async_copy(w2_hbm.at[target], w2_ref.at[target], sems.at[1, part]),
            pltpu.make_async_copy(
                gain_hbm.at[:, source], gain_ref.at[:, target], small_sems.at[0, part]
            ),
            pltpu.make_async_copy(
                bias_hbm.at[:, source], bias_ref.at[:, target], small_sems.at[1, part]
            ),
        ]
    for copy in copies:
        copy.start()
    for copy in copies:
        copy.wait()


def attend_kernel(experts, rows, cap, w1_ref, w2_ref, *refs):
    arrived, compact = dict(zip(ORDER, refs[:experts])), refs[experts : 2 * experts]
    factor_ref, home_ref = refs[2 * experts :]
    messages = [arrived[step] for step in range(experts)]
    width = messages[0].shape[1]
    count = experts * rows
    here = lax.axis_index("expert")
    meta = sum(m[4 * rows :, :].astype(F32) for m in messages)
    same = (iota((count, count), 0) == iota((count, count), 1)).astype(BF16)
    columns = dot_nt(same, meta.astype(BF16))
    match = columns[:, 0:1] == meta[1:2, :]
    scale = 1.0 / math.sqrt(HEAD)
    parts = []
    for head in range(width // HEAD):
        lanes = slice(head * HEAD, (head + 1) * HEAD)

        def stacked(kind):
            return jnp.concatenate(
                [m[kind * rows : (kind + 1) * rows, lanes] for m in messages], axis=0
            )

        score = dot_nt(stacked(0), stacked(1)) * scale
        masked = jnp.where(match, score, NEGATIVE)
        largest = jnp.max(masked, axis=-1, keepdims=True)
        weight = jnp.where(match, jnp.exp(masked - largest), 0.0)
        total = jnp.sum(weight, axis=-1, keepdims=True)
        context = dot(weight.astype(BF16), stacked(2)) / total
        parts.append((stacked(3).astype(F32) + context).astype(BF16))
    states = jnp.concatenate(parts, axis=1)
    first, second = meta[2:3, :].astype(jnp.int32), meta[3:4, :].astype(jnp.int32)
    expert = here ^ iota((META, count), 0)
    named = ((first == expert) | (second == expert)) & (iota((META, count), 0) < experts)
    before = (iota((count, count), 0) < iota((count, count), 1)) & (
        iota((count, count), 0) // rows == iota((count, count), 1) // rows
    )
    slot = dot(named.astype(BF16), before.astype(BF16)).astype(jnp.int32)
    block = (iota((META, count), 1) // rows) ^ iota((META, count), 0)
    spot = jnp.where(named, block * cap + slot, -1)
    home = jnp.where(named, slot, -1)[:, 0:rows].astype(F32).astype(BF16)
    home = dot_nt(same[0:rows, 0:rows], home).astype(jnp.int32)
    for step in range(experts):
        place = iota((rows, home_ref.shape[1]), 1) == home[:, step : step + 1]
        home_ref[step * rows : (step + 1) * rows, :] = place.astype(BF16)
    kinds = dot_nt(same[0:rows, 0:rows], meta[:, 0:rows].astype(BF16))
    leads = kinds[:, 2:3].astype(jnp.int32) == (here ^ 1)
    place = iota((rows, home_ref.shape[1]), 1) == home[:, 1:2]
    for k in range(2):
        half = jnp.where(leads, kinds[:, 4 + k : 5 + k], kinds[:, 6 + k : 7 + k])
        at = (experts + k) * rows
        home_ref[at : at + rows, :] = jnp.where(place, half, 0.0).astype(BF16)
    for step, out in zip(ORDER, compact):
        place = iota((experts * cap, count), 0) == spot[step : step + 1, :]
        place = place.astype(BF16)
        out[...] = dot(place, states).astype(BF16)
    leads = first == here
    lines = jnp.where(iota((META, count), 0) == 3, leads.astype(F32), 0.0)
    for k in range(2):
        half = jnp.where(leads, meta[4 + k : 5 + k, :], meta[6 + k : 7 + k, :])
        lines = jnp.where(iota((META, count), 0) == k, half, lines)
    factor_ref[...] = jnp.zeros(factor_ref.shape, F32)
    factor_ref[:, 0:META] = dot_nt(place, lines.astype(BF16))


def pair_kernel(left_ref, right_ref, out_ref):
    width = left_ref.shape[1]
    out_ref[:, 0:width] = left_ref[...]
    out_ref[:, width:] = right_ref[...]


def first_kernel(tile, *refs):
    blocks, (gain_ref, bias_ref, w_ref, out_ref, n_ref) = refs[:-5], refs[-5:]
    width, model = min(block.shape[1] for block in blocks), n_ref.shape[1]
    pieces = [
        (block, slice(at, at + width)) for block in blocks for at in range(0, block.shape[1], width)
    ]
    for at in range(0, n_ref.shape[0], META):
        rows = slice(at, at + META)
        values = [block[rows, cols].astype(F32) for block, cols in pieces]
        center = jnp.sum(sum(values), axis=-1, keepdims=True) * (1.0 / model)
        shifted = [value - center for value in values]
        spread = sum(value * value for value in shifted)
        spread = jnp.sum(spread, axis=-1, keepdims=True) * (1.0 / model)
        scale = lax.rsqrt(spread + EPSILON)
        for k, value in enumerate(shifted):
            cols = slice(k * width, (k + 1) * width)
            normed = value * scale * gain_ref[:, cols] + bias_ref[:, cols]
            n_ref[rows, cols] = normed.astype(BF16)
    for at in range(0, w_ref.shape[1], tile):
        cols = slice(at, at + tile)
        out_ref[:, cols] = jnp.maximum(dot(n_ref[...], w_ref[:, cols]), 0.0).astype(BF16)


def second_kernel(tile, a_ref, w_ref, kept_ref, *sent):
    columns, rows = kept_ref.shape[1], sent[0].shape[0]
    lower = lax.axis_index("mp") == 0
    for at in range(0, columns, tile):
        low = dot(a_ref[...], w_ref[:, at : at + tile])
        high = dot(a_ref[...], w_ref[:, columns + at : columns + at + tile])
        kept_ref[:, at : at + tile] = jnp.where(lower, low, high).astype(BF16)
        other = jnp.where(lower, high, low).astype(BF16)
        for k, out_ref in enumerate(sent):
            out_ref[:, at : at + tile] = other[k * rows : (k + 1) * rows, :]


def half_kernel(tile, other, a_ref, w_ref, *outs):
    columns, rows = outs[0].shape[1], outs[0].shape[0]
    half = lax.axis_index("mp")
    half = 1 - half if other else half
    for at in range(columns // tile):
        part = dot(a_ref[...], w_ref[:, columns_at(half * (columns // tile) + at, tile)])
        for k, out_ref in enumerate(outs):
            out_ref[:, at * tile : (at + 1) * tile] = part[k * rows : (k + 1) * rows, :].astype(BF16)


def plain_kernel(start, kept_ref, got_ref, *outs):
    cap = outs[0].shape[0]
    for k, out_ref in enumerate(outs):
        rows, half = slice(start + k * cap, start + (k + 1) * cap), slice(k * cap, (k + 1) * cap)
        total = kept_ref[rows, :].astype(F32) + got_ref[half, :].astype(F32)
        out_ref[...] = total.astype(BF16)


def base_kernel(start, kept_ref, got_ref, factor_ref, *refs):
    blocks, bases, factors, states = refs[: len(PAIRS)], refs[-5:-3], refs[-3:-1], refs[-1]
    here = lax.axis_index("expert")
    cap, width = bases[0].shape[0], blocks[0].shape[1] // 2
    for steps, block in zip(PAIRS, blocks):
        for k, step in enumerate(steps):
            piece = block[start : start + 2 * cap, k * width : (k + 1) * width]
            states[:, columns_at(here ^ step, width)] = piece.astype(F32)
    for k in range(2):
        rows, half = slice(start + k * cap, start + (k + 1) * cap), slice(k * cap, (k + 1) * cap)
        weight = factor_ref[rows, 0:1] + factor_ref[rows, 1:2]
        total = kept_ref[rows, :].astype(F32) + got_ref[half, :].astype(F32)
        bases[k][...] = total * weight + factor_ref[rows, 3:4] * states[half, :]
        factors[k][...] = jnp.broadcast_to(weight, factors[k].shape)


def low_kernel(kept_ref, got_ref, factor_ref, *refs):
    blocks, (base_ref, near_ref, weight_ref, states) = refs[: len(PAIRS)], refs[-4:]
    here = lax.axis_index("expert")
    cap, width = base_ref.shape[0], blocks[0].shape[1] // 2
    for steps, block in zip(PAIRS, blocks):
        for k, step in enumerate(steps):
            piece = block[0 : 2 * cap, k * width : (k + 1) * width]
            states[:, columns_at(here ^ step, width)] = piece.astype(F32)
    weight = factor_ref[0 : 2 * cap, 0:1] + factor_ref[0 : 2 * cap, 1:2]
    total = kept_ref[0 : 2 * cap, :].astype(F32) + got_ref[...].astype(F32)
    total = total * weight + factor_ref[0 : 2 * cap, 3:4] * states[...]
    base_ref[...] = total[0:cap, :]
    near_ref[...] = total[cap:, :].astype(BF16)
    weight_ref[...] = jnp.broadcast_to(weight[0:cap, :], weight_ref.shape)


def join_kernel(came_ref, base_ref, factor_ref, out_ref):
    total = base_ref[...] + factor_ref[:, 0:1] * came_ref[...].astype(F32)
    out_ref[...] = total.astype(BF16)


def sum_kernel(tile, steps, place_ref, *refs):
    returned, far_ref, out_ref = refs[:-2], refs[-2], refs[-1]
    rows, cap = out_ref.shape[0], far_ref.shape[0]
    last = place_ref.shape[0] // rows
    terms = [*zip(steps, returned), (last - 2, far_ref), (last - 1, far_ref)]
    for at in range(0, out_ref.shape[1], tile):
        cols = slice(at, at + tile)
        share = [
            dot(place_ref[step * rows : (step + 1) * rows, 0:cap], block[:, cols])
            for step, block in terms
        ]
        out_ref[:, cols] = sum(share)


def mix_kernel(tile, place_ref, share_ref, came_ref, base_ref, factor_ref, out_hbm, out_ref, sems):
    rows, cap = out_ref.shape[0], came_ref.shape[0]
    copies = []
    for at in range(0, out_ref.shape[1], tile):
        cols = slice(at, at + tile)
        own = base_ref[:, cols] + factor_ref[:, 0:1] * came_ref[:, cols].astype(F32)
        own = dot(place_ref[0:rows, 0:cap], own.astype(BF16))
        out_ref[:, cols] = (share_ref[:, cols] + own).astype(BF16)
        copies.append(
            pltpu.make_async_copy(out_ref.at[:, cols], out_hbm.at[:, cols], sems.at[at // tile])
        )
        copies[-1].start()
    for copy in copies:
        copy.wait()


def head_shards(
    hidden,
    queries,
    memory,
    target_pair,
    source_pair,
    routes,
    route_weight,
    norm_gain,
    norm_bias,
    expert_in,
    expert_out,
):
    rows, columns = hidden.shape
    experts = lax.axis_size("expert")
    width = columns // experts
    cap = 2 * rows // experts * 5 // 4
    model = 2 * columns
    hidden_units = expert_in.shape[2]

    def along(array, step):
        if step == 0:
            return array
        return lax.ppermute(array, "expert", [(i, i ^ step) for i in range(experts)])

    def swap(array, axis):
        return lax.ppermute(array, axis, [(0, 1), (1, 0)])

    def across(array):
        pairs = [(2 * i + j, 2 * (i ^ 1) + 1 - j) for i in range(experts) for j in range(2)]
        return lax.ppermute(array, ("expert", "dp"), pairs)

    def pack(steps, *after):
        return call(
            functools.partial(pack_kernel, steps),
            [struct(4 * rows + KINDS, width)] * len(steps),
            [IN_HBM] * 7 + [IN_ANY] * len(after),
            scratch=[
                pltpu.VMEM((len(steps), rows, 2, width), BF16),
                pltpu.VMEM((1, rows), jnp.int32),
                pltpu.VMEM((1, rows), jnp.int32),
                pltpu.VMEM((2, rows), jnp.int32),
                pltpu.VMEM((2, rows), F32),
                pltpu.SemaphoreType.DMA((3, len(steps))),
                pltpu.SemaphoreType.DMA((4,)),
            ],
            moved=LATER if after else 0,
        )(
            in_hbm(queries),
            in_hbm(memory),
            in_hbm(hidden),
            in_hbm(target_pair.reshape(1, rows)),
            in_hbm(source_pair.reshape(1, rows)),
            in_hbm(routes.T),
            in_hbm(route_weight.T),
            *after,
        )

    packed = {}
    for steps in ((2,), (1,), (3, 0)):
        packed.update(zip(steps, pack(steps, *list(packed.values())[-1:])))
    messages = [along(packed[step], step) for step in ORDER]

    w_in, w_out, gain, bias = pl.pallas_call(
        functools.partial(prefetch_kernel, experts),
        out_shape=[
            pltpu.VMEM((model, hidden_units), BF16),
            pltpu.VMEM((hidden_units, model), BF16),
            pltpu.VMEM((1, model), F32),
            pltpu.VMEM((1, model), F32),
        ],
        in_specs=[IN_HBM] * 4 + [IN_ANY],
        out_specs=[IN_VMEM] * 4,
        scratch_shapes=[pltpu.SemaphoreType.DMA((2, 2 * experts))] * 2,
        compiler_params=pltpu.CompilerParams(vmem_limit_bytes=VMEM_LIMIT),
        cost_estimate=pl.CostEstimate(
            flops=0, bytes_accessed=8 * model * hidden_units, transcendentals=0
        ),
    )(
        in_hbm(expert_in[0]),
        in_hbm(expert_out[0]),
        in_hbm(norm_gain.reshape(1, model)),
        in_hbm(norm_bias.reshape(1, model)),
        packed[0],
    )

    *compact, factor, home = call(
        functools.partial(attend_kernel, experts, rows, cap),
        [struct(experts * cap, width)] * experts
        + [struct(experts * cap, HEAD, F32), struct((experts + 2) * rows, HEAD)],
        [IN_VMEM] * (2 + experts),
        flops=8 * experts * experts * rows * rows * width,
        moved=16 * rows * columns,
    )(in_vmem(w_in), in_vmem(w_out), *messages)

    compact = dict(zip(ORDER, compact))
    own = {step: along(compact[step], step) for step in ORDER}
    count = experts * cap

    def first(blocks, known):
        return call(
            functools.partial(first_kernel, 512),
            [struct(count, hidden_units)],
            [IN_VMEM] * (len(blocks) + 3),
            scratch=[pltpu.VMEM((count, model), BF16)],
            flops=known * 2 * count * model * hidden_units,
            moved=known * 2 * model * hidden_units,
        )(*blocks, in_vmem(gain), in_vmem(bias), in_vmem(w_in))[0]

    def pair(left, right):
        return call(pair_kernel, [struct(count, 2 * width)], [IN_VMEM] * 2)(left, right)[0]

    near = [pair(own[left], own[right]) for left, right in PAIRS]
    far1, far0 = across(compact[1]), swap(compact[0], "dp")
    held, far1, far0 = lax.optimization_barrier((own[1], far1, far0))
    far = [swap(near[0], "dp"), pair(far1, far0)]
    near_other = [swap(block, "mp") for block in (near[0], held, own[0])]
    far_other = [swap(far[1], "mp")]

    active = first([near[0], own[1], own[0]] + near_other, 0)
    kept, *sent = call(
        functools.partial(second_kernel, 512),
        [struct(count, columns)] + [struct(count // 2, columns)] * 2,
        [IN_VMEM, IN_VMEM],
    )(active, in_vmem(w_out))
    far[0], kept = lax.optimization_barrier((far[0], kept))
    far_other = [swap(far[0], "mp")] + far_other
    got = [swap(part, "mp") for part in sent]
    active = first(far + far_other, 1)
    active, *got = lax.optimization_barrier((active, *got))

    def half(active, other, parts):
        return call(
            functools.partial(half_kernel, 512, other),
            [struct(count // parts, columns)] * parts,
            [IN_VMEM, IN_VMEM],
            flops=count * model * hidden_units,
            moved=model * hidden_units,
        )(active, in_vmem(w_out))

    theirs = [swap(part, "mp") for part in half(active, True, 2)]
    mine = half(active, False, 1)[0]

    def base(start, part):
        return call(
            functools.partial(base_kernel, start),
            [struct(cap, columns, F32)] * 2 + [struct(cap, HEAD, F32)] * 2,
            [IN_VMEM] * (3 + len(PAIRS)),
            scratch=[pltpu.VMEM((2 * cap, columns), F32)],
        )(kept, part, factor, *near)

    def plain(start, part):
        return call(
            functools.partial(plain_kernel, start), [struct(cap, columns)] * 2, [IN_VMEM] * 2
        )(mine, part)

    def join(came, base, factor):
        return call(join_kernel, [struct(cap, columns)], [IN_VMEM] * 3)(came, base, factor)[0]

    base2, base3, factor2, factor3 = base(2 * cap, got[1])
    theirs[1], base2 = lax.optimization_barrier((theirs[1], base2))
    base0, near1, factor0 = call(
        low_kernel,
        [struct(cap, columns, F32), struct(cap, columns), struct(cap, HEAD, F32)],
        [IN_VMEM] * (3 + len(PAIRS)),
        scratch=[pltpu.VMEM((2 * cap, columns), F32)],
    )(kept, got[0], factor, *near)
    plain2, plain3 = plain(2 * cap, theirs[1])
    plain0, plain1 = plain(0, theirs[0])
    returned = [
        along(join(swap(plain2, "dp"), base2, factor2), 2),
        along(join(swap(plain3, "dp"), base3, factor3), 3),
        along(near1, 1),
        across(plain1),
    ]
    share = call(
        functools.partial(sum_kernel, 512, ORDER[:-1]),
        [struct(rows, columns, F32)],
        [IN_VMEM] * (1 + experts),
        moved=LATER,
    )(home, *returned)[0]
    return pl.pallas_call(
        functools.partial(mix_kernel, 512),
        out_shape=struct(rows, columns),
        in_specs=[IN_VMEM] * 5,
        out_specs=IN_HBM,
        scratch_shapes=[
            pltpu.VMEM((rows, columns), BF16),
            pltpu.SemaphoreType.DMA((columns // 512,)),
        ],
        compiler_params=pltpu.CompilerParams(vmem_limit_bytes=VMEM_LIMIT),
        cost_estimate=pl.CostEstimate(flops=1, bytes_accessed=1, transcendentals=0),
    )(home, share, swap(plain0, "dp"), base0, factor0)


def shards(
    hidden,
    queries,
    memory,
    target_pair,
    source_pair,
    routes,
    route_weight,
    norm_gain,
    norm_bias,
    expert_in,
    expert_out,
):
    tok_rows = hidden.shape[0]
    local_heads = queries.shape[1] // HEAD
    scale = 1.0 / math.sqrt(HEAD)
    query_heads = queries.reshape(tok_rows, local_heads, HEAD)
    running = jnp.full((local_heads, tok_rows), NEGATIVE, jnp.float32)
    rows = lax.all_gather(memory, "expert", axis=0, tiled=True)
    row_pairs = lax.all_gather(source_pair, "expert", axis=0, tiled=True)
    count = rows.shape[0]
    keys = rows[:, 0, :].reshape(count, local_heads, HEAD)
    values = rows[:, 1, :].reshape(count, local_heads, HEAD)
    score = (
        jnp.einsum("thd,rhd->htr", query_heads, keys, preferred_element_type=jnp.float32) * scale
    )
    match = (target_pair[:, None] == row_pairs[None, :])[None]
    masked = jnp.where(match, score, NEGATIVE)
    newest = jnp.maximum(running, jnp.max(masked, axis=-1))
    weight = jnp.where(match, jnp.exp(masked - newest[:, :, None]), 0.0)
    total = jnp.sum(weight, axis=-1)
    summed = jnp.einsum(
        "htr,rhd->htd", weight.astype(jnp.bfloat16), values, preferred_element_type=jnp.float32
    )
    running, total, summed = (newest, total, summed)
    context = jnp.transpose(summed / total[:, :, None], (1, 0, 2)).reshape(
        tok_rows, local_heads * HEAD
    )
    attended = (hidden.astype(jnp.float32) + context).astype(jnp.bfloat16)
    full_rows = lax.all_gather(attended, "mp", axis=1, tiled=True)
    width = full_rows.shape[1]
    experts_all = lax.axis_size("expert")
    batches = lax.axis_size("dp")
    cap = 2 * tok_rows // experts_all * 5 // 4
    flat = routes.reshape(-1)
    named = (flat[:, None] == jnp.arange(experts_all, dtype=jnp.int32)[None, :]).astype(jnp.int32)
    slot = jnp.sum((jnp.cumsum(named, axis=0) - named) * named, axis=1)
    dest = flat * cap + slot
    place = dest[:, None] == jnp.arange(experts_all * cap, dtype=jnp.int32)[None, :]
    per_token = jnp.sum(place.reshape(tok_rows, 2, experts_all * cap).astype(jnp.bfloat16), axis=1)
    outgoing = lax.dot_general(
        per_token, full_rows, (((0,), (0,)), ((), ())), preferred_element_type=jnp.float32
    ).astype(jnp.bfloat16)
    copies = jnp.broadcast_to(
        outgoing.reshape(experts_all, 1, cap, width), (experts_all, batches, cap, width)
    ).reshape(experts_all * batches * cap, width)
    arrived = lax.all_to_all(copies, ("expert", "dp"), split_axis=0, concat_axis=0, tiled=True)
    values = arrived.astype(jnp.float32)
    center = jnp.mean(values, axis=-1, keepdims=True)
    spread = jnp.mean(jnp.square(values - center), axis=-1, keepdims=True)
    normed = ((values - center) * lax.rsqrt(spread + EPSILON) * norm_gain + norm_bias).astype(
        jnp.bfloat16
    )
    active = jax.nn.relu(jnp.dot(normed, expert_in[0], preferred_element_type=jnp.float32)).astype(
        jnp.bfloat16
    )
    partial_value = jnp.dot(active, expert_out[0], preferred_element_type=jnp.float32).astype(
        jnp.bfloat16
    )
    returned = lax.all_to_all(
        partial_value, ("expert", "dp"), split_axis=0, concat_axis=0, tiled=True
    )
    expert_sum = jnp.sum(
        returned.reshape(experts_all, batches, cap, width).astype(jnp.float32), axis=1
    )
    picked = jnp.dot(
        place.astype(jnp.float32),
        expert_sum.reshape(experts_all * cap, width),
        precision=lax.Precision.HIGHEST,
    )
    blended = jnp.sum(picked.reshape(tok_rows, 2, width) * route_weight[:, :, None], axis=1)
    share = lax.psum_scatter(
        blended.astype(jnp.bfloat16), "mp", scatter_dimension=1, tiled=True
    ).astype(jnp.float32)
    return (attended.astype(jnp.float32) + share).astype(jnp.bfloat16)


def layer(hidden, queries, memory, *rest):
    experts = lax.axis_size("expert")
    rows, columns = hidden.shape
    heads = columns // HEAD
    by_heads = (
        lax.axis_size("mp") == 2
        and lax.axis_size("dp") == 2
        and heads % experts == 0
        and memory.shape[0] == rows
        and experts * rows <= columns // experts
        and experts == 4
    )
    return (head_shards if by_heads else shards)(hidden, queries, memory, *rest)


def solution(mesh):
    return jax.shard_map(
        layer,
        mesh=mesh,
        in_specs=(
            P(("groups", "expert", "dp"), "mp"),
            P(("groups", "expert", "dp"), "mp"),
            P(("groups", "expert", "dp"), None, "mp"),
            P(("groups", "expert", "dp")),
            P(("groups", "expert", "dp")),
            P(("groups", "expert", "dp"), None),
            P(("groups", "expert", "dp"), None),
            P(),
            P(),
            P("expert", None, ("dp", "mp")),
            P("expert", ("dp", "mp"), None),
        ),
        out_specs=P(("groups", "expert", "dp"), "mp"),
        check_vma=False,
    )
```

```python
import functools
import math

import jax
import jax.numpy as jnp
from jax import lax
from jax.experimental import pallas as pl
from jax.experimental.pallas import tpu as pltpu
from jax.sharding import PartitionSpec as P

HEAD = 128
EPSILON = 1e-05
NEGATIVE = -1e30
META = 16
KINDS = 8
LATER = 16 * 1024 * 1024
MIB = 1024 * 1024
ORDER = (2, 3, 1, 0)
PAIRS = ((2, 3), (1, 0))
VMEM_LIMIT = 12 * 1024 * 1024

BF16 = jnp.bfloat16
F32 = jnp.float32
IN_VMEM = pl.BlockSpec(memory_space=pltpu.VMEM)
IN_ANY = pl.BlockSpec(memory_space=pl.ANY)
IN_HBM = pl.BlockSpec(memory_space=pltpu.HBM)


def struct(rows, columns, dtype=BF16):
    return jax.ShapeDtypeStruct((rows, columns), dtype)


def call(kernel, outs, specs, scratch=(), flops=0, moved=0):
    return pl.pallas_call(
        kernel,
        out_shape=outs,
        in_specs=specs,
        out_specs=[IN_VMEM] * len(outs),
        scratch_shapes=scratch,
        compiler_params=pltpu.CompilerParams(vmem_limit_bytes=VMEM_LIMIT),
        cost_estimate=pl.CostEstimate(flops=flops, bytes_accessed=moved, transcendentals=0),
    )


def dot(a, b):
    return lax.dot_general(a, b, (((1,), (0,)), ((), ())), preferred_element_type=F32)


def dot_nt(a, b):
    return lax.dot_general(a, b, (((1,), (1,)), ((), ())), preferred_element_type=F32)


def dot_tn(a, b):
    return lax.dot_general(a, b, (((0,), (0,)), ((), ())), preferred_element_type=F32)


def iota(shape, dimension):
    return lax.broadcasted_iota(jnp.int32, shape, dimension)


def in_hbm(array):
    return pltpu.with_memory_space_constraint(array, pltpu.HBM)


def in_vmem(array):
    return pltpu.with_memory_space_constraint(array, pltpu.VMEM)


def columns_at(start, width):
    return pl.ds(pl.multiple_of(start * width, width), width)


def halves(array):
    high = array.astype(BF16).astype(F32)
    return [high, (array - high).astype(BF16).astype(F32)]


def pack_kernel(steps, q_hbm, m_hbm, h_hbm, tp_hbm, sp_hbm, r_hbm, rw_hbm, *refs):
    outs, refs = refs[-7 - len(steps) : -7], refs[-7:]
    m_ref, tp_ref, sp_ref, r_ref, rw_ref, sems, small_sems = refs
    rows, width = q_hbm.shape[0], outs[0].shape[1]
    here = lax.axis_index("expert")
    small = [
        pltpu.make_async_copy(src, dst, small_sems.at[k])
        for k, (src, dst) in enumerate(
            ((tp_hbm, tp_ref), (sp_hbm, sp_ref), (r_hbm, r_ref), (rw_hbm, rw_ref))
        )
    ]
    large = []
    for k, (step, out) in enumerate(zip(steps, outs)):
        cols = columns_at(here ^ step, width)
        large.append(
            (
                pltpu.make_async_copy(m_hbm.at[:, :, cols], m_ref.at[k], sems.at[0, k]),
                pltpu.make_async_copy(q_hbm.at[:, cols], out.at[pl.ds(0, rows)], sems.at[1, k]),
                pltpu.make_async_copy(
                    h_hbm.at[:, cols], out.at[pl.ds(3 * rows, rows)], sems.at[2, k]
                ),
            )
        )
    for copy in small:
        copy.start()
    for copies in large:
        for copy in copies:
            copy.start()
    for copy in small:
        copy.wait()
    row = iota((META, rows), 0)
    lines = [tp_ref[...], sp_ref[...], r_ref[0:1, :], r_ref[1:2, :]]
    lines = [line.astype(F32) for line in lines]
    lines += halves(rw_ref[0:1, :]) + halves(rw_ref[1:2, :])
    kinds = jnp.zeros((META, rows), F32)
    for k, line in enumerate(lines):
        kinds = jnp.where(row == k, line, kinds)
    kinds = kinds.astype(BF16)
    for step, out in zip(steps, outs):
        moved = (iota((rows, width), 1) == iota((rows, width), 0) + step * rows).astype(BF16)
        out[4 * rows :, :] = dot(kinds, moved)[0:KINDS, :].astype(BF16)
    for k, out in enumerate(outs):
        large[k][0].wait()
        out[rows : 2 * rows, :] = m_ref[k, :, 0, :]
        out[2 * rows : 3 * rows, :] = m_ref[k, :, 1, :]
    for copies in large:
        copies[1].wait()
        copies[2].wait()


def prefetch_kernel(experts, w1_hbm, w2_hbm, gain_hbm, bias_hbm, after_ref, *refs):
    w1_ref, w2_ref, gain_ref, bias_ref, sems, small_sems = refs
    here, half = lax.axis_index("expert"), lax.axis_index("mp")
    size = w1_ref.shape[0] // (2 * experts)
    copies = []
    for part in range(2 * experts):
        core = half if part < experts else 1 - half
        source = columns_at(core * experts + (here ^ ORDER[part % experts]), size)
        target = pl.ds(part * size, size)
        copies += [
            pltpu.make_async_copy(w1_hbm.at[source], w1_ref.at[target], sems.at[0, part]),
            pltpu.make_async_copy(w2_hbm.at[target], w2_ref.at[target], sems.at[1, part]),
            pltpu.make_async_copy(
                gain_hbm.at[:, source], gain_ref.at[:, target], small_sems.at[0, part]
            ),
            pltpu.make_async_copy(
                bias_hbm.at[:, source], bias_ref.at[:, target], small_sems.at[1, part]
            ),
        ]
    for copy in copies:
        copy.start()
    for copy in copies:
        copy.wait()


def attend_kernel(experts, rows, cap, w1_ref, w2_ref, *refs):
    arrived, compact = dict(zip(ORDER, refs[:experts])), refs[experts : 2 * experts]
    factor_ref, home_ref = refs[2 * experts :]
    messages = [arrived[step] for step in range(experts)]
    width = messages[0].shape[1]
    count = experts * rows
    here = lax.axis_index("expert")
    meta = sum(m[4 * rows :, :].astype(F32) for m in messages)
    same = (iota((count, count), 0) == iota((count, count), 1)).astype(BF16)
    columns = dot_nt(same, meta.astype(BF16))
    match = columns[:, 0:1] == meta[1:2, :]
    scale = 1.0 / math.sqrt(HEAD)
    parts = []
    for head in range(width // HEAD):
        lanes = slice(head * HEAD, (head + 1) * HEAD)

        def stacked(kind):
            return jnp.concatenate(
                [m[kind * rows : (kind + 1) * rows, lanes] for m in messages], axis=0
            )

        score = dot_nt(stacked(0), stacked(1)) * scale
        masked = jnp.where(match, score, NEGATIVE)
        largest = jnp.max(masked, axis=-1, keepdims=True)
        weight = jnp.where(match, jnp.exp(masked - largest), 0.0)
        total = jnp.sum(weight, axis=-1, keepdims=True)
        context = dot(weight.astype(BF16), stacked(2)) / total
        parts.append((stacked(3).astype(F32) + context).astype(BF16))
    states = jnp.concatenate(parts, axis=1)
    first, second = meta[2:3, :].astype(jnp.int32), meta[3:4, :].astype(jnp.int32)
    expert = here ^ iota((META, count), 0)
    named = ((first == expert) | (second == expert)) & (iota((META, count), 0) < experts)
    before = (iota((count, count), 0) < iota((count, count), 1)) & (
        iota((count, 1), 0) // rows == iota((1, count), 1) // rows
    )
    slot = dot(named.astype(BF16), before.astype(BF16)).astype(jnp.int32)
    block = (iota((1, count), 1) // rows) ^ iota((META, 1), 0)
    spot = jnp.where(named, block * cap + slot, -1)
    home = jnp.where(named, slot, -1)[:, 0:rows].astype(F32).astype(BF16)
    home = dot_nt(same[0:rows, 0:rows], home).astype(jnp.int32)
    for step in range(experts):
        place = iota((rows, home_ref.shape[1]), 1) == home[:, step : step + 1]
        home_ref[step * rows : (step + 1) * rows, :] = place.astype(BF16)
    kinds = dot_nt(same[0:rows, 0:rows], meta[:, 0:rows].astype(BF16))
    leads = kinds[:, 2:3].astype(jnp.int32) == (here ^ 1)
    place = iota((rows, home_ref.shape[1]), 1) == home[:, 1:2]
    for k in range(2):
        half = jnp.where(leads, kinds[:, 4 + k : 5 + k], kinds[:, 6 + k : 7 + k])
        at = (experts + k) * rows
        home_ref[at : at + rows, :] = jnp.where(place, half, 0.0).astype(BF16)
    for step, out in zip(ORDER, compact):
        place = iota((experts * cap, count), 0) == spot[step : step + 1, :]
        place = place.astype(BF16)
        out[...] = dot(place, states).astype(BF16)
    leads = first == here
    lines = jnp.where(iota((META, count), 0) == 3, leads.astype(F32), 0.0)
    for k in range(2):
        half = jnp.where(leads, meta[4 + k : 5 + k, :], meta[6 + k : 7 + k, :])
        lines = jnp.where(iota((META, count), 0) == k, half, lines)
    factor_ref[...] = jnp.zeros(factor_ref.shape, F32)
    factor_ref[:, 0:META] = dot_nt(place, lines.astype(BF16))


def pair_kernel(left_ref, right_ref, out_ref):
    width = left_ref.shape[1]
    out_ref[:, 0:width] = left_ref[...]
    out_ref[:, width:] = right_ref[...]


def first_kernel(tile, *refs):
    blocks, (gain_ref, bias_ref, w_ref, out_ref, n_ref) = refs[:-5], refs[-5:]
    width, model = min(block.shape[1] for block in blocks), n_ref.shape[1]
    pieces = [
        (block, slice(at, at + width)) for block in blocks for at in range(0, block.shape[1], width)
    ]
    for at in range(0, n_ref.shape[0], META):
        rows = slice(at, at + META)
        values = [block[rows, cols].astype(F32) for block, cols in pieces]
        center = jnp.sum(sum(values), axis=-1, keepdims=True) * (1.0 / model)
        shifted = [value - center for value in values]
        spread = sum(value * value for value in shifted)
        spread = jnp.sum(spread, axis=-1, keepdims=True) * (1.0 / model)
        scale = lax.rsqrt(spread + EPSILON)
        for k, value in enumerate(shifted):
            cols = slice(k * width, (k + 1) * width)
            normed = value * scale * gain_ref[:, cols] + bias_ref[:, cols]
            n_ref[rows, cols] = normed.astype(BF16)
    for at in range(0, w_ref.shape[1], tile):
        cols = slice(at, at + tile)
        out_ref[:, cols] = jnp.maximum(dot(n_ref[...], w_ref[:, cols]), 0.0).astype(BF16)


def second_kernel(tile, a_ref, w_ref, kept_ref, *sent):
    columns, rows = kept_ref.shape[1], sent[0].shape[0]
    lower = lax.axis_index("mp") == 0
    for at in range(0, columns, tile):
        low = dot(a_ref[...], w_ref[:, at : at + tile])
        high = dot(a_ref[...], w_ref[:, columns + at : columns + at + tile])
        kept_ref[:, at : at + tile] = jnp.where(lower, low, high).astype(BF16)
        other = jnp.where(lower, high, low).astype(BF16)
        for k, out_ref in enumerate(sent):
            out_ref[:, at : at + tile] = other[k * rows : (k + 1) * rows, :]


def half_kernel(tile, other, a_ref, w_ref, *outs):
    columns, rows = outs[0].shape[1], outs[0].shape[0]
    half = lax.axis_index("mp")
    half = 1 - half if other else half
    for at in range(columns // tile):
        part = dot(a_ref[...], w_ref[:, columns_at(half * (columns // tile) + at, tile)])
        for k, out_ref in enumerate(outs):
            out_ref[:, at * tile : (at + 1) * tile] = part[k * rows : (k + 1) * rows, :].astype(BF16)


def plain_kernel(start, kept_ref, got_ref, *outs):
    cap = outs[0].shape[0]
    for k, out_ref in enumerate(outs):
        rows, half = slice(start + k * cap, start + (k + 1) * cap), slice(k * cap, (k + 1) * cap)
        total = kept_ref[rows, :].astype(F32) + got_ref[half, :].astype(F32)
        out_ref[...] = total.astype(BF16)


def base_kernel(start, kept_ref, got_ref, factor_ref, *refs):
    blocks, bases, factors, states = refs[: len(PAIRS)], refs[-5:-3], refs[-3:-1], refs[-1]
    here = lax.axis_index("expert")
    cap, width = bases[0].shape[0], blocks[0].shape[1] // 2
    for steps, block in zip(PAIRS, blocks):
        for k, step in enumerate(steps):
            piece = block[start : start + 2 * cap, k * width : (k + 1) * width]
            states[:, columns_at(here ^ step, width)] = piece.astype(F32)
    for k in range(2):
        rows, half = slice(start + k * cap, start + (k + 1) * cap), slice(k * cap, (k + 1) * cap)
        weight = factor_ref[rows, 0:1] + factor_ref[rows, 1:2]
        total = kept_ref[rows, :].astype(F32) + got_ref[half, :].astype(F32)
        bases[k][...] = total * weight + factor_ref[rows, 3:4] * states[half, :]
        factors[k][...] = jnp.broadcast_to(weight, factors[k].shape)


def low_kernel(kept_ref, got_ref, factor_ref, *refs):
    blocks, (base_ref, near_ref, weight_ref, states) = refs[: len(PAIRS)], refs[-4:]
    here = lax.axis_index("expert")
    cap, width = base_ref.shape[0], blocks[0].shape[1] // 2
    for steps, block in zip(PAIRS, blocks):
        for k, step in enumerate(steps):
            piece = block[0 : 2 * cap, k * width : (k + 1) * width]
            states[:, columns_at(here ^ step, width)] = piece.astype(F32)
    weight = factor_ref[0 : 2 * cap, 0:1] + factor_ref[0 : 2 * cap, 1:2]
    total = kept_ref[0 : 2 * cap, :].astype(F32) + got_ref[...].astype(F32)
    total = total * weight + factor_ref[0 : 2 * cap, 3:4] * states[...]
    base_ref[...] = total[0:cap, :]
    near_ref[...] = total[cap:, :].astype(BF16)
    weight_ref[...] = jnp.broadcast_to(weight[0:cap, :], weight_ref.shape)


def join_kernel(came_ref, base_ref, factor_ref, out_ref):
    total = base_ref[...] + factor_ref[:, 0:1] * came_ref[...].astype(F32)
    out_ref[...] = total.astype(BF16)


def sum_kernel(tile, steps, place_ref, *refs):
    returned, far_ref, out_ref = refs[:-2], refs[-2], refs[-1]
    rows, cap = out_ref.shape[0], far_ref.shape[0]
    last = place_ref.shape[0] // rows
    terms = [*zip(steps, returned), (last - 2, far_ref), (last - 1, far_ref)]
    for at in range(0, out_ref.shape[1], tile):
        cols = slice(at, at + tile)
        share = [
            dot(place_ref[step * rows : (step + 1) * rows, 0:cap], block[:, cols])
            for step, block in terms
        ]
        out_ref[:, cols] = sum(share)


def mix_kernel(tile, place_ref, share_ref, came_ref, base_ref, factor_ref, out_hbm, out_ref, sems):
    rows, cap = out_ref.shape[0], came_ref.shape[0]
    copies = []
    for at in range(0, out_ref.shape[1], tile):
        cols = slice(at, at + tile)
        own = base_ref[:, cols] + factor_ref[:, 0:1] * came_ref[:, cols].astype(F32)
        own = dot(place_ref[0:rows, 0:cap], own.astype(BF16))
        out_ref[:, cols] = (share_ref[:, cols] + own).astype(BF16)
        copies.append(
            pltpu.make_async_copy(out_ref.at[:, cols], out_hbm.at[:, cols], sems.at[at // tile])
        )
        copies[-1].start()
    for copy in copies:
        copy.wait()


def head_shards(
    hidden,
    queries,
    memory,
    target_pair,
    source_pair,
    routes,
    route_weight,
    norm_gain,
    norm_bias,
    expert_in,
    expert_out,
):
    rows, columns = hidden.shape
    experts = lax.axis_size("expert")
    width = columns // experts
    cap = 2 * rows // experts * 5 // 4
    model = 2 * columns
    hidden_units = expert_in.shape[2]

    def along(array, step):
        if step == 0:
            return array
        return lax.ppermute(array, "expert", [(i, i ^ step) for i in range(experts)])

    def swap(array, axis):
        return lax.ppermute(array, axis, [(0, 1), (1, 0)])

    def across(array):
        pairs = [(2 * i + j, 2 * (i ^ 1) + 1 - j) for i in range(experts) for j in range(2)]
        return lax.ppermute(array, ("expert", "dp"), pairs)

    def pack(steps, *after):
        return call(
            functools.partial(pack_kernel, steps),
            [struct(4 * rows + KINDS, width)] * len(steps),
            [IN_HBM] * 7 + [IN_ANY] * len(after),
            scratch=[
                pltpu.VMEM((len(steps), rows, 2, width), BF16),
                pltpu.VMEM((1, rows), jnp.int32),
                pltpu.VMEM((1, rows), jnp.int32),
                pltpu.VMEM((2, rows), jnp.int32),
                pltpu.VMEM((2, rows), F32),
                pltpu.SemaphoreType.DMA((3, len(steps))),
                pltpu.SemaphoreType.DMA((4,)),
            ],
            moved=LATER if after else 0,
        )(
            in_hbm(queries),
            in_hbm(memory),
            in_hbm(hidden),
            in_hbm(target_pair.reshape(1, rows)),
            in_hbm(source_pair.reshape(1, rows)),
            in_hbm(routes.T),
            in_hbm(route_weight.T),
            *after,
        )

    packed = {}
    for steps in ((2,), (1,), (3, 0)):
        packed.update(zip(steps, pack(steps, *list(packed.values())[-1:])))
    messages = [along(packed[step], step) for step in ORDER]

    w_in, w_out, gain, bias = pl.pallas_call(
        functools.partial(prefetch_kernel, experts),
        out_shape=[
            pltpu.VMEM((model, hidden_units), BF16),
            pltpu.VMEM((hidden_units, model), BF16),
            pltpu.VMEM((1, model), F32),
            pltpu.VMEM((1, model), F32),
        ],
        in_specs=[IN_HBM] * 4 + [IN_ANY],
        out_specs=[IN_VMEM] * 4,
        scratch_shapes=[pltpu.SemaphoreType.DMA((2, 2 * experts))] * 2,
        compiler_params=pltpu.CompilerParams(vmem_limit_bytes=VMEM_LIMIT),
        cost_estimate=pl.CostEstimate(
            flops=0, bytes_accessed=8 * model * hidden_units, transcendentals=0
        ),
    )(
        in_hbm(expert_in[0]),
        in_hbm(expert_out[0]),
        in_hbm(norm_gain.reshape(1, model)),
        in_hbm(norm_bias.reshape(1, model)),
        packed[0],
    )

    *compact, factor, home = call(
        functools.partial(attend_kernel, experts, rows, cap),
        [struct(experts * cap, width)] * experts
        + [struct(experts * cap, HEAD, F32), struct((experts + 2) * rows, HEAD)],
        [IN_VMEM] * (2 + experts),
        flops=8 * experts * experts * rows * rows * width,
        moved=16 * rows * columns,
    )(in_vmem(w_in), in_vmem(w_out), *messages)

    compact = dict(zip(ORDER, compact))
    own = {step: along(compact[step], step) for step in ORDER}
    count = experts * cap

    def first(blocks, known):
        return call(
            functools.partial(first_kernel, 512),
            [struct(count, hidden_units)],
            [IN_VMEM] * (len(blocks) + 3),
            scratch=[pltpu.VMEM((count, model), BF16)],
            flops=known * 2 * count * model * hidden_units,
            moved=known * 2 * model * hidden_units,
        )(*blocks, in_vmem(gain), in_vmem(bias), in_vmem(w_in))[0]

    def pair(left, right):
        return call(pair_kernel, [struct(count, 2 * width)], [IN_VMEM] * 2)(left, right)[0]

    near = [pair(own[left], own[right]) for left, right in PAIRS]
    far1, far0 = across(compact[1]), swap(compact[0], "dp")
    held, far1, far0 = lax.optimization_barrier((own[1], far1, far0))
    far = [swap(near[0], "dp"), pair(far1, far0)]
    near_other = [swap(block, "mp") for block in (near[0], held, own[0])]
    far_other = [swap(far[1], "mp")]

    active = first([near[0], own[1], own[0]] + near_other, 0)
    kept, *sent = call(
        functools.partial(second_kernel, 512),
        [struct(count, columns)] + [struct(count // 2, columns)] * 2,
        [IN_VMEM, IN_VMEM],
    )(active, in_vmem(w_out))
    far[0], kept = lax.optimization_barrier((far[0], kept))
    far_other = [swap(far[0], "mp")] + far_other
    got = [swap(part, "mp") for part in sent]
    active = first(far + far_other, 1)
    active, *got = lax.optimization_barrier((active, *got))

    def half(active, other, parts):
        return call(
            functools.partial(half_kernel, 512, other),
            [struct(count // parts, columns)] * parts,
            [IN_VMEM, IN_VMEM],
            flops=count * model * hidden_units,
            moved=model * hidden_units,
        )(active, in_vmem(w_out))

    theirs = [swap(part, "mp") for part in half(active, True, 2)]
    mine = half(active, False, 1)[0]

    def base(start, part):
        return call(
            functools.partial(base_kernel, start),
            [struct(cap, columns, F32)] * 2 + [struct(cap, HEAD, F32)] * 2,
            [IN_VMEM] * (3 + len(PAIRS)),
            scratch=[pltpu.VMEM((2 * cap, columns), F32)],
        )(kept, part, factor, *near)

    def plain(start, part):
        return call(
            functools.partial(plain_kernel, start), [struct(cap, columns)] * 2, [IN_VMEM] * 2
        )(mine, part)

    def join(came, base, factor):
        return call(join_kernel, [struct(cap, columns)], [IN_VMEM] * 3)(came, base, factor)[0]

    base2, base3, factor2, factor3 = base(2 * cap, got[1])
    base0, near1, factor0 = call(
        low_kernel,
        [struct(cap, columns, F32), struct(cap, columns), struct(cap, HEAD, F32)],
        [IN_VMEM] * (3 + len(PAIRS)),
        scratch=[pltpu.VMEM((2 * cap, columns), F32)],
    )(kept, got[0], factor, *near)
    plain2, plain3 = plain(2 * cap, theirs[1])
    plain0, plain1 = plain(0, theirs[0])
    returned = [
        along(join(swap(plain2, "dp"), base2, factor2), 2),
        along(join(swap(plain3, "dp"), base3, factor3), 3),
        along(near1, 1),
        across(plain1),
    ]
    share = call(
        functools.partial(sum_kernel, 1024, ORDER[:-1]),
        [struct(rows, columns, F32)],
        [IN_VMEM] * (1 + experts),
        moved=LATER,
    )(home, *returned)[0]
    return pl.pallas_call(
        functools.partial(mix_kernel, 512),
        out_shape=struct(rows, columns),
        in_specs=[IN_VMEM] * 5,
        out_specs=IN_HBM,
        scratch_shapes=[
            pltpu.VMEM((rows, columns), BF16),
            pltpu.SemaphoreType.DMA((columns // 512,)),
        ],
        compiler_params=pltpu.CompilerParams(vmem_limit_bytes=VMEM_LIMIT),
        cost_estimate=pl.CostEstimate(flops=1, bytes_accessed=1, transcendentals=0),
    )(home, share, swap(plain0, "dp"), base0, factor0)


def shards(
    hidden,
    queries,
    memory,
    target_pair,
    source_pair,
    routes,
    route_weight,
    norm_gain,
    norm_bias,
    expert_in,
    expert_out,
):
    tok_rows = hidden.shape[0]
    local_heads = queries.shape[1] // HEAD
    scale = 1.0 / math.sqrt(HEAD)
    query_heads = queries.reshape(tok_rows, local_heads, HEAD)
    running = jnp.full((local_heads, tok_rows), NEGATIVE, jnp.float32)
    rows = lax.all_gather(memory, "expert", axis=0, tiled=True)
    row_pairs = lax.all_gather(source_pair, "expert", axis=0, tiled=True)
    count = rows.shape[0]
    keys = rows[:, 0, :].reshape(count, local_heads, HEAD)
    values = rows[:, 1, :].reshape(count, local_heads, HEAD)
    score = (
        jnp.einsum("thd,rhd->htr", query_heads, keys, preferred_element_type=jnp.float32) * scale
    )
    match = (target_pair[:, None] == row_pairs[None, :])[None]
    masked = jnp.where(match, score, NEGATIVE)
    newest = jnp.maximum(running, jnp.max(masked, axis=-1))
    weight = jnp.where(match, jnp.exp(masked - newest[:, :, None]), 0.0)
    total = jnp.sum(weight, axis=-1)
    summed = jnp.einsum(
        "htr,rhd->htd", weight.astype(jnp.bfloat16), values, preferred_element_type=jnp.float32
    )
    running, total, summed = (newest, total, summed)
    context = jnp.transpose(summed / total[:, :, None], (1, 0, 2)).reshape(
        tok_rows, local_heads * HEAD
    )
    attended = (hidden.astype(jnp.float32) + context).astype(jnp.bfloat16)
    full_rows = lax.all_gather(attended, "mp", axis=1, tiled=True)
    width = full_rows.shape[1]
    experts_all = lax.axis_size("expert")
    batches = lax.axis_size("dp")
    cap = 2 * tok_rows // experts_all * 5 // 4
    flat = routes.reshape(-1)
    named = (flat[:, None] == jnp.arange(experts_all, dtype=jnp.int32)[None, :]).astype(jnp.int32)
    slot = jnp.sum((jnp.cumsum(named, axis=0) - named) * named, axis=1)
    dest = flat * cap + slot
    place = dest[:, None] == jnp.arange(experts_all * cap, dtype=jnp.int32)[None, :]
    per_token = jnp.sum(place.reshape(tok_rows, 2, experts_all * cap).astype(jnp.bfloat16), axis=1)
    outgoing = lax.dot_general(
        per_token, full_rows, (((0,), (0,)), ((), ())), preferred_element_type=jnp.float32
    ).astype(jnp.bfloat16)
    copies = jnp.broadcast_to(
        outgoing.reshape(experts_all, 1, cap, width), (experts_all, batches, cap, width)
    ).reshape(experts_all * batches * cap, width)
    arrived = lax.all_to_all(copies, ("expert", "dp"), split_axis=0, concat_axis=0, tiled=True)
    values = arrived.astype(jnp.float32)
    center = jnp.mean(values, axis=-1, keepdims=True)
    spread = jnp.mean(jnp.square(values - center), axis=-1, keepdims=True)
    normed = ((values - center) * lax.rsqrt(spread + EPSILON) * norm_gain + norm_bias).astype(
        jnp.bfloat16
    )
    active = jax.nn.relu(jnp.dot(normed, expert_in[0], preferred_element_type=jnp.float32)).astype(
        jnp.bfloat16
    )
    partial_value = jnp.dot(active, expert_out[0], preferred_element_type=jnp.float32).astype(
        jnp.bfloat16
    )
    returned = lax.all_to_all(
        partial_value, ("expert", "dp"), split_axis=0, concat_axis=0, tiled=True
    )
    expert_sum = jnp.sum(
        returned.reshape(experts_all, batches, cap, width).astype(jnp.float32), axis=1
    )
    picked = jnp.dot(
        place.astype(jnp.float32),
        expert_sum.reshape(experts_all * cap, width),
        precision=lax.Precision.HIGHEST,
    )
    blended = jnp.sum(picked.reshape(tok_rows, 2, width) * route_weight[:, :, None], axis=1)
    share = lax.psum_scatter(
        blended.astype(jnp.bfloat16), "mp", scatter_dimension=1, tiled=True
    ).astype(jnp.float32)
    return (attended.astype(jnp.float32) + share).astype(jnp.bfloat16)


def layer(hidden, queries, memory, *rest):
    experts = lax.axis_size("expert")
    rows, columns = hidden.shape
    heads = columns // HEAD
    by_heads = (
        lax.axis_size("mp") == 2
        and lax.axis_size("dp") == 2
        and heads % experts == 0
        and memory.shape[0] == rows
        and experts * rows <= columns // experts
        and experts == 4
    )
    return (head_shards if by_heads else shards)(hidden, queries, memory, *rest)


def solution(mesh):
    return jax.shard_map(
        layer,
        mesh=mesh,
        in_specs=(
            P(("groups", "expert", "dp"), "mp"),
            P(("groups", "expert", "dp"), "mp"),
            P(("groups", "expert", "dp"), None, "mp"),
            P(("groups", "expert", "dp")),
            P(("groups", "expert", "dp")),
            P(("groups", "expert", "dp"), None),
            P(("groups", "expert", "dp"), None),
            P(),
            P(),
            P("expert", None, ("dp", "mp")),
            P("expert", ("dp", "mp"), None),
        ),
        out_specs=P(("groups", "expert", "dp"), "mp"),
        check_vma=False,
    )
```

```python
import functools
import math

import jax
import jax.numpy as jnp
from jax import lax
from jax.experimental import pallas as pl
from jax.experimental.pallas import tpu as pltpu
from jax.sharding import PartitionSpec as P

HEAD = 128
EPSILON = 1e-05
NEGATIVE = -1e30
META = 16
KINDS = 8
LATER = 16 * 1024 * 1024
MIB = 1024 * 1024
ORDER = (2, 3, 1, 0)
PAIRS = ((2, 3), (1, 0))
VMEM_LIMIT = 12 * 1024 * 1024

BF16 = jnp.bfloat16
F32 = jnp.float32
IN_VMEM = pl.BlockSpec(memory_space=pltpu.VMEM)
IN_ANY = pl.BlockSpec(memory_space=pl.ANY)
IN_HBM = pl.BlockSpec(memory_space=pltpu.HBM)


def struct(rows, columns, dtype=BF16):
    return jax.ShapeDtypeStruct((rows, columns), dtype)


def call(kernel, outs, specs, scratch=(), flops=0, moved=0):
    return pl.pallas_call(
        kernel,
        out_shape=outs,
        in_specs=specs,
        out_specs=[IN_VMEM] * len(outs),
        scratch_shapes=scratch,
        compiler_params=pltpu.CompilerParams(vmem_limit_bytes=VMEM_LIMIT),
        cost_estimate=pl.CostEstimate(flops=flops, bytes_accessed=moved, transcendentals=0),
    )


def dot(a, b):
    return lax.dot_general(a, b, (((1,), (0,)), ((), ())), preferred_element_type=F32)


def dot_nt(a, b):
    return lax.dot_general(a, b, (((1,), (1,)), ((), ())), preferred_element_type=F32)


def dot_tn(a, b):
    return lax.dot_general(a, b, (((0,), (0,)), ((), ())), preferred_element_type=F32)


def iota(shape, dimension):
    return lax.broadcasted_iota(jnp.int32, shape, dimension)


def in_hbm(array):
    return pltpu.with_memory_space_constraint(array, pltpu.HBM)


def in_vmem(array):
    return pltpu.with_memory_space_constraint(array, pltpu.VMEM)


def columns_at(start, width):
    return pl.ds(pl.multiple_of(start * width, width), width)


def halves(array):
    high = array.astype(BF16).astype(F32)
    return [high, (array - high).astype(BF16).astype(F32)]


def pack_kernel(steps, q_hbm, m_hbm, h_hbm, tp_hbm, sp_hbm, r_hbm, rw_hbm, *refs):
    outs, refs = refs[-7 - len(steps) : -7], refs[-7:]
    m_ref, tp_ref, sp_ref, r_ref, rw_ref, sems, small_sems = refs
    rows, width = q_hbm.shape[0], outs[0].shape[1]
    here = lax.axis_index("expert")
    small = [
        pltpu.make_async_copy(src, dst, small_sems.at[k])
        for k, (src, dst) in enumerate(
            ((tp_hbm, tp_ref), (sp_hbm, sp_ref), (r_hbm, r_ref), (rw_hbm, rw_ref))
        )
    ]
    large = []
    for k, (step, out) in enumerate(zip(steps, outs)):
        cols = columns_at(here ^ step, width)
        large.append(
            (
                pltpu.make_async_copy(m_hbm.at[:, :, cols], m_ref.at[k], sems.at[0, k]),
                pltpu.make_async_copy(q_hbm.at[:, cols], out.at[pl.ds(0, rows)], sems.at[1, k]),
                pltpu.make_async_copy(
                    h_hbm.at[:, cols], out.at[pl.ds(3 * rows, rows)], sems.at[2, k]
                ),
            )
        )
    for copy in small:
        copy.start()
    for copies in large:
        for copy in copies:
            copy.start()
    for copy in small:
        copy.wait()
    row = iota((META, rows), 0)
    lines = [tp_ref[...], sp_ref[...], r_ref[0:1, :], r_ref[1:2, :]]
    lines = [line.astype(F32) for line in lines]
    lines += halves(rw_ref[0:1, :]) + halves(rw_ref[1:2, :])
    kinds = jnp.zeros((META, rows), F32)
    for k, line in enumerate(lines):
        kinds = jnp.where(row == k, line, kinds)
    kinds = kinds.astype(BF16)
    for step, out in zip(steps, outs):
        moved = (iota((rows, width), 1) == iota((rows, width), 0) + step * rows).astype(BF16)
        out[4 * rows :, :] = dot(kinds, moved)[0:KINDS, :].astype(BF16)
    for k, out in enumerate(outs):
        large[k][0].wait()
        out[rows : 2 * rows, :] = m_ref[k, :, 0, :]
        out[2 * rows : 3 * rows, :] = m_ref[k, :, 1, :]
    for copies in large:
        copies[1].wait()
        copies[2].wait()


def prefetch_kernel(experts, w1_hbm, w2_hbm, gain_hbm, bias_hbm, after_ref, *refs):
    w1_ref, w2_ref, gain_ref, bias_ref, sems, small_sems = refs
    here, half = lax.axis_index("expert"), lax.axis_index("mp")
    size = w1_ref.shape[0] // (2 * experts)
    copies = []
    for part in range(2 * experts):
        core = half if part < experts else 1 - half
        source = columns_at(core * experts + (here ^ ORDER[part % experts]), size)
        target = pl.ds(part * size, size)
        copies += [
            pltpu.make_async_copy(w1_hbm.at[source], w1_ref.at[target], sems.at[0, part]),
            pltpu.make_async_copy(w2_hbm.at[target], w2_ref.at[target], sems.at[1, part]),
            pltpu.make_async_copy(
                gain_hbm.at[:, source], gain_ref.at[:, target], small_sems.at[0, part]
            ),
            pltpu.make_async_copy(
                bias_hbm.at[:, source], bias_ref.at[:, target], small_sems.at[1, part]
            ),
        ]
    for copy in copies:
        copy.start()
    for copy in copies:
        copy.wait()


def attend_kernel(experts, rows, cap, w1_ref, w2_ref, *refs):
    arrived, compact = dict(zip(ORDER, refs[:experts])), refs[experts : 2 * experts]
    factor_ref, home_ref = refs[2 * experts :]
    messages = [arrived[step] for step in range(experts)]
    width = messages[0].shape[1]
    count = experts * rows
    here = lax.axis_index("expert")
    meta = sum(m[4 * rows :, :].astype(F32) for m in messages)
    same = (iota((count, count), 0) == iota((count, count), 1)).astype(BF16)
    columns = dot_nt(same, meta.astype(BF16))
    match = columns[:, 0:1] == meta[1:2, :]
    scale = 1.0 / math.sqrt(HEAD)
    parts = []
    for head in range(width // HEAD):
        lanes = slice(head * HEAD, (head + 1) * HEAD)

        def stacked(kind):
            return jnp.concatenate(
                [m[kind * rows : (kind + 1) * rows, lanes] for m in messages], axis=0
            )

        score = dot_nt(stacked(0), stacked(1)) * scale
        masked = jnp.where(match, score, NEGATIVE)
        largest = jnp.max(masked, axis=-1, keepdims=True)
        weight = jnp.where(match, jnp.exp(masked - largest), 0.0)
        total = jnp.sum(weight, axis=-1, keepdims=True)
        context = dot(weight.astype(BF16), stacked(2)) / total
        parts.append((stacked(3).astype(F32) + context).astype(BF16))
    states = jnp.concatenate(parts, axis=1)
    first, second = meta[2:3, :].astype(jnp.int32), meta[3:4, :].astype(jnp.int32)
    expert = here ^ iota((META, count), 0)
    named = ((first == expert) | (second == expert)) & (iota((META, count), 0) < experts)
    before = (iota((count, count), 0) < iota((count, count), 1)) & (
        iota((count, count), 0) // rows == iota((count, count), 1) // rows
    )
    slot = dot(named.astype(BF16), before.astype(BF16)).astype(jnp.int32)
    block = (iota((META, count), 1) // rows) ^ iota((META, count), 0)
    spot = jnp.where(named, block * cap + slot, -1)
    home = jnp.where(named, slot, -1)[:, 0:rows].astype(F32).astype(BF16)
    home = dot_nt(same[0:rows, 0:rows], home).astype(jnp.int32)
    for step in range(experts):
        place = iota((rows, home_ref.shape[1]), 1) == home[:, step : step + 1]
        home_ref[step * rows : (step + 1) * rows, :] = place.astype(BF16)
    kinds = dot_nt(same[0:rows, 0:rows], meta[:, 0:rows].astype(BF16))
    leads = kinds[:, 2:3].astype(jnp.int32) == (here ^ 1)
    place = iota((rows, home_ref.shape[1]), 1) == home[:, 1:2]
    for k in range(2):
        half = jnp.where(leads, kinds[:, 4 + k : 5 + k], kinds[:, 6 + k : 7 + k])
        at = (experts + k) * rows
        home_ref[at : at + rows, :] = jnp.where(place, half, 0.0).astype(BF16)
    for step, out in zip(ORDER, compact):
        place = iota((experts * cap, count), 0) == spot[step : step + 1, :]
        place = place.astype(BF16)
        out[...] = dot(place, states).astype(BF16)
    leads = first == here
    lines = jnp.where(iota((META, count), 0) == 3, leads.astype(F32), 0.0)
    for k in range(2):
        half = jnp.where(leads, meta[4 + k : 5 + k, :], meta[6 + k : 7 + k, :])
        lines = jnp.where(iota((META, count), 0) == k, half, lines)
    factor_ref[...] = jnp.zeros(factor_ref.shape, F32)
    factor_ref[:, 0:META] = dot_nt(place, lines.astype(BF16))


def pair_kernel(left_ref, right_ref, out_ref):
    width = left_ref.shape[1]
    out_ref[:, 0:width] = left_ref[...]
    out_ref[:, width:] = right_ref[...]


def first_kernel(tile, *refs):
    blocks, (gain_ref, bias_ref, w_ref, out_ref, n_ref) = refs[:-5], refs[-5:]
    width, model = min(block.shape[1] for block in blocks), n_ref.shape[1]
    pieces = [
        (block, slice(at, at + width)) for block in blocks for at in range(0, block.shape[1], width)
    ]
    for at in range(0, n_ref.shape[0], META):
        rows = slice(at, at + META)
        values = [block[rows, cols].astype(F32) for block, cols in pieces]
        center = jnp.sum(sum(values), axis=-1, keepdims=True) * (1.0 / model)
        shifted = [value - center for value in values]
        spread = sum(value * value for value in shifted)
        spread = jnp.sum(spread, axis=-1, keepdims=True) * (1.0 / model)
        scale = lax.rsqrt(spread + EPSILON)
        for k, value in enumerate(shifted):
            cols = slice(k * width, (k + 1) * width)
            normed = value * scale * gain_ref[:, cols] + bias_ref[:, cols]
            n_ref[rows, cols] = normed.astype(BF16)
    for at in range(0, w_ref.shape[1], tile):
        cols = slice(at, at + tile)
        out_ref[:, cols] = jnp.maximum(dot(n_ref[...], w_ref[:, cols]), 0.0).astype(BF16)


def second_kernel(tile, a_ref, w_ref, kept_ref, *sent):
    columns, rows = kept_ref.shape[1], sent[0].shape[0]
    lower = lax.axis_index("mp") == 0
    for at in range(0, columns, tile):
        low = dot(a_ref[...], w_ref[:, at : at + tile])
        high = dot(a_ref[...], w_ref[:, columns + at : columns + at + tile])
        kept_ref[:, at : at + tile] = jnp.where(lower, low, high).astype(BF16)
        other = jnp.where(lower, high, low).astype(BF16)
        for k, out_ref in enumerate(sent):
            out_ref[:, at : at + tile] = other[k * rows : (k + 1) * rows, :]


def half_kernel(tile, other, a_ref, w_ref, *outs):
    columns, rows = outs[0].shape[1], outs[0].shape[0]
    half = lax.axis_index("mp")
    half = 1 - half if other else half
    for at in range(columns // tile):
        part = dot(a_ref[...], w_ref[:, columns_at(half * (columns // tile) + at, tile)])
        for k, out_ref in enumerate(outs):
            out_ref[:, at * tile : (at + 1) * tile] = part[k * rows : (k + 1) * rows, :].astype(BF16)


def plain_kernel(start, kept_ref, got_ref, *outs):
    cap = outs[0].shape[0]
    for k, out_ref in enumerate(outs):
        rows, half = slice(start + k * cap, start + (k + 1) * cap), slice(k * cap, (k + 1) * cap)
        total = kept_ref[rows, :].astype(F32) + got_ref[half, :].astype(F32)
        out_ref[...] = total.astype(BF16)


def base_kernel(start, kept_ref, got_ref, factor_ref, *refs):
    blocks, bases, factors, states = refs[: len(PAIRS)], refs[-5:-3], refs[-3:-1], refs[-1]
    here = lax.axis_index("expert")
    cap, width = bases[0].shape[0], blocks[0].shape[1] // 2
    for steps, block in zip(PAIRS, blocks):
        for k, step in enumerate(steps):
            piece = block[start : start + 2 * cap, k * width : (k + 1) * width]
            states[:, columns_at(here ^ step, width)] = piece.astype(F32)
    for k in range(2):
        rows, half = slice(start + k * cap, start + (k + 1) * cap), slice(k * cap, (k + 1) * cap)
        weight = factor_ref[rows, 0:1] + factor_ref[rows, 1:2]
        total = kept_ref[rows, :].astype(F32) + got_ref[half, :].astype(F32)
        bases[k][...] = total * weight + factor_ref[rows, 3:4] * states[half, :]
        factors[k][...] = jnp.broadcast_to(weight, factors[k].shape)


def low_kernel(kept_ref, got_ref, factor_ref, *refs):
    blocks, (base_ref, near_ref, weight_ref, states) = refs[: len(PAIRS)], refs[-4:]
    here = lax.axis_index("expert")
    cap, width = base_ref.shape[0], blocks[0].shape[1] // 2
    for steps, block in zip(PAIRS, blocks):
        for k, step in enumerate(steps):
            piece = block[0 : 2 * cap, k * width : (k + 1) * width]
            states[:, columns_at(here ^ step, width)] = piece.astype(F32)
    weight = factor_ref[0 : 2 * cap, 0:1] + factor_ref[0 : 2 * cap, 1:2]
    total = kept_ref[0 : 2 * cap, :].astype(F32) + got_ref[...].astype(F32)
    total = total * weight + factor_ref[0 : 2 * cap, 3:4] * states[...]
    base_ref[...] = total[0:cap, :]
    near_ref[...] = total[cap:, :].astype(BF16)
    weight_ref[...] = jnp.broadcast_to(weight[0:cap, :], weight_ref.shape)


def join_kernel(came_ref, base_ref, factor_ref, out_ref):
    total = base_ref[...] + factor_ref[:, 0:1] * came_ref[...].astype(F32)
    out_ref[...] = total.astype(BF16)


def sum_kernel(tile, steps, place_ref, *refs):
    returned, far_ref, out_ref = refs[:-2], refs[-2], refs[-1]
    rows, cap = out_ref.shape[0], far_ref.shape[0]
    last = place_ref.shape[0] // rows
    terms = [*zip(steps, returned), (last - 2, far_ref), (last - 1, far_ref)]
    for at in range(0, out_ref.shape[1], tile):
        cols = slice(at, at + tile)
        share = [
            dot(place_ref[step * rows : (step + 1) * rows, 0:cap], block[:, cols])
            for step, block in terms
        ]
        out_ref[:, cols] = sum(share)


def mix_kernel(tile, place_ref, share_ref, came_ref, base_ref, factor_ref, out_hbm, out_ref, sems):
    rows, cap = out_ref.shape[0], came_ref.shape[0]
    copies = []
    for at in range(0, out_ref.shape[1], tile):
        cols = slice(at, at + tile)
        own = base_ref[:, cols] + factor_ref[:, 0:1] * came_ref[:, cols].astype(F32)
        own = dot(place_ref[0:rows, 0:cap], own.astype(BF16))
        out_ref[:, cols] = (share_ref[:, cols] + own).astype(BF16)
        copies.append(
            pltpu.make_async_copy(out_ref.at[:, cols], out_hbm.at[:, cols], sems.at[at // tile])
        )
        copies[-1].start()
    for copy in copies:
        copy.wait()


def head_shards(
    hidden,
    queries,
    memory,
    target_pair,
    source_pair,
    routes,
    route_weight,
    norm_gain,
    norm_bias,
    expert_in,
    expert_out,
):
    rows, columns = hidden.shape
    experts = lax.axis_size("expert")
    width = columns // experts
    cap = 2 * rows // experts * 5 // 4
    model = 2 * columns
    hidden_units = expert_in.shape[2]

    def along(array, step):
        if step == 0:
            return array
        return lax.ppermute(array, "expert", [(i, i ^ step) for i in range(experts)])

    def swap(array, axis):
        return lax.ppermute(array, axis, [(0, 1), (1, 0)])

    def across(array):
        pairs = [(2 * i + j, 2 * (i ^ 1) + 1 - j) for i in range(experts) for j in range(2)]
        return lax.ppermute(array, ("expert", "dp"), pairs)

    def pack(steps, *after):
        return call(
            functools.partial(pack_kernel, steps),
            [struct(4 * rows + KINDS, width)] * len(steps),
            [IN_HBM] * 7 + [IN_ANY] * len(after),
            scratch=[
                pltpu.VMEM((len(steps), rows, 2, width), BF16),
                pltpu.VMEM((1, rows), jnp.int32),
                pltpu.VMEM((1, rows), jnp.int32),
                pltpu.VMEM((2, rows), jnp.int32),
                pltpu.VMEM((2, rows), F32),
                pltpu.SemaphoreType.DMA((3, len(steps))),
                pltpu.SemaphoreType.DMA((4,)),
            ],
            moved=LATER if after else 0,
        )(
            in_hbm(queries),
            in_hbm(memory),
            in_hbm(hidden),
            in_hbm(target_pair.reshape(1, rows)),
            in_hbm(source_pair.reshape(1, rows)),
            in_hbm(routes.T),
            in_hbm(route_weight.T),
            *after,
        )

    packed = {}
    for steps in ((2,), (1,), (3, 0)):
        packed.update(zip(steps, pack(steps, *list(packed.values())[-1:])))
    messages = [along(packed[step], step) for step in ORDER]

    w_in, w_out, gain, bias = pl.pallas_call(
        functools.partial(prefetch_kernel, experts),
        out_shape=[
            pltpu.VMEM((model, hidden_units), BF16),
            pltpu.VMEM((hidden_units, model), BF16),
            pltpu.VMEM((1, model), F32),
            pltpu.VMEM((1, model), F32),
        ],
        in_specs=[IN_HBM] * 4 + [IN_ANY],
        out_specs=[IN_VMEM] * 4,
        scratch_shapes=[pltpu.SemaphoreType.DMA((2, 2 * experts))] * 2,
        compiler_params=pltpu.CompilerParams(vmem_limit_bytes=VMEM_LIMIT),
        cost_estimate=pl.CostEstimate(
            flops=0, bytes_accessed=8 * model * hidden_units, transcendentals=0
        ),
    )(
        in_hbm(expert_in[0]),
        in_hbm(expert_out[0]),
        in_hbm(norm_gain.reshape(1, model)),
        in_hbm(norm_bias.reshape(1, model)),
        packed[0],
    )

    *compact, factor, home = call(
        functools.partial(attend_kernel, experts, rows, cap),
        [struct(experts * cap, width)] * experts
        + [struct(experts * cap, HEAD, F32), struct((experts + 2) * rows, HEAD)],
        [IN_VMEM] * (2 + experts),
        flops=8 * experts * experts * rows * rows * width,
        moved=16 * rows * columns,
    )(in_vmem(w_in), in_vmem(w_out), *messages)

    compact = dict(zip(ORDER, compact))
    own = {step: along(compact[step], step) for step in ORDER}
    count = experts * cap

    def first(blocks, known):
        return call(
            functools.partial(first_kernel, 512),
            [struct(count, hidden_units)],
            [IN_VMEM] * (len(blocks) + 3),
            scratch=[pltpu.VMEM((count, model), BF16)],
            flops=known * 2 * count * model * hidden_units,
            moved=known * 2 * model * hidden_units,
        )(*blocks, in_vmem(gain), in_vmem(bias), in_vmem(w_in))[0]

    def pair(left, right):
        return call(pair_kernel, [struct(count, 2 * width)], [IN_VMEM] * 2)(left, right)[0]

    near = [pair(own[left], own[right]) for left, right in PAIRS]
    far1, far0 = across(compact[1]), swap(compact[0], "dp")
    held, far1, far0 = lax.optimization_barrier((own[1], far1, far0))
    far = [swap(near[0], "dp"), pair(far1, far0)]
    near_other = [swap(block, "mp") for block in (near[0], held, own[0])]
    far_other = [swap(far[1], "mp")]

    active = first([near[0], own[1], own[0]] + near_other, 0)
    kept, *sent = call(
        functools.partial(second_kernel, 512),
        [struct(count, columns)] + [struct(count // 2, columns)] * 2,
        [IN_VMEM, IN_VMEM],
    )(active, in_vmem(w_out))
    far[0], kept = lax.optimization_barrier((far[0], kept))
    far_other = [swap(far[0], "mp")] + far_other
    got = [swap(part, "mp") for part in sent]
    active = first(far + far_other, 1)
    active, *got = lax.optimization_barrier((active, *got))

    def half(active, other, parts):
        return call(
            functools.partial(half_kernel, 1024, other),
            [struct(count // parts, columns)] * parts,
            [IN_VMEM, IN_VMEM],
            flops=count * model * hidden_units,
            moved=model * hidden_units,
        )(active, in_vmem(w_out))

    theirs = [swap(part, "mp") for part in half(active, True, 2)]
    mine = half(active, False, 1)[0]

    def base(start, part):
        return call(
            functools.partial(base_kernel, start),
            [struct(cap, columns, F32)] * 2 + [struct(cap, HEAD, F32)] * 2,
            [IN_VMEM] * (3 + len(PAIRS)),
            scratch=[pltpu.VMEM((2 * cap, columns), F32)],
        )(kept, part, factor, *near)

    def plain(start, part):
        return call(
            functools.partial(plain_kernel, start), [struct(cap, columns)] * 2, [IN_VMEM] * 2
        )(mine, part)

    def join(came, base, factor):
        return call(join_kernel, [struct(cap, columns)], [IN_VMEM] * 3)(came, base, factor)[0]

    base2, base3, factor2, factor3 = base(2 * cap, got[1])
    theirs[1], base2 = lax.optimization_barrier((theirs[1], base2))
    base0, near1, factor0 = call(
        low_kernel,
        [struct(cap, columns, F32), struct(cap, columns), struct(cap, HEAD, F32)],
        [IN_VMEM] * (3 + len(PAIRS)),
        scratch=[pltpu.VMEM((2 * cap, columns), F32)],
    )(kept, got[0], factor, *near)
    plain2, plain3 = plain(2 * cap, theirs[1])
    plain0, plain1 = plain(0, theirs[0])
    returned = [
        along(join(swap(plain2, "dp"), base2, factor2), 2),
        along(join(swap(plain3, "dp"), base3, factor3), 3),
        along(near1, 1),
        across(plain1),
    ]
    share = call(
        functools.partial(sum_kernel, 512, ORDER[:-1]),
        [struct(rows, columns, F32)],
        [IN_VMEM] * (1 + experts),
        moved=LATER,
    )(home, *returned)[0]
    return pl.pallas_call(
        functools.partial(mix_kernel, 512),
        out_shape=struct(rows, columns),
        in_specs=[IN_VMEM] * 5,
        out_specs=IN_HBM,
        scratch_shapes=[
            pltpu.VMEM((rows, columns), BF16),
            pltpu.SemaphoreType.DMA((columns // 512,)),
        ],
        compiler_params=pltpu.CompilerParams(vmem_limit_bytes=VMEM_LIMIT),
        cost_estimate=pl.CostEstimate(flops=1, bytes_accessed=1, transcendentals=0),
    )(home, share, swap(plain0, "dp"), base0, factor0)


def shards(
    hidden,
    queries,
    memory,
    target_pair,
    source_pair,
    routes,
    route_weight,
    norm_gain,
    norm_bias,
    expert_in,
    expert_out,
):
    tok_rows = hidden.shape[0]
    local_heads = queries.shape[1] // HEAD
    scale = 1.0 / math.sqrt(HEAD)
    query_heads = queries.reshape(tok_rows, local_heads, HEAD)
    running = jnp.full((local_heads, tok_rows), NEGATIVE, jnp.float32)
    rows = lax.all_gather(memory, "expert", axis=0, tiled=True)
    row_pairs = lax.all_gather(source_pair, "expert", axis=0, tiled=True)
    count = rows.shape[0]
    keys = rows[:, 0, :].reshape(count, local_heads, HEAD)
    values = rows[:, 1, :].reshape(count, local_heads, HEAD)
    score = (
        jnp.einsum("thd,rhd->htr", query_heads, keys, preferred_element_type=jnp.float32) * scale
    )
    match = (target_pair[:, None] == row_pairs[None, :])[None]
    masked = jnp.where(match, score, NEGATIVE)
    newest = jnp.maximum(running, jnp.max(masked, axis=-1))
    weight = jnp.where(match, jnp.exp(masked - newest[:, :, None]), 0.0)
    total = jnp.sum(weight, axis=-1)
    summed = jnp.einsum(
        "htr,rhd->htd", weight.astype(jnp.bfloat16), values, preferred_element_type=jnp.float32
    )
    running, total, summed = (newest, total, summed)
    context = jnp.transpose(summed / total[:, :, None], (1, 0, 2)).reshape(
        tok_rows, local_heads * HEAD
    )
    attended = (hidden.astype(jnp.float32) + context).astype(jnp.bfloat16)
    full_rows = lax.all_gather(attended, "mp", axis=1, tiled=True)
    width = full_rows.shape[1]
    experts_all = lax.axis_size("expert")
    batches = lax.axis_size("dp")
    cap = 2 * tok_rows // experts_all * 5 // 4
    flat = routes.reshape(-1)
    named = (flat[:, None] == jnp.arange(experts_all, dtype=jnp.int32)[None, :]).astype(jnp.int32)
    slot = jnp.sum((jnp.cumsum(named, axis=0) - named) * named, axis=1)
    dest = flat * cap + slot
    place = dest[:, None] == jnp.arange(experts_all * cap, dtype=jnp.int32)[None, :]
    per_token = jnp.sum(place.reshape(tok_rows, 2, experts_all * cap).astype(jnp.bfloat16), axis=1)
    outgoing = lax.dot_general(
        per_token, full_rows, (((0,), (0,)), ((), ())), preferred_element_type=jnp.float32
    ).astype(jnp.bfloat16)
    copies = jnp.broadcast_to(
        outgoing.reshape(experts_all, 1, cap, width), (experts_all, batches, cap, width)
    ).reshape(experts_all * batches * cap, width)
    arrived = lax.all_to_all(copies, ("expert", "dp"), split_axis=0, concat_axis=0, tiled=True)
    values = arrived.astype(jnp.float32)
    center = jnp.mean(values, axis=-1, keepdims=True)
    spread = jnp.mean(jnp.square(values - center), axis=-1, keepdims=True)
    normed = ((values - center) * lax.rsqrt(spread + EPSILON) * norm_gain + norm_bias).astype(
        jnp.bfloat16
    )
    active = jax.nn.relu(jnp.dot(normed, expert_in[0], preferred_element_type=jnp.float32)).astype(
        jnp.bfloat16
    )
    partial_value = jnp.dot(active, expert_out[0], preferred_element_type=jnp.float32).astype(
        jnp.bfloat16
    )
    returned = lax.all_to_all(
        partial_value, ("expert", "dp"), split_axis=0, concat_axis=0, tiled=True
    )
    expert_sum = jnp.sum(
        returned.reshape(experts_all, batches, cap, width).astype(jnp.float32), axis=1
    )
    picked = jnp.dot(
        place.astype(jnp.float32),
        expert_sum.reshape(experts_all * cap, width),
        precision=lax.Precision.HIGHEST,
    )
    blended = jnp.sum(picked.reshape(tok_rows, 2, width) * route_weight[:, :, None], axis=1)
    share = lax.psum_scatter(
        blended.astype(jnp.bfloat16), "mp", scatter_dimension=1, tiled=True
    ).astype(jnp.float32)
    return (attended.astype(jnp.float32) + share).astype(jnp.bfloat16)


def layer(hidden, queries, memory, *rest):
    experts = lax.axis_size("expert")
    rows, columns = hidden.shape
    heads = columns // HEAD
    by_heads = (
        lax.axis_size("mp") == 2
        and lax.axis_size("dp") == 2
        and heads % experts == 0
        and memory.shape[0] == rows
        and experts * rows <= columns // experts
        and experts == 4
    )
    return (head_shards if by_heads else shards)(hidden, queries, memory, *rest)


def solution(mesh):
    return jax.shard_map(
        layer,
        mesh=mesh,
        in_specs=(
            P(("groups", "expert", "dp"), "mp"),
            P(("groups", "expert", "dp"), "mp"),
            P(("groups", "expert", "dp"), None, "mp"),
            P(("groups", "expert", "dp")),
            P(("groups", "expert", "dp")),
            P(("groups", "expert", "dp"), None),
            P(("groups", "expert", "dp"), None),
            P(),
            P(),
            P("expert", None, ("dp", "mp")),
            P("expert", ("dp", "mp"), None),
        ),
        out_specs=P(("groups", "expert", "dp"), "mp"),
        check_vma=False,
    )
```
